512 devices in a mesh: heads: 8 (over y, core), groups: 64 (over z, x).
Axes of the slice: x: 4, y: 4, z: 16, core: 2. Of those that a mesh axis runs over, the one named last changes fastest.
Arguments:
- hidden_rows: bfloat16 [192, 8192], P(None, 'groups'), may hold values from -6 to 6
- qkv_weight: bfloat16 [8192, 10240], P('groups', 'heads'), may hold values from -1 to 1
- out_weight: bfloat16 [8192, 8192], P('heads', 'groups'), may hold values from -0.0625 to 0.0625
- norm_gain: float32 [8192], P('groups'), may hold values from 0.5 to 1.5
- next_weight: bfloat16 [8192, 10240], P('groups', 'heads'), may hold values from -0.0625 to 0.0625
- cache_keys: bfloat16 [49152, 1024], P('groups', 'heads'), may hold values from -6 to 6
- cache_values: bfloat16 [49152, 1024], P('groups', 'heads'), may hold values from -6 to 6
- group_lengths: int32 [128], replicated, may hold values from 128 to 384, as said below
- group_owner: int32 [128], replicated, may hold values from 0 to 63, as said below
- group_start: int32 [128], replicated, may hold values from 0 to 32640, as said below
- listed_rows: int32 [192], replicated, may hold values from 0 to 32767, as said below
Outputs:
- hidden_out: bfloat16 [192, 8192], P(None, 'groups')
- next_qkv: bfloat16 [192, 10240], P('groups', 'heads')
The draws below stay inside these ranges and needn't reach their ends.
Inputs may be any that keep to these rules, and one draw needn't show every extreme that they name: `group_lengths`: multiples of 128; groups 2k and 2k+1 together hold 512 tokens. `group_owner`: group 2k is held by owner k; every owner holds exactly two groups; one owner holds 768 tokens. The intervals from group_start to group_start + group_lengths - 1 of all groups tile 0 to 32767. `listed_rows`: distinct and increasing.
All inputs are finite; a program needn't handle non-finite values.
Results may differ from the reference program's by a relative error of at most 0.0085.
Values may be sent and summed in bfloat16 or wider, within the bound.
No kernel may reach another device: no remote copies, remote signals or barrier semaphores. Data moves between devices by JAX's collectives and lax.ppermute only.
A program may use at most 64 MiB of HBM per device.

```python
import jax
import jax.numpy as jnp
from jax import lax

D = 8192
KVH = 8
HD = 128
GQ = 8
BLK = 128
PAIR = 4
R = 192
CAP = 768
SEQ = 32768
N_GROUPS = 64


def draw_hidden_rows(key, part):
    rows = jnp.clip(jax.random.normal(jax.random.fold_in(key, 301), (R, D), jnp.float32), -6.0, 6.0)
    return jnp.clip(rows, -6.0, 6.0).astype(jnp.bfloat16)


def draw_qkv_weight(key, part):
    weights = jnp.clip(jax.random.normal(jax.random.fold_in(key, 302), (D, KVH * (GQ + 2) * HD), jnp.float32), -6.0, 6.0) * D ** (-0.5)
    return jnp.clip(weights, -1.0, 1.0).astype(jnp.bfloat16)


def draw_cache_keys(key, part):
    total_rows = N_GROUPS * CAP
    rows = jnp.clip(jax.random.normal(jax.random.fold_in(key, 303), (total_rows, KVH * HD), jnp.float32), -6.0, 6.0)
    return rows.astype(jnp.bfloat16)


def group_layout(key):
    base = jax.random.fold_in(key, 91)
    streams = jax.random.split(base, 5)
    count = N_GROUPS
    leading = jax.random.randint(streams[0], (count,), 1, PAIR)
    widest = jax.random.randint(streams[1], (), 0, count)
    partner = (widest + 1 + jax.random.randint(streams[2], (), 0, count - 1)) % count
    leading = leading.at[widest].set(PAIR - 1).at[partner].set(1)
    mapping = jax.random.permutation(streams[3], count)
    where_widest = jnp.argmax(mapping == widest)
    moved = mapping[partner]
    mapping = mapping.at[where_widest].set(moved).at[partner].set(widest)
    lengths = jnp.stack([leading, PAIR - leading], axis=1).reshape(2 * count) * BLK
    owners = jnp.stack([jnp.arange(count), mapping], axis=1).reshape(2 * count)
    order = jax.random.permutation(streams[4], 2 * count)
    ordered = lengths[order]
    sorted_starts = jnp.cumsum(ordered) - ordered
    starts = jnp.zeros((2 * count,), jnp.int32).at[order].set(sorted_starts.astype(jnp.int32))
    return (lengths.astype(jnp.int32), owners.astype(jnp.int32), starts.astype(jnp.int32))


def draw_group_lengths(key, part):
    return group_layout(key)[0]


def draw_group_owner(key, part):
    return group_layout(key)[1]


def draw_group_start(key, part):
    return group_layout(key)[2]


def draw_listed_rows(key, part):
    shuffled = jax.random.permutation(jax.random.fold_in(key, 17), SEQ)
    return jnp.sort(shuffled[:R]).astype(jnp.int32)


def block_levels(rng, shape, shards, smallest, largest):
    loudness = 1.0
    for position, shards_of in shards:
        steps = jax.random.uniform(jax.random.fold_in(jax.random.fold_in(rng, 6), position), (shards_of,), jnp.float32, smallest / len(shards), largest / len(shards))
        loudness = loudness * jnp.repeat(jnp.exp(steps), shape[position] // shards_of).reshape((-1,) + (1,) * (len(shape) - 1 - position))
    return loudness


def centred(stream_key, dims, deviation, most, shards=(), held_as=jnp.bfloat16):
    drawn = deviation * jax.random.normal(stream_key, dims, jnp.float32)
    if shards:
        drawn = drawn * block_levels(stream_key, dims, shards, -0.22, 0.18)
    return jnp.clip(drawn, -most, most).astype(held_as)


def setup_inputs(seed: int = 0) -> dict:
    key_of = jax.random.split(jax.random.key(seed), 12)
    hidden_rows = draw_hidden_rows(jax.random.fold_in(key_of[11], 71), 0)
    qkv_weight = draw_qkv_weight(jax.random.fold_in(key_of[11], 71), 0)
    out_weight = centred(key_of[2], (KVH * GQ * HD, D), (KVH * GQ * HD) ** -0.5, 0.0625, ((0, 8), (1, 64)))
    norm_gain = jnp.clip(1.0 + 0.1 * jax.random.normal(key_of[3], (D,), jnp.float32), 0.5, 1.5)
    next_weight = centred(key_of[4], (D, KVH * (GQ + 2) * HD), D ** -0.5, 0.0625, ((0, 64), (1, 8)))
    cache_keys = draw_cache_keys(jax.random.fold_in(key_of[11], 71), 0)
    cache_values = centred(key_of[6], (N_GROUPS * CAP, KVH * HD), 1.0, 6.0, ((0, 64), (1, 8)))
    group_lengths = draw_group_lengths(jax.random.fold_in(key_of[11], 71), 0)
    group_owner = draw_group_owner(jax.random.fold_in(key_of[11], 71), 0)
    group_start = draw_group_start(jax.random.fold_in(key_of[11], 71), 0)
    listed_rows = draw_listed_rows(jax.random.fold_in(key_of[11], 71), 0)
    return dict(hidden_rows=hidden_rows, qkv_weight=qkv_weight, out_weight=out_weight, norm_gain=norm_gain, next_weight=next_weight, cache_keys=cache_keys, cache_values=cache_values, group_lengths=group_lengths, group_owner=group_owner, group_start=group_start, listed_rows=listed_rows)


theta_base = 500000.0
epsilon = 1e-05
masked_score = -1e+30

def angles(positions, half_dim):
    freq = theta_base ** (-(jnp.arange(half_dim).astype(jnp.float32) * 2.0 / (2 * half_dim)))
    phase = positions.astype(jnp.float32)[:, None] * freq[None, :]
    return (jnp.cos(phase), jnp.sin(phase))

def rotate(vectors, cosine, sine):
    half_dim = vectors.shape[-1] // 2
    lower = vectors[..., :half_dim]
    upper = vectors[..., half_dim:]
    return jnp.concatenate([lower * cosine - upper * sine, upper * cosine + lower * sine], axis=-1)

def layout(owner_index, group_lengths, group_owner, group_start, listed_rows, cap_blocks, block_rows):
    block_len = (group_lengths // block_rows).astype(jnp.int32)
    holder = (group_owner == owner_index).astype(jnp.int32)
    held_blocks = holder * block_len
    offset = (jnp.cumsum(held_blocks) - held_blocks).astype(jnp.int32)
    block_ids = jnp.arange(cap_blocks).astype(jnp.int32)[:, None]
    member = ((holder[None, :] == 1) & (block_ids >= offset[None, :]) & (block_ids < offset[None, :] + block_len[None, :])).astype(jnp.int32)
    shift_blk = lax.optimization_barrier(jnp.sum(member * group_start[None, :], axis=1)).astype(jnp.int32)
    begin_blk = lax.optimization_barrier(jnp.sum(member * (group_start[None, :] + (block_ids - offset[None, :]) * block_rows), axis=1)).astype(jnp.int32)
    live_blk = lax.optimization_barrier(jnp.sum(member, axis=1)) > 0
    inside = jnp.arange(block_rows).astype(jnp.int32)[None, :]
    key_pos = (begin_blk[:, None] + inside).reshape(-1)
    key_shift = (shift_blk[:, None] + 0 * inside).reshape(-1)
    key_live = (live_blk[:, None] & (inside >= 0)).reshape(-1)
    listed_hit = jnp.any(key_pos[:, None] == listed_rows[None, :], axis=1)
    return (key_pos, key_shift, key_live & jnp.logical_not(listed_hit))

def combine(first_part, second_part):
    peak_one, total_one, numer_one = first_part
    peak_two, total_two, numer_two = second_part
    highest = jnp.maximum(peak_one, peak_two)
    scale_one = jnp.exp(peak_one - highest)
    scale_two = jnp.exp(peak_two - highest)
    return (highest, total_one * scale_one + total_two * scale_two, numer_one * scale_one[..., None] + numer_two * scale_two[..., None])

def owner_partial(owner_index, queries, keys_new, values_new, cache_keys, cache_values, group_lengths, group_owner, group_start, listed_rows):
    local_rows = R // N_GROUPS
    key_pos, key_shift, key_live = layout(owner_index, group_lengths, group_owner, group_start, listed_rows, CAP // BLK, BLK)
    slab_keys = lax.dynamic_slice_in_dim(cache_keys, owner_index * CAP, CAP).astype(jnp.float32).reshape(CAP, KVH, HD)
    cosine, sine = angles(key_shift, HD // 2)
    rotated = rotate(slab_keys, cosine[:, None], sine[:, None]).astype(jnp.bfloat16)
    slab_values = lax.dynamic_slice_in_dim(cache_values, owner_index * CAP, CAP).reshape(CAP, KVH, HD)
    first_row = owner_index * local_rows
    own_keys = lax.dynamic_slice_in_dim(keys_new, first_row, local_rows)
    own_values = lax.dynamic_slice_in_dim(values_new, first_row, local_rows)
    own_pos = lax.dynamic_slice_in_dim(listed_rows, first_row, local_rows).astype(jnp.int32)
    all_keys = jnp.concatenate([rotated, own_keys], axis=0).astype(jnp.float32)
    all_values = jnp.concatenate([slab_values, own_values], axis=0).astype(jnp.float32)
    all_pos = jnp.concatenate([key_pos.astype(jnp.int32), own_pos], axis=0)
    all_live = jnp.concatenate([key_live, jnp.ones((local_rows,), bool)], axis=0)
    scores = jnp.einsum('rhgd,khd->rhgk', queries.astype(jnp.float32), all_keys) * HD ** (-0.5)
    allowed = (all_live[None, :] & (all_pos[None, :] <= listed_rows[:, None]))[:, None, None, :]
    scores = jnp.where(allowed, scores, masked_score)
    peaks = lax.optimization_barrier(jnp.max(scores, axis=-1))
    weights = jnp.where(allowed, jnp.exp(scores - peaks[..., None]), 0.0)
    totals = lax.optimization_barrier(jnp.sum(weights, axis=-1))
    rounded = lax.optimization_barrier(weights.astype(jnp.bfloat16))
    numerator = jnp.einsum('rhgk,khd->rhgd', rounded.astype(jnp.float32), all_values)
    return (peaks, totals, numerator)

def reference(hidden_rows, qkv_weight, out_weight, norm_gain, next_weight, cache_keys, cache_values, group_lengths, group_owner, group_start, listed_rows):
    mixed = jnp.dot(hidden_rows, qkv_weight, preferred_element_type=jnp.float32).reshape(R, KVH, GQ + 2, HD)
    cosine, sine = angles(listed_rows, HD // 2)
    queries = rotate(mixed[:, :, :GQ], cosine[:, None, None], sine[:, None, None]).astype(jnp.bfloat16)
    keys_new = rotate(mixed[:, :, GQ], cosine[:, None], sine[:, None]).astype(jnp.bfloat16)
    values_new = mixed[:, :, GQ + 1].astype(jnp.bfloat16)

    def advance(carry, owner_index):
        partial_now = owner_partial(owner_index, queries, keys_new, values_new, cache_keys, cache_values, group_lengths, group_owner, group_start, listed_rows)
        return (combine(carry, partial_now), None)
    initial = (jnp.full((R, KVH, GQ), masked_score, jnp.float32), jnp.zeros((R, KVH, GQ), jnp.float32), jnp.zeros((R, KVH, GQ, HD), jnp.float32))
    (peaks, totals, numerator), _ = lax.scan(advance, initial, jnp.arange(N_GROUPS).astype(jnp.int32))
    heads_out = (numerator / totals[..., None]).astype(jnp.bfloat16).reshape(R, KVH * GQ * HD)
    attended = jnp.dot(heads_out, out_weight, preferred_element_type=jnp.float32)
    resid = hidden_rows.astype(jnp.float32) + attended
    squares = lax.optimization_barrier(jnp.sum(resid * resid, axis=1))
    normed = (resid * lax.rsqrt(squares / D + epsilon)[:, None] * norm_gain[None, :]).astype(jnp.bfloat16)
    next_qkv = jnp.dot(normed, next_weight, preferred_element_type=jnp.float32).astype(jnp.bfloat16)
    return (resid.astype(jnp.bfloat16), next_qkv)
```

```python
import functools

import jax
import jax.numpy as jnp
from jax import lax
from jax.experimental import pallas as pl
from jax.experimental.pallas import tpu as pltpu
from jax.sharding import Mesh
from jax.sharding import PartitionSpec as P

D = 8192
HD = 128
GQ = 8
BLK = 128
NZ = 16
NX = 4
NH = 8
RI = 3
XR = NZ * RI
TILE = 16
GROUPS = ("z", "x")
theta_base = 500000.0
epsilon = 1e-05
masked_score = -1e30
least_peak = -1e28
never = 2**30
LOG2E = 1.4426950408889634

bf16 = jnp.bfloat16
f32 = jnp.float32


def vmem_call(kernel, out_shape, operands, scratch=(), limit=32):
    space = pl.BlockSpec(memory_space=pltpu.VMEM)
    outs = jax.tree.map(lambda _: space, out_shape)
    return pl.pallas_call(
        kernel,
        out_shape=out_shape,
        in_specs=[space] * len(operands),
        out_specs=outs,
        scratch_shapes=list(scratch),
        compiler_params=pltpu.CompilerParams(vmem_limit_bytes=limit * 2**20),
    )(*operands)


def shaped(shape, dtype):
    return jax.ShapeDtypeStruct(shape, dtype)


def three_pieces(value):
    high = value.astype(bf16).astype(f32)
    rest = value - high
    middle = rest.astype(bf16).astype(f32)
    low = (rest - middle).astype(bf16).astype(f32)
    return high, middle, low


def angles(positions, half_dim):
    freq = theta_base ** (-(jnp.arange(half_dim).astype(f32) * 2.0 / (2 * half_dim)))
    phase = positions.astype(f32)[:, None] * freq[None, :]
    return (jnp.cos(phase), jnp.sin(phase))


def rope_factors(positions):
    cosine, sine = angles(positions, HD // 2)
    return jnp.concatenate([cosine, cosine], -1), jnp.concatenate([-sine, sine], -1)


def rotate_kernel(keys_ref, cos_ref, sin_ref, out_ref):
    for b in range(keys_ref.shape[0] // BLK):
        block = keys_ref[b * BLK : (b + 1) * BLK, :].astype(f32)
        turned = (
            block * cos_ref[b : b + 1, :]
            + pltpu.roll(block, HD // 2, 1) * sin_ref[b : b + 1, :]
        )
        turned = turned.astype(bf16).astype(f32)
        out_ref[:, b * BLK : (b + 1) * BLK] = turned.T.astype(bf16)


def project_kernel(hidden_ref, weight_ref, gain_ref, out_ref):
    rows = hidden_ref.shape[0]
    new = lax.broadcasted_iota(jnp.int32, (rows, 1), 0)
    src = (new % NZ) * (NX * RI) + (new // XR) * RI + (new % XR) // NZ
    chosen = lax.broadcasted_iota(jnp.int32, (rows, rows), 1) == src
    moved = jnp.dot(
        jnp.where(chosen, 1.0, 0.0).astype(bf16), hidden_ref[...], preferred_element_type=f32
    ).astype(bf16)
    high, middle, low = three_pieces(gain_ref[...])
    sub = lax.broadcasted_iota(jnp.int32, (TILE, HD), 0)
    gain = jnp.where(
        sub == 0, high, jnp.where(sub == 1, middle, jnp.where(sub == 2, low, 0.0))
    ).astype(bf16)
    zero = jnp.zeros((TILE, HD), bf16)
    for x in range(NX):
        part = moved[x * XR : (x + 1) * XR, :]
        product = jnp.dot(part, weight_ref[...], preferred_element_type=f32).astype(bf16)
        for i in range(RI):
            band = product[i * TILE : (i + 1) * TILE, :]
            for j in range(GQ + 2):
                slot = 2 * (i * 4) + j if j < GQ else 2 * (12 + i) + (j - GQ)
                out_ref[x, slot] = band[:, j * HD : (j + 1) * HD]
            out_ref[x, 32 + i] = part[i * TILE : (i + 1) * TILE, :]
        out_ref[x, 30] = zero
        out_ref[x, 31] = zero
        out_ref[x, 35] = gain


def sum_x_kernel(in_ref, tiles_ref, hidden_ref, gain_ref):
    for t in range(32):
        total = in_ref[0, t].astype(f32)
        for x in range(1, NX):
            total = total + in_ref[x, t].astype(f32)
        tiles_ref[t // 2, t % 2] = total.astype(bf16)
    for x in range(NX):
        for i in range(RI):
            hidden_ref[x, i] = in_ref[x, 32 + i]
        pieces = in_ref[x, 35].astype(f32)
        gain_ref[x : x + 1, :] = pieces[0:1] + pieces[1:2] + pieces[2:3]


def rope_kernel(in_ref, factors_ref, copies_ref, own_ref):
    for s in range(2):
        total = in_ref[0, s].astype(f32)
        for z in range(1, NZ):
            total = total + in_ref[z, s].astype(f32)
        turned = total * factors_ref[s, 0] + pltpu.roll(total, HD // 2, 1) * factors_ref[s, 1]
        turned = turned.astype(bf16)
        own_ref[s] = turned
        for z in range(NZ):
            copies_ref[z, s] = turned


def attend_kernel(
    queries_ref, keys_ref, values_ref, new_ref, keypos_ref, rowpos_ref, out_ref, score_ref
):
    held = keys_ref.shape[2]
    blocks = held // BLK
    scale = HD ** (-0.5) * LOG2E
    contract_last = (((1,), (1,)), ((), ()))
    new_keys = jnp.concatenate([new_ref[x, 0] for x in range(NX)], axis=0)
    new_values = jnp.concatenate([new_ref[x, 1] for x in range(NX)], axis=0)
    fresh = new_keys.shape[0]
    for i in range(RI):
        queries = jnp.concatenate(
            [queries_ref[4 * i + g // 2, g % 2] for g in range(GQ)], axis=0
        )
        row_pos = jnp.concatenate([rowpos_ref[i]] * GQ, axis=0)
        peak = jnp.full((HD, BLK), least_peak, f32)
        for x in range(NX):
            score = jnp.dot(queries, keys_ref[x], preferred_element_type=f32)
            for b in range(blocks):
                n = x * blocks + b
                cut = jnp.where(
                    keypos_ref[n : n + 1, :] <= row_pos,
                    score[:, b * BLK : (b + 1) * BLK],
                    masked_score,
                )
                score_ref[:, n * BLK : (n + 1) * BLK] = cut
                peak = jnp.maximum(peak, cut)
        n = NX * blocks
        score = lax.dot_general(queries, new_keys, contract_last, preferred_element_type=f32)
        last = jnp.where(keypos_ref[n : n + 1, :fresh] <= row_pos[:, :fresh], score, masked_score)
        top = jnp.maximum(
            jnp.max(peak, axis=1, keepdims=True), jnp.max(last, axis=1, keepdims=True)
        )
        top = top * scale
        weight = jnp.exp2(last * scale - top)
        total_last = jnp.sum(weight, axis=1, keepdims=True)
        numer = jnp.dot(weight.astype(bf16), new_values, preferred_element_type=f32)
        total = jnp.zeros((HD, BLK), f32)
        for x in range(NX):
            weights = []
            for b in range(blocks):
                n = x * blocks + b
                weight = jnp.exp2(score_ref[:, n * BLK : (n + 1) * BLK] * scale - top)
                total = total + weight
                weights.append(weight.astype(bf16))
            numer = numer + jnp.dot(
                jnp.concatenate(weights, axis=1), values_ref[x], preferred_element_type=f32
            )
        total = jnp.sum(total, axis=1, keepdims=True) + total_last
        some = total > 0.0
        share = numer * jnp.where(some, 1.0 / jnp.where(some, total, 1.0), 0.0)
        level = top + jnp.where(some, jnp.log2(jnp.where(some, total, 1.0)), 0.0)
        share_at = (NX * blocks + i) * BLK
        score_ref[:, share_at : share_at + BLK] = share
        level_at = (NX * blocks + RI + i) * BLK
        score_ref[:, level_at : level_at + BLK] = jnp.broadcast_to(level, (HD, BLK))
    lane = lax.broadcasted_iota(jnp.int32, (8, HD), 1)
    for z in range(NZ):
        parts = []
        tail = jnp.zeros((8, HD), f32)
        for k in range(RI):
            row = 24 * z + 8 * k
            i, r = row // HD, row % HD
            share_at = (NX * blocks + i) * BLK
            level_at = (NX * blocks + RI + i) * BLK
            parts.append(score_ref[r : r + 8, share_at : share_at + BLK])
            for p, piece in enumerate(three_pieces(score_ref[r : r + 8, level_at : level_at + BLK])):
                tail = jnp.where(lane == 3 * k + p, piece, tail)
        out_ref[z] = jnp.concatenate(parts + [tail], axis=0).astype(bf16)


def combine_kernel(in_ref, out_ref):
    level = [[None] * RI for _ in range(NZ)]
    top = [None] * RI
    for z in range(NZ):
        tail = in_ref[z].astype(f32)[24:32, :]
        for k in range(RI):
            value = tail[:, 3 * k : 3 * k + 1] + tail[:, 3 * k + 1 : 3 * k + 2]
            value = value + tail[:, 3 * k + 2 : 3 * k + 3]
            level[z][k] = value
            top[k] = value if z == 0 else jnp.maximum(top[k], value)
    numer = jnp.zeros((8 * RI, HD), f32)
    total = jnp.zeros((8 * RI, 1), f32)
    for z in range(NZ):
        factor = jnp.concatenate([jnp.exp2(level[z][k] - top[k]) for k in range(RI)], axis=0)
        numer = numer + in_ref[z].astype(f32)[: 8 * RI, :] * factor
        total = total + factor
    result = (numer / total).astype(bf16)
    for z in range(NZ):
        out_ref[z] = result


def output_kernel(heads_ref, weight_ref, out_ref):
    rows = heads_ref[...]
    bands = []
    for i in range(RI):
        at = i * GQ * TILE
        bands.append(
            jnp.concatenate([rows[at + g * TILE : at + (g + 1) * TILE, :] for g in range(GQ)], axis=1)
        )
    attended = jnp.concatenate(bands, axis=0)
    for x in range(NX):
        term = jnp.dot(attended, weight_ref[x], preferred_element_type=f32).astype(bf16)
        for h in range(NH):
            out_ref[h, :, x * HD : (x + 1) * HD] = term


def next_kernel(terms_ref, hidden_ref, gain_ref, weight_ref, resid_ref, out_ref, cut_ref):
    attended = terms_ref[0].astype(f32)
    for h in range(1, NH):
        attended = attended + terms_ref[h].astype(f32)
    squares = jnp.zeros((XR, 1), f32)
    product = jnp.zeros((XR, weight_ref.shape[2]), f32)
    for x in range(NX):
        before = jnp.concatenate([hidden_ref[x, i] for i in range(RI)], axis=0).astype(f32)
        resid = before + attended[:, x * HD : (x + 1) * HD]
        resid_ref[x] = resid.astype(bf16)
        squares = squares + jnp.sum(resid * resid, axis=1, keepdims=True)
        gained = (resid * gain_ref[x : x + 1, :]).astype(bf16)
        product = product + jnp.dot(gained, weight_ref[x], preferred_element_type=f32)
    for i in range(RI):
        for j in range(GQ + 2):
            cut_ref[:, i * (GQ + 2) + j, :] = product[
                i * TILE : (i + 1) * TILE, j * HD : (j + 1) * HD
            ]
    lane = lax.broadcasted_iota(jnp.int32, (TILE, HD), 1)
    tail = jnp.zeros((TILE, HD), f32)
    for i in range(RI):
        for p, piece in enumerate(three_pieces(squares[i * TILE : (i + 1) * TILE, :])):
            tail = jnp.where(lane == 3 * i + p, piece, tail)
    cut_ref[:, 30, :] = tail
    cut_ref[:, 31, :] = jnp.zeros((TILE, HD), f32)
    out_ref[...] = cut_ref[...].astype(bf16)


def finish_kernel(in_ref, out_ref):
    total = in_ref[0].astype(f32)
    for z in range(1, NZ):
        total = total + in_ref[z].astype(f32)
    rows = []
    for i in range(RI):
        squares = total[30:31, 3 * i : 3 * i + 1] + total[30:31, 3 * i + 1 : 3 * i + 2]
        squares = squares + total[30:31, 3 * i + 2 : 3 * i + 3]
        factor = lax.rsqrt(squares / D + epsilon)
        at = i * (GQ + 2)
        rows.append(
            jnp.concatenate(
                [total[at + j : at + j + 1, :] * factor for j in range(GQ + 2)], axis=1
            )
        )
    out_ref[...] = jnp.concatenate(rows, axis=0).astype(bf16)


def reorder_kernel(in_ref, out_ref):
    rows = out_ref.shape[0]
    new = lax.broadcasted_iota(jnp.int32, (rows, 1), 0)
    src = ((new // RI) % NX) * XR + (new % RI) * NZ + new // (NX * RI)
    chosen = lax.broadcasted_iota(jnp.int32, (rows, rows), 1) == src
    data = jnp.concatenate([in_ref[x] for x in range(NX)], axis=0)
    out_ref[...] = jnp.dot(
        jnp.where(chosen, 1.0, 0.0).astype(bf16), data, preferred_element_type=f32
    ).astype(bf16)


def key_layout(z, group_lengths, group_owner, group_start, listed_rows, blocks):
    owners = z * NX + jnp.arange(NX, dtype=jnp.int32)
    length = group_lengths // BLK
    holder = (group_owner[None, :] == owners[:, None]).astype(jnp.int32)
    count = group_owner.shape[0]
    before = jnp.arange(count)[None, :] < jnp.arange(count)[:, None]
    held = holder * length[None, :]
    offset = jnp.sum(jnp.where(before[None], held[:, None, :], 0), axis=2)
    ids = jnp.arange(blocks, dtype=jnp.int32)[None, :, None]
    member = (
        (holder[:, None, :] == 1)
        & (ids >= offset[:, None, :])
        & (ids < offset[:, None, :] + length[None, None, :])
    ).astype(jnp.int32)
    start = group_start[None, None, :]
    shift = jnp.sum(member * start, axis=2)
    begin = jnp.sum(member * (start + (ids - offset[:, None, :]) * BLK), axis=2)
    live = jnp.sum(member, axis=2) > 0
    position = begin[:, :, None] + jnp.arange(BLK, dtype=jnp.int32)
    hit = jnp.any(position[..., None] == listed_rows, axis=-1)
    position = jnp.where(live[:, :, None] & ~hit, position, never)
    return shift, position.reshape(NX * blocks, BLK)


def on_device(
    hidden_rows,
    qkv_weight,
    out_weight,
    norm_gain,
    next_weight,
    cache_keys,
    cache_values,
    group_lengths,
    group_owner,
    group_start,
    listed_rows,
):
    z = lax.axis_index("z")
    x = lax.axis_index("x")
    held = cache_keys.shape[0]
    blocks = held // BLK
    a2a = functools.partial(lax.all_to_all, split_axis=0, concat_axis=0, tiled=True)

    payload = vmem_call(
        project_kernel,
        shaped((NX, 36, TILE, HD), bf16),
        (hidden_rows, qkv_weight, norm_gain.reshape(1, HD)),
    )
    payload = a2a(payload, "x")

    shift, key_pos = key_layout(
        z, group_lengths, group_owner, group_start, listed_rows, blocks
    )
    own_shift = lax.dynamic_slice_in_dim(shift, x, 1, axis=0)[0]
    by_zxi = listed_rows.reshape(NZ, NX, RI)
    row_pos = lax.dynamic_slice_in_dim(by_zxi, x, 1, axis=1)[:, 0].T
    tile_row = jnp.where(z < 12, z // 4, jnp.minimum(z - 12, RI - 1))
    tile_pos = lax.dynamic_slice_in_dim(row_pos, tile_row, 1, axis=0)[0]
    new_pos = lax.dynamic_slice_in_dim(by_zxi, tile_row, 1, axis=2)[:, :, 0].T.reshape(-1)
    new_pos = jnp.where((z >= 12) & (z < 12 + RI), new_pos, never)
    new_pos = jnp.concatenate([new_pos, jnp.full((BLK - NZ * NX,), never, jnp.int32)])
    key_pos = jnp.concatenate([key_pos, new_pos[None]], axis=0)
    wide_row_pos = jnp.broadcast_to(row_pos[:, :, None], (RI, NZ, BLK))
    cosine, sine = rope_factors(jnp.concatenate([own_shift, tile_pos]))
    keys_turned = vmem_call(
        rotate_kernel,
        shaped((HD, held), bf16),
        (cache_keys, cosine[:blocks], sine[:blocks]),
    )
    turns = jnp.stack([cosine[blocks:], sine[blocks:]])
    still = jnp.stack([jnp.ones_like(turns[0]), jnp.zeros_like(turns[0])])
    factors = jnp.stack([turns, jnp.where(z < 12, turns, still)])
    keys_x = lax.all_gather(keys_turned, "x", axis=0)
    values_x = lax.all_gather(cache_values, "x", axis=0)
    out_weight_x = lax.all_gather(out_weight, "x", axis=0)
    next_weight_x = lax.all_gather(next_weight, "x", axis=0)

    tiles, hidden_x, gain_x = vmem_call(
        sum_x_kernel,
        (
            shaped((NZ, 2, TILE, HD), bf16),
            shaped((NX, RI, TILE, HD), bf16),
            shaped((NX, HD), f32),
        ),
        (payload,),
    )
    copies, own = vmem_call(
        rope_kernel,
        (shaped((NZ, 2, TILE, HD), bf16), shaped((2, TILE, HD), bf16)),
        (a2a(tiles, "z"), factors),
    )
    new_x = lax.all_gather(own, "x", axis=0)
    queries = a2a(copies, "z")
    parts = vmem_call(
        attend_kernel,
        shaped((NZ, 32, HD), bf16),
        (queries, keys_x, values_x, new_x, key_pos, wide_row_pos),
        scratch=[pltpu.VMEM((HD, (NX * blocks + 2 * RI) * BLK), f32)],
    )
    share = vmem_call(
        combine_kernel, shaped((NZ, 8 * RI, HD), bf16), (a2a(parts, "z"),)
    )
    heads_out = a2a(share, "z").reshape(XR * GQ, HD)
    terms = vmem_call(
        output_kernel, shaped((NH, XR, NX * HD), bf16), (heads_out, out_weight_x)
    )
    resid, products = vmem_call(
        next_kernel,
        (shaped((NX, XR, HD), bf16), shaped((NZ, 32, HD), bf16)),
        (a2a(terms, "heads"), hidden_x, gain_x, next_weight_x),
        scratch=[pltpu.VMEM((NZ, 32, HD), f32)],
    )
    resid = a2a(resid, "x")
    hidden_out = vmem_call(reorder_kernel, shaped(hidden_rows.shape, bf16), (resid,))
    next_qkv = vmem_call(
        finish_kernel, shaped((RI, (GQ + 2) * HD), bf16), (a2a(products, "z"),)
    )
    return hidden_out, next_qkv


def solution(mesh):
    split = Mesh(mesh.devices.reshape(NH, NZ, NX), ("heads", "z", "x"))
    return jax.shard_map(
        on_device,
        mesh=split,
        in_specs=(
            P(None, GROUPS),
            P(GROUPS, "heads"),
            P("heads", GROUPS),
            P(GROUPS),
            P(GROUPS, "heads"),
            P(GROUPS, "heads"),
            P(GROUPS, "heads"),
            P(),
            P(),
            P(),
            P(),
        ),
        out_specs=(P(None, GROUPS), P(GROUPS, "heads")),
        check_vma=False,
    )
```

```python
import functools

import jax
import jax.numpy as jnp
from jax import lax
from jax.experimental import pallas as pl
from jax.experimental.pallas import tpu as pltpu
from jax.sharding import Mesh
from jax.sharding import PartitionSpec as P

D = 8192
HD = 128
GQ = 8
BLK = 128
NZ = 16
NX = 4
NH = 8
RI = 3
XR = NZ * RI
TILE = 16
GROUPS = ("z", "x")
theta_base = 500000.0
epsilon = 1e-05
masked_score = -1e30
least_peak = -1e28
never = 2**30
LOG2E = 1.4426950408889634

bf16 = jnp.bfloat16
f32 = jnp.float32


def vmem_call(kernel, out_shape, operands, scratch=(), limit=32, scalars=0, hbm=False):
    space = pl.BlockSpec(memory_space=pltpu.VMEM)
    outs = jax.tree.map(lambda _: space, out_shape)
    rest = pl.BlockSpec(memory_space=pltpu.HBM) if hbm else space
    small = pl.BlockSpec(memory_space=pltpu.SMEM)
    return pl.pallas_call(
        kernel,
        out_shape=out_shape,
        in_specs=[small] * scalars + [rest] * (len(operands) - scalars),
        out_specs=outs,
        scratch_shapes=list(scratch),
        compiler_params=pltpu.CompilerParams(vmem_limit_bytes=limit * 2**20),
    )(*operands)


def shaped(shape, dtype):
    return jax.ShapeDtypeStruct(shape, dtype)


def three_pieces(value):
    high = value.astype(bf16).astype(f32)
    rest = value - high
    middle = rest.astype(bf16).astype(f32)
    low = (rest - middle).astype(bf16).astype(f32)
    return high, middle, low


def angles(positions, half_dim):
    freq = theta_base ** (-(jnp.arange(half_dim).astype(f32) * 2.0 / (2 * half_dim)))
    phase = positions.astype(f32)[:, None] * freq[None, :]
    return (jnp.cos(phase), jnp.sin(phase))


def rope_factors(positions):
    cosine, sine = angles(positions, HD // 2)
    return jnp.concatenate([cosine, cosine], -1), jnp.concatenate([-sine, sine], -1)


def rotate_kernel(keys_ref, values_ref, cos_ref, sin_ref, out_ref):
    blocks = keys_ref.shape[0] // BLK
    for b in range(blocks):
        out_ref[blocks + b] = values_ref[b * BLK : (b + 1) * BLK, :]
        block = keys_ref[b * BLK : (b + 1) * BLK, :].astype(f32)
        turned = (
            block * cos_ref[b : b + 1, :]
            + pltpu.roll(block, HD // 2, 1) * sin_ref[b : b + 1, :]
        )
        turned = turned.astype(bf16).astype(f32)
        out_ref[b] = turned.T.astype(bf16)


def project_kernel(hidden_hbm, weight_hbm, gain_hbm, out_ref, hidden_ref, weight_ref, gain_ref, sems):
    copies = [
        pltpu.make_async_copy(src, dst, sems.at[n])
        for n, (src, dst) in enumerate(
            ((hidden_hbm, hidden_ref), (gain_hbm, gain_ref), (weight_hbm, weight_ref))
        )
    ]
    for copy in copies:
        copy.start()
    rows = hidden_ref.shape[0]
    new = lax.broadcasted_iota(jnp.int32, (rows, 1), 0)
    src = (new % NZ) * (NX * RI) + (new // XR) * RI + (new % XR) // NZ
    chosen = lax.broadcasted_iota(jnp.int32, (rows, rows), 1) == src
    choice = jnp.where(chosen, 1.0, 0.0).astype(bf16)
    copies[0].wait()
    copies[1].wait()
    moved = jnp.dot(
        choice, hidden_ref[...], preferred_element_type=f32
    ).astype(bf16)
    high, middle, low = three_pieces(gain_ref[...])
    sub = lax.broadcasted_iota(jnp.int32, (TILE, HD), 0)
    gain = jnp.where(
        sub == 0, high, jnp.where(sub == 1, middle, jnp.where(sub == 2, low, 0.0))
    ).astype(bf16)
    zero = jnp.zeros((TILE, HD), bf16)
    copies[2].wait()
    for x in range(NX):
        part = moved[x * XR : (x + 1) * XR, :]
        product = jnp.dot(part, weight_ref[...], preferred_element_type=f32).astype(bf16)
        for i in range(RI):
            band = product[i * TILE : (i + 1) * TILE, :]
            for j in range(GQ + 2):
                slot = 2 * (i * 4) + j if j < GQ else 2 * (12 + i) + (j - GQ)
                out_ref[x, slot] = band[:, j * HD : (j + 1) * HD]
            out_ref[x, 32 + i] = part[i * TILE : (i + 1) * TILE, :]
        out_ref[x, 30] = zero
        out_ref[x, 31] = zero
        out_ref[x, 35] = gain


def sum_x_kernel(x_ref, in_ref, tiles_ref, hidden_ref, gain_ref):
    for t in range(32):
        total = in_ref[0, t].astype(f32)
        for x in range(1, NX):
            total = total + in_ref[x, t].astype(f32)
        tiles_ref[t // 2, t % 2] = total.astype(bf16)
    for s in range(NX):
        src = (x_ref[0] + NX - s) % NX
        for i in range(RI):
            hidden_ref[s, i] = in_ref[src, 32 + i]
        pieces = in_ref[src, 35].astype(f32)
        gain_ref[s : s + 1, :] = pieces[0:1] + pieces[1:2] + pieces[2:3]


def rope_kernel(in_ref, factors_ref, copies_ref, own_ref):
    for s in range(2):
        total = in_ref[0, s].astype(f32)
        for z in range(1, NZ):
            total = total + in_ref[z, s].astype(f32)
        turned = total * factors_ref[s, 0] + pltpu.roll(total, HD // 2, 1) * factors_ref[s, 1]
        turned = turned.astype(bf16)
        own_ref[s] = turned
        for z in range(NZ):
            copies_ref[z, s] = turned


def attend_kernel(queries_ref, keypos_ref, rowpos_ref, *refs):
    cache_refs, new_refs, (out_ref, score_ref) = refs[:NX], refs[NX : 2 * NX], refs[2 * NX :]
    blocks = cache_refs[0].shape[0] // 2
    scale = HD ** (-0.5) * LOG2E
    contract_last = (((1,), (1,)), ((), ()))
    new_keys = jnp.concatenate([ref[0] for ref in new_refs], axis=0)
    new_values = jnp.concatenate([ref[1] for ref in new_refs], axis=0)
    fresh = new_keys.shape[0]
    for i in range(RI):
        queries = jnp.concatenate(
            [queries_ref[4 * i + g // 2, g % 2] for g in range(GQ)], axis=0
        )
        row_pos = jnp.concatenate([rowpos_ref[i]] * GQ, axis=0)
        peak = jnp.full((HD, BLK), least_peak, f32)
        for x in range(NX):
            keys = jnp.concatenate([cache_refs[x][b] for b in range(blocks)], axis=1)
            score = jnp.dot(queries, keys, preferred_element_type=f32)
            for b in range(blocks):
                n = x * blocks + b
                cut = jnp.where(
                    keypos_ref[n : n + 1, :] <= row_pos,
                    score[:, b * BLK : (b + 1) * BLK],
                    masked_score,
                )
                score_ref[:, n * BLK : (n + 1) * BLK] = cut
                peak = jnp.maximum(peak, cut)
        n = NX * blocks
        score = lax.dot_general(queries, new_keys, contract_last, preferred_element_type=f32)
        last = jnp.where(keypos_ref[n : n + 1, :fresh] <= row_pos[:, :fresh], score, masked_score)
        top = jnp.maximum(
            jnp.max(peak, axis=1, keepdims=True), jnp.max(last, axis=1, keepdims=True)
        )
        top = top * scale
        weight = jnp.exp2(last * scale - top)
        total_last = jnp.sum(weight, axis=1, keepdims=True)
        numer = jnp.dot(weight.astype(bf16), new_values, preferred_element_type=f32)
        total = jnp.zeros((HD, BLK), f32)
        for x in range(NX):
            weights = []
            for b in range(blocks):
                n = x * blocks + b
                weight = jnp.exp2(score_ref[:, n * BLK : (n + 1) * BLK] * scale - top)
                total = total + weight
                weights.append(weight.astype(bf16))
            values = jnp.concatenate([cache_refs[x][blocks + b] for b in range(blocks)], axis=0)
            numer = numer + jnp.dot(
                jnp.concatenate(weights, axis=1), values, preferred_element_type=f32
            )
        total = jnp.sum(total, axis=1, keepdims=True) + total_last
        some = total > 0.0
        share = numer * jnp.where(some, 1.0 / jnp.where(some, total, 1.0), 0.0)
        level = top + jnp.where(some, jnp.log2(jnp.where(some, total, 1.0)), 0.0)
        share_at = (NX * blocks + i) * BLK
        score_ref[:, share_at : share_at + BLK] = share
        level_at = (NX * blocks + RI + i) * BLK
        score_ref[:, level_at : level_at + BLK] = jnp.broadcast_to(level, (HD, BLK))
    lane = lax.broadcasted_iota(jnp.int32, (8, HD), 1)
    for z in range(NZ):
        parts = []
        tail = jnp.zeros((8, HD), f32)
        for k in range(RI):
            row = 24 * z + 8 * k
            i, r = row // HD, row % HD
            share_at = (NX * blocks + i) * BLK
            level_at = (NX * blocks + RI + i) * BLK
            parts.append(score_ref[r : r + 8, share_at : share_at + BLK])
            for p, piece in enumerate(three_pieces(score_ref[r : r + 8, level_at : level_at + BLK])):
                tail = jnp.where(lane == 3 * k + p, piece, tail)
        out_ref[z] = jnp.concatenate(parts + [tail], axis=0).astype(bf16)


def combine_kernel(in_ref, out_ref):
    level = [[None] * RI for _ in range(NZ)]
    top = [None] * RI
    for z in range(NZ):
        tail = in_ref[z].astype(f32)[24:32, :]
        for k in range(RI):
            value = tail[:, 3 * k : 3 * k + 1] + tail[:, 3 * k + 1 : 3 * k + 2]
            value = value + tail[:, 3 * k + 2 : 3 * k + 3]
            level[z][k] = value
            top[k] = value if z == 0 else jnp.maximum(top[k], value)
    numer = jnp.zeros((8 * RI, HD), f32)
    total = jnp.zeros((8 * RI, 1), f32)
    for z in range(NZ):
        factor = jnp.concatenate([jnp.exp2(level[z][k] - top[k]) for k in range(RI)], axis=0)
        numer = numer + in_ref[z].astype(f32)[: 8 * RI, :] * factor
        total = total + factor
    result = (numer / total).astype(bf16)
    for z in range(NZ):
        out_ref[z] = result


def output_kernel(heads_ref, *refs):
    weight_refs, out_ref = refs[:NX], refs[NX]
    rows = heads_ref[...]
    bands = []
    for i in range(RI):
        at = i * GQ * TILE
        bands.append(
            jnp.concatenate([rows[at + g * TILE : at + (g + 1) * TILE, :] for g in range(GQ)], axis=1)
        )
    attended = jnp.concatenate(bands, axis=0)
    for x in range(NX):
        term = jnp.dot(attended, weight_refs[x][...], preferred_element_type=f32).astype(bf16)
        for h in range(NH):
            out_ref[h, :, x * HD : (x + 1) * HD] = term


def next_kernel(terms_ref, hidden_ref, gain_ref, *refs):
    weight_refs, resid_refs, (out_ref, cut_ref) = refs[:NX], refs[NX : 2 * NX], refs[2 * NX :]
    attended = terms_ref[0].astype(f32)
    for h in range(1, NH):
        attended = attended + terms_ref[h].astype(f32)
    squares = jnp.zeros((XR, 1), f32)
    product = jnp.zeros((XR, weight_refs[0].shape[1]), f32)
    for x in range(NX):
        before = jnp.concatenate([hidden_ref[x, i] for i in range(RI)], axis=0).astype(f32)
        resid = before + attended[:, x * HD : (x + 1) * HD]
        resid_refs[x][...] = resid.astype(bf16)
        squares = squares + jnp.sum(resid * resid, axis=1, keepdims=True)
        gained = (resid * gain_ref[x : x + 1, :]).astype(bf16)
        product = product + jnp.dot(gained, weight_refs[x][...], preferred_element_type=f32)
    for i in range(RI):
        for j in range(GQ + 2):
            cut_ref[:, i * (GQ + 2) + j, :] = product[
                i * TILE : (i + 1) * TILE, j * HD : (j + 1) * HD
            ]
    lane = lax.broadcasted_iota(jnp.int32, (TILE, HD), 1)
    tail = jnp.zeros((TILE, HD), f32)
    for i in range(RI):
        for p, piece in enumerate(three_pieces(squares[i * TILE : (i + 1) * TILE, :])):
            tail = jnp.where(lane == 3 * i + p, piece, tail)
    cut_ref[:, 30, :] = tail
    cut_ref[:, 31, :] = jnp.zeros((TILE, HD), f32)
    out_ref[...] = cut_ref[...].astype(bf16)


def finish_kernel(in_ref, out_ref):
    total = in_ref[0].astype(f32)
    for z in range(1, NZ):
        total = total + in_ref[z].astype(f32)
    rows = []
    for i in range(RI):
        squares = total[30:31, 3 * i : 3 * i + 1] + total[30:31, 3 * i + 1 : 3 * i + 2]
        squares = squares + total[30:31, 3 * i + 2 : 3 * i + 3]
        factor = lax.rsqrt(squares / D + epsilon)
        at = i * (GQ + 2)
        rows.append(
            jnp.concatenate(
                [total[at + j : at + j + 1, :] * factor for j in range(GQ + 2)], axis=1
            )
        )
    out_ref[...] = jnp.concatenate(rows, axis=0).astype(bf16)


def reorder_kernel(x_ref, *refs):
    in_refs, out_ref = refs[:NX], refs[NX]
    rows = out_ref.shape[0]
    new = lax.broadcasted_iota(jnp.int32, (rows, 1), 0)
    source = ((new // RI) % NX + NX - x_ref[0]) % NX
    src = source * XR + (new % RI) * NZ + new // (NX * RI)
    chosen = lax.broadcasted_iota(jnp.int32, (rows, rows), 1) == src
    data = jnp.concatenate([ref[...] for ref in in_refs], axis=0)
    out_ref[...] = jnp.dot(
        jnp.where(chosen, 1.0, 0.0).astype(bf16), data, preferred_element_type=f32
    ).astype(bf16)


def key_layout(owners, group_lengths, group_owner, group_start, listed_rows, blocks):
    length = group_lengths // BLK
    holder = (group_owner[None, :] == owners[:, None]).astype(jnp.int32)
    count = group_owner.shape[0]
    before = jnp.arange(count)[None, :] < jnp.arange(count)[:, None]
    held = holder * length[None, :]
    offset = jnp.sum(jnp.where(before[None], held[:, None, :], 0), axis=2)
    ids = jnp.arange(blocks, dtype=jnp.int32)[None, :, None]
    member = (
        (holder[:, None, :] == 1)
        & (ids >= offset[:, None, :])
        & (ids < offset[:, None, :] + length[None, None, :])
    ).astype(jnp.int32)
    start = group_start[None, None, :]
    shift = jnp.sum(member * start, axis=2)
    begin = jnp.sum(member * (start + (ids - offset[:, None, :]) * BLK), axis=2)
    live = jnp.sum(member, axis=2) > 0
    position = begin[:, :, None] + jnp.arange(BLK, dtype=jnp.int32)
    hit = jnp.any(position[..., None] == listed_rows, axis=-1)
    position = jnp.where(live[:, :, None] & ~hit, position, never)
    return shift, position.reshape(NX * blocks, BLK)


def on_device(
    hidden_rows,
    qkv_weight,
    out_weight,
    norm_gain,
    next_weight,
    cache_keys,
    cache_values,
    group_lengths,
    group_owner,
    group_start,
    listed_rows,
):
    z = lax.axis_index("z")
    x = lax.axis_index("x")
    held = cache_keys.shape[0]
    blocks = held // BLK
    a2a = functools.partial(lax.all_to_all, split_axis=0, concat_axis=0, tiled=True)

    def shifted(array, step):
        return lax.ppermute(array, "x", [(n, (n + step) % NX) for n in range(NX)])

    def from_x(array):
        return [array] + [shifted(array, step) for step in range(1, NX)]

    payload = vmem_call(
        project_kernel,
        shaped((NX, 36, TILE, HD), bf16),
        (hidden_rows, qkv_weight, norm_gain.reshape(1, HD)),
        scratch=[
            pltpu.VMEM(hidden_rows.shape, bf16),
            pltpu.VMEM(qkv_weight.shape, bf16),
            pltpu.VMEM((1, HD), f32),
            pltpu.SemaphoreType.DMA((3,)),
        ],
        hbm=True,
        limit=60,
    )
    payload = a2a(payload, "x")

    sources = (x + NX - jnp.arange(NX, dtype=jnp.int32)) % NX
    shift, key_pos = key_layout(
        z * NX + sources, group_lengths, group_owner, group_start, listed_rows, blocks
    )
    by_xiz = listed_rows.reshape(NZ, NX, RI).transpose(1, 2, 0)
    row_pos = lax.dynamic_slice_in_dim(by_xiz, x, 1, axis=0)[0]
    tile_row = jnp.where(z < 12, z // 4, jnp.minimum(z - 12, RI - 1))
    tile_pos = lax.dynamic_slice_in_dim(by_xiz, tile_row, 1, axis=1)[:, 0]
    tile_pos = jnp.sum(
        jnp.where(sources[:, None, None] == jnp.arange(NX)[None, :, None], tile_pos[None], 0), axis=1
    )
    fresh = (z >= 12) & (z < 12 + RI)
    new_pos = jnp.where(fresh, tile_pos.reshape(-1), never)
    new_pos = jnp.concatenate([new_pos, jnp.full((BLK - NZ * NX,), never, jnp.int32)])
    key_pos = jnp.concatenate([key_pos, new_pos[None]], axis=0)
    wide_row_pos = jnp.broadcast_to(row_pos[:, :, None], (RI, NZ, BLK))
    cosine, sine = rope_factors(jnp.concatenate([shift[0], tile_pos[0]]))
    cache = vmem_call(
        rotate_kernel,
        shaped((2 * blocks, BLK, HD), bf16),
        (cache_keys, cache_values, cosine[:blocks], sine[:blocks]),
    )
    turns = jnp.stack([cosine[blocks:], sine[blocks:]])
    still = jnp.stack([jnp.ones_like(turns[0]), jnp.zeros_like(turns[0])])
    factors = jnp.stack([turns, jnp.where(z < 12, turns, still)])

    x_scalar = x.reshape(1).astype(jnp.int32)
    tiles, hidden_x, gain_x = vmem_call(
        sum_x_kernel,
        (
            shaped((NZ, 2, TILE, HD), bf16),
            shaped((NX, RI, TILE, HD), bf16),
            shaped((NX, HD), f32),
        ),
        (x_scalar, payload),
        scalars=1,
    )
    tiles, cache = lax.optimization_barrier((tiles, cache))
    caches = from_x(cache)
    copies, own = vmem_call(
        rope_kernel,
        (shaped((NZ, 2, TILE, HD), bf16), shaped((2, TILE, HD), bf16)),
        (a2a(tiles, "z"), factors),
    )
    queries = a2a(copies, "z")
    news = from_x(own)
    parts = vmem_call(
        attend_kernel,
        shaped((NZ, 32, HD), bf16),
        (queries, key_pos, wide_row_pos, *caches, *news),
        scratch=[pltpu.VMEM((HD, (NX * blocks + 2 * RI) * BLK), f32)],
    )
    parts, out_weight = lax.optimization_barrier((parts, out_weight))
    out_weights = from_x(out_weight)
    parts, out_weights = lax.optimization_barrier((a2a(parts, "z"), out_weights))
    share = vmem_call(combine_kernel, shaped((NZ, 8 * RI, HD), bf16), (parts,))
    share, next_weight = lax.optimization_barrier((share, next_weight))
    next_weights = from_x(next_weight)
    heads_out, next_weights = lax.optimization_barrier((a2a(share, "z"), next_weights))
    heads_out = heads_out.reshape(XR * GQ, HD)
    terms = vmem_call(
        output_kernel, shaped((NH, XR, NX * HD), bf16), (heads_out, *out_weights)
    )
    *resids, products = vmem_call(
        next_kernel,
        (*[shaped((XR, HD), bf16)] * NX, shaped((NZ, 32, HD), bf16)),
        (a2a(terms, "heads"), hidden_x, gain_x, *next_weights),
        scratch=[pltpu.VMEM((NZ, 32, HD), f32)],
    )
    resids = [resids[0]] + [shifted(resids[s], NX - s) for s in range(1, NX)]
    hidden_out = vmem_call(
        reorder_kernel, shaped(hidden_rows.shape, bf16), (x_scalar, *resids), scalars=1
    )
    next_qkv = vmem_call(
        finish_kernel, shaped((RI, (GQ + 2) * HD), bf16), (a2a(products, "z"),)
    )
    return hidden_out, next_qkv


def solution(mesh):
    split = Mesh(mesh.devices.reshape(NH, NZ, NX), ("heads", "z", "x"))
    return jax.shard_map(
        on_device,
        mesh=split,
        in_specs=(
            P(None, GROUPS),
            P(GROUPS, "heads"),
            P("heads", GROUPS),
            P(GROUPS),
            P(GROUPS, "heads"),
            P(GROUPS, "heads"),
            P(GROUPS, "heads"),
            P(),
            P(),
            P(),
            P(),
        ),
        out_specs=(P(None, GROUPS), P(GROUPS, "heads")),
        check_vma=False,
    )
```

```python
import functools

import jax
import jax.numpy as jnp
from jax import lax
from jax.experimental import pallas as pl
from jax.experimental.pallas import tpu as pltpu
from jax.sharding import Mesh
from jax.sharding import PartitionSpec as P

D = 8192
HD = 128
GQ = 8
BLK = 128
NZ = 16
NX = 4
NH = 8
FRESH = 16
RI = 3
XR = NZ * RI
TILE = 16
QT = RI * GQ
KT = 2 * NX * RI
HT = QT + KT
GROUPS = ("z", "x")
theta_base = 500000.0
epsilon = 1e-05
masked_score = -1e30
least_peak = -1e28
never = 2**30
LOG2E = 1.4426950408889634

bf16 = jnp.bfloat16
f32 = jnp.float32


def vmem_call(kernel, out_shape, operands, scratch=(), limit=32, scalars=0, hbm=False):
    space = pl.BlockSpec(memory_space=pltpu.VMEM)
    outs = jax.tree.map(lambda _: space, out_shape)
    rest = pl.BlockSpec(memory_space=pltpu.HBM) if hbm else space
    small = pl.BlockSpec(memory_space=pltpu.SMEM)
    return pl.pallas_call(
        kernel,
        out_shape=out_shape,
        in_specs=[small] * scalars + [rest] * (len(operands) - scalars),
        out_specs=outs,
        scratch_shapes=list(scratch),
        compiler_params=pltpu.CompilerParams(vmem_limit_bytes=limit * 2**20),
    )(*operands)


def shaped(shape, dtype):
    return jax.ShapeDtypeStruct(shape, dtype)


def three_pieces(value):
    high = value.astype(bf16).astype(f32)
    rest = value - high
    middle = rest.astype(bf16).astype(f32)
    low = (rest - middle).astype(bf16).astype(f32)
    return high, middle, low


def angles(positions, half_dim):
    freq = theta_base ** (-(jnp.arange(half_dim).astype(f32) * 2.0 / (2 * half_dim)))
    phase = positions.astype(f32)[:, None] * freq[None, :]
    return (jnp.cos(phase), jnp.sin(phase))


def rope_factors(positions):
    cosine, sine = angles(positions, HD // 2)
    return jnp.concatenate([cosine, cosine], -1), jnp.concatenate([-sine, sine], -1)


def bundle_kernel(keys_ref, values_ref, cos_ref, sin_ref, out_weight_ref, next_weight_ref, out_ref, weights_ref):
    blocks = keys_ref.shape[0] // BLK
    for b in range(blocks):
        out_ref[blocks + b] = values_ref[b * BLK : (b + 1) * BLK, :]
        block = keys_ref[b * BLK : (b + 1) * BLK, :].astype(f32)
        turned = (
            block * cos_ref[b : b + 1, :]
            + pltpu.roll(block, HD // 2, 1) * sin_ref[b : b + 1, :]
        )
        turned = turned.astype(bf16).astype(f32)
        out_ref[b] = turned.T.astype(bf16)
    for g in range(GQ):
        weights_ref[g] = out_weight_ref[g * HD : (g + 1) * HD, :]
    for j in range(GQ + 2):
        weights_ref[GQ + j] = next_weight_ref[:, j * HD : (j + 1) * HD]


def project_kernel(hidden_hbm, weight_hbm, gain_hbm, out_ref, hidden_ref, weight_ref, gain_ref, sems):
    copies = [
        pltpu.make_async_copy(src, dst, sems.at[n])
        for n, (src, dst) in enumerate(
            ((hidden_hbm, hidden_ref), (gain_hbm, gain_ref), (weight_hbm, weight_ref))
        )
    ]
    for copy in copies:
        copy.start()
    rows = hidden_ref.shape[0]
    new = lax.broadcasted_iota(jnp.int32, (rows, 1), 0)
    src = (new % NZ) * (NX * RI) + (new // XR) * RI + (new % XR) // NZ
    chosen = lax.broadcasted_iota(jnp.int32, (rows, rows), 1) == src
    choice = jnp.where(chosen, 1.0, 0.0).astype(bf16)
    copies[0].wait()
    copies[1].wait()
    moved = jnp.dot(
        choice, hidden_ref[...], preferred_element_type=f32
    ).astype(bf16)
    high, middle, low = three_pieces(gain_ref[...])
    sub = lax.broadcasted_iota(jnp.int32, (TILE, HD), 0)
    gain = jnp.where(
        sub == 0, high, jnp.where(sub == 1, middle, jnp.where(sub == 2, low, 0.0))
    ).astype(bf16)
    copies[2].wait()
    for x in range(NX):
        part = moved[x * XR : (x + 1) * XR, :]
        product = jnp.dot(part, weight_ref[...], preferred_element_type=f32).astype(bf16)
        for i in range(RI):
            band = product[i * TILE : (i + 1) * TILE, :]
            for j in range(GQ):
                out_ref[x, i * GQ + j] = band[:, j * HD : (j + 1) * HD]
            for j in range(2):
                tile = band[:, (GQ + j) * HD : (GQ + j + 1) * HD]
                for to in range(NX):
                    out_ref[to, QT + j * NX * RI + x * RI + i] = tile
            out_ref[x, HT + i] = part[i * TILE : (i + 1) * TILE, :]
        out_ref[x, HT + RI] = gain


def sum_x_kernel(x_ref, in_ref, tiles_ref, hidden_ref, gain_ref, cut_ref):
    def total(t):
        result = in_ref[0, t].astype(f32)
        for x in range(1, NX):
            result = result + in_ref[x, t].astype(f32)
        return result

    for k in range(KT):
        cut_ref[:, k, :] = total(QT + k)
    rows = [total(t) for t in range(QT)]
    halves = [row[h * 8 : (h + 1) * 8, :] for row in rows for h in range(2)]
    for z in range(NZ):
        block = halves[z * RI : (z + 1) * RI] + [cut_ref[z]]
        tiles_ref[z] = jnp.concatenate(block, axis=0).astype(bf16)
    for s in range(NX):
        src = (x_ref[0] + NX - s) % NX
        for i in range(RI):
            hidden_ref[s, i] = in_ref[src, HT + i]
        pieces = in_ref[src, HT + RI].astype(f32)
        gain_ref[s : s + 1, :] = pieces[0:1] + pieces[1:2] + pieces[2:3]


def rope_kernel(in_ref, cos_ref, sin_ref, copies_ref, new_ref):
    total = in_ref[0].astype(f32)
    for z in range(1, NZ):
        total = total + in_ref[z].astype(f32)
    turned = total * cos_ref[...] + pltpu.roll(total, HD // 2, 1) * sin_ref[...]
    queries = turned[: 8 * RI, :].astype(bf16)
    for z in range(NZ):
        copies_ref[z] = queries
    new = turned[8 * RI :, :]
    pad = jnp.zeros((FRESH - NX * RI, HD), f32)
    new_ref[0] = jnp.concatenate([new[: NX * RI, :], pad], axis=0).astype(bf16)
    new_ref[1] = jnp.concatenate([new[NX * RI :, :], pad], axis=0).astype(bf16)


def attend_kernel(queries_ref, keypos_ref, rowpos_ref, new_ref, *refs):
    cache_refs, (out_ref, score_ref) = refs[:NX], refs[NX:]
    blocks = cache_refs[0].shape[0] // 2
    scale = HD ** (-0.5) * LOG2E
    contract_last = (((1,), (1,)), ((), ()))
    new_keys, new_values = new_ref[0], new_ref[1]
    fresh = new_keys.shape[0]
    every = queries_ref[...]
    for i in range(RI):
        queries = every[i * HD : (i + 1) * HD, :]
        row_pos = jnp.concatenate([rowpos_ref[i]] * GQ, axis=0)
        peak = jnp.full((HD, BLK), least_peak, f32)
        for x in range(NX):
            keys = jnp.concatenate([cache_refs[x][b] for b in range(blocks)], axis=1)
            score = jnp.dot(queries, keys, preferred_element_type=f32)
            for b in range(blocks):
                n = x * blocks + b
                cut = jnp.where(
                    keypos_ref[n : n + 1, :] <= row_pos,
                    score[:, b * BLK : (b + 1) * BLK],
                    masked_score,
                )
                score_ref[:, n * BLK : (n + 1) * BLK] = cut
                peak = jnp.maximum(peak, cut)
        n = NX * blocks
        score = lax.dot_general(queries, new_keys, contract_last, preferred_element_type=f32)
        last = jnp.where(keypos_ref[n : n + 1, :fresh] <= row_pos[:, :fresh], score, masked_score)
        top = jnp.maximum(
            jnp.max(peak, axis=1, keepdims=True), jnp.max(last, axis=1, keepdims=True)
        )
        top = top * scale
        weight = jnp.exp2(last * scale - top)
        total_last = jnp.sum(weight, axis=1, keepdims=True)
        numer = jnp.dot(weight.astype(bf16), new_values, preferred_element_type=f32)
        total = jnp.zeros((HD, BLK), f32)
        for x in range(NX):
            weights = []
            for b in range(blocks):
                n = x * blocks + b
                weight = jnp.exp2(score_ref[:, n * BLK : (n + 1) * BLK] * scale - top)
                total = total + weight
                weights.append(weight.astype(bf16))
            values = jnp.concatenate([cache_refs[x][blocks + b] for b in range(blocks)], axis=0)
            numer = numer + jnp.dot(
                jnp.concatenate(weights, axis=1), values, preferred_element_type=f32
            )
        total = jnp.sum(total, axis=1, keepdims=True) + total_last
        some = total > 0.0
        share = numer * jnp.where(some, 1.0 / jnp.where(some, total, 1.0), 0.0)
        level = top + jnp.where(some, jnp.log2(jnp.where(some, total, 1.0)), 0.0)
        share_at = (NX * blocks + i) * BLK
        score_ref[:, share_at : share_at + BLK] = share
        level_at = (NX * blocks + RI + i) * BLK
        score_ref[:, level_at : level_at + BLK] = jnp.broadcast_to(level, (HD, BLK))
    lane = lax.broadcasted_iota(jnp.int32, (8, HD), 1)
    for z in range(NZ):
        parts = []
        tail = jnp.zeros((8, HD), f32)
        for k in range(RI):
            row = 24 * z + 8 * k
            i, r = row // HD, row % HD
            share_at = (NX * blocks + i) * BLK
            level_at = (NX * blocks + RI + i) * BLK
            parts.append(score_ref[r : r + 8, share_at : share_at + BLK])
            for p, piece in enumerate(three_pieces(score_ref[r : r + 8, level_at : level_at + BLK])):
                tail = jnp.where(lane == 3 * k + p, piece, tail)
        out_ref[z] = jnp.concatenate(parts + [tail], axis=0).astype(bf16)


def combine_kernel(in_ref, out_ref):
    level = [[None] * RI for _ in range(NZ)]
    top = [None] * RI
    for z in range(NZ):
        tail = in_ref[z].astype(f32)[24:32, :]
        for k in range(RI):
            value = tail[:, 3 * k : 3 * k + 1] + tail[:, 3 * k + 1 : 3 * k + 2]
            value = value + tail[:, 3 * k + 2 : 3 * k + 3]
            level[z][k] = value
            top[k] = value if z == 0 else jnp.maximum(top[k], value)
    numer = jnp.zeros((8 * RI, HD), f32)
    total = jnp.zeros((8 * RI, 1), f32)
    for z in range(NZ):
        factor = jnp.concatenate([jnp.exp2(level[z][k] - top[k]) for k in range(RI)], axis=0)
        numer = numer + in_ref[z].astype(f32)[: 8 * RI, :] * factor
        total = total + factor
    result = (numer / total).astype(bf16)
    for z in range(NZ):
        out_ref[z] = result


def output_kernel(heads_ref, *refs):
    weight_refs, out_ref = [ref.at[pl.ds(0, GQ)] for ref in refs[:NX]], refs[NX]
    rows = heads_ref[...]
    bands = []
    for i in range(RI):
        at = i * GQ * TILE
        bands.append(
            jnp.concatenate([rows[at + g * TILE : at + (g + 1) * TILE, :] for g in range(GQ)], axis=1)
        )
    attended = jnp.concatenate(bands, axis=0)
    for x in range(NX):
        term = jnp.dot(attended, weight_refs[x][...].reshape(GQ * HD, HD), preferred_element_type=f32).astype(bf16)
        for h in range(NH):
            out_ref[h, :, x * HD : (x + 1) * HD] = term


def next_kernel(terms_ref, hidden_ref, gain_ref, *refs):
    weight_refs = [ref.at[pl.ds(GQ, GQ + 2)] for ref in refs[:NX]]
    resid_refs, (out_ref, cut_ref) = refs[NX : 2 * NX], refs[2 * NX :]
    attended = terms_ref[0].astype(f32)
    for h in range(1, NH):
        attended = attended + terms_ref[h].astype(f32)
    squares = jnp.zeros((XR, 1), f32)
    product = jnp.zeros((XR, (GQ + 2) * HD), f32)
    for x in range(NX):
        before = jnp.concatenate([hidden_ref[x, i] for i in range(RI)], axis=0).astype(f32)
        resid = before + attended[:, x * HD : (x + 1) * HD]
        resid_refs[x][...] = resid.astype(bf16)
        squares = squares + jnp.sum(resid * resid, axis=1, keepdims=True)
        gained = (resid * gain_ref[x : x + 1, :]).astype(bf16)
        weight = jnp.concatenate([weight_refs[x][j] for j in range(GQ + 2)], axis=1)
        product = product + jnp.dot(gained, weight, preferred_element_type=f32)
    for i in range(RI):
        for j in range(GQ + 2):
            cut_ref[:, i * (GQ + 2) + j, :] = product[
                i * TILE : (i + 1) * TILE, j * HD : (j + 1) * HD
            ]
    lane = lax.broadcasted_iota(jnp.int32, (TILE, HD), 1)
    tail = jnp.zeros((TILE, HD), f32)
    for i in range(RI):
        for p, piece in enumerate(three_pieces(squares[i * TILE : (i + 1) * TILE, :])):
            tail = jnp.where(lane == 3 * i + p, piece, tail)
    cut_ref[:, 30, :] = tail
    cut_ref[:, 31, :] = jnp.zeros((TILE, HD), f32)
    out_ref[...] = cut_ref[...].astype(bf16)


def finish_kernel(in_ref, out_ref):
    total = in_ref[0].astype(f32)
    for z in range(1, NZ):
        total = total + in_ref[z].astype(f32)
    rows = []
    for i in range(RI):
        squares = total[30:31, 3 * i : 3 * i + 1] + total[30:31, 3 * i + 1 : 3 * i + 2]
        squares = squares + total[30:31, 3 * i + 2 : 3 * i + 3]
        factor = lax.rsqrt(squares / D + epsilon)
        at = i * (GQ + 2)
        rows.append(
            jnp.concatenate(
                [total[at + j : at + j + 1, :] * factor for j in range(GQ + 2)], axis=1
            )
        )
    out_ref[...] = jnp.concatenate(rows, axis=0).astype(bf16)


def reorder_kernel(x_ref, *refs):
    in_refs, out_ref = refs[:NX], refs[NX]
    rows = out_ref.shape[0]
    new = lax.broadcasted_iota(jnp.int32, (rows, 1), 0)
    source = ((new // RI) % NX + NX - x_ref[0]) % NX
    src = source * XR + (new % RI) * NZ + new // (NX * RI)
    chosen = lax.broadcasted_iota(jnp.int32, (rows, rows), 1) == src
    data = jnp.concatenate([ref[...] for ref in in_refs], axis=0)
    out_ref[...] = jnp.dot(
        jnp.where(chosen, 1.0, 0.0).astype(bf16), data, preferred_element_type=f32
    ).astype(bf16)


def key_layout(owners, group_lengths, group_owner, group_start, listed_rows, blocks):
    length = group_lengths // BLK
    holder = (group_owner[None, :] == owners[:, None]).astype(jnp.int32)
    count = group_owner.shape[0]
    before = jnp.arange(count)[None, :] < jnp.arange(count)[:, None]
    held = holder * length[None, :]
    offset = jnp.sum(jnp.where(before[None], held[:, None, :], 0), axis=2)
    ids = jnp.arange(blocks, dtype=jnp.int32)[None, :, None]
    member = (
        (holder[:, None, :] == 1)
        & (ids >= offset[:, None, :])
        & (ids < offset[:, None, :] + length[None, None, :])
    ).astype(jnp.int32)
    start = group_start[None, None, :]
    shift = jnp.sum(member * start, axis=2)
    begin = jnp.sum(member * (start + (ids - offset[:, None, :]) * BLK), axis=2)
    live = jnp.sum(member, axis=2) > 0
    position = begin[:, :, None] + jnp.arange(BLK, dtype=jnp.int32)
    hit = jnp.any(position[..., None] == listed_rows, axis=-1)
    position = jnp.where(live[:, :, None] & ~hit, position, never)
    return shift, position.reshape(NX * blocks, BLK)


def on_device(
    hidden_rows,
    qkv_weight,
    out_weight,
    norm_gain,
    next_weight,
    cache_keys,
    cache_values,
    group_lengths,
    group_owner,
    group_start,
    listed_rows,
):
    z = lax.axis_index("z")
    x = lax.axis_index("x")
    held = cache_keys.shape[0]
    blocks = held // BLK
    a2a = functools.partial(lax.all_to_all, split_axis=0, concat_axis=0, tiled=True)

    def shifted(array, step):
        return lax.ppermute(array, "x", [(n, (n + step) % NX) for n in range(NX)])

    def after(array, first):
        return lax.optimization_barrier((array, first))[0]

    payload = vmem_call(
        project_kernel,
        shaped((NX, HT + RI + 1, TILE, HD), bf16),
        (hidden_rows, qkv_weight, norm_gain.reshape(1, HD)),
        scratch=[
            pltpu.VMEM(hidden_rows.shape, bf16),
            pltpu.VMEM(qkv_weight.shape, bf16),
            pltpu.VMEM((1, HD), f32),
            pltpu.SemaphoreType.DMA((3,)),
        ],
        hbm=True,
        limit=60,
    )
    payload = a2a(payload, "x")

    sources = (x + NX - jnp.arange(NX, dtype=jnp.int32)) % NX
    shift, key_pos = key_layout(
        z * NX + sources, group_lengths, group_owner, group_start, listed_rows, blocks
    )
    by_zxi = listed_rows.reshape(NZ, NX, RI)
    row_pos = lax.dynamic_slice_in_dim(by_zxi, x, 1, axis=1)[:, 0].T
    new_pos = lax.dynamic_slice_in_dim(by_zxi, z, 1, axis=0).reshape(-1)
    own = 8 * RI * z + jnp.arange(8 * RI)
    chosen = (own // HD * NZ + own % NZ)[:, None] == jnp.arange(XR)[None, :]
    query_pos = jnp.sum(jnp.where(chosen, row_pos.reshape(1, XR), 0), axis=1)
    rest = jnp.full((BLK - NX * RI,), never, jnp.int32)
    key_pos = jnp.concatenate([key_pos, jnp.concatenate([new_pos, rest])[None]], axis=0)
    wide_row_pos = jnp.broadcast_to(row_pos[:, :, None], (RI, NZ, BLK))
    cosine, sine = rope_factors(
        jnp.concatenate([query_pos, new_pos, jnp.zeros((NX * RI,), jnp.int32), shift[0]])
    )
    rows = 8 * RI + KT
    cache, weights = vmem_call(
        bundle_kernel,
        (shaped((2 * blocks, BLK, HD), bf16), shaped((2 * GQ + 2, HD, HD), bf16)),
        (cache_keys, cache_values, cosine[rows:], sine[rows:], out_weight, next_weight),
    )

    x_scalar = x.reshape(1).astype(jnp.int32)
    tiles, hidden_x, gain_x = vmem_call(
        sum_x_kernel,
        (
            shaped((NZ, rows, HD), bf16),
            shaped((NX, RI, TILE, HD), bf16),
            shaped((NX, HD), f32),
        ),
        (x_scalar, payload),
        scratch=[pltpu.VMEM((NZ, KT, HD), f32)],
        scalars=1,
    )
    caches = [cache] + [shifted(after(cache, tiles), step) for step in (1, 3)]
    copies, new = vmem_call(
        rope_kernel,
        (shaped((NZ, 8 * RI, HD), bf16), shaped((2, FRESH, HD), bf16)),
        (a2a(tiles, "z"), cosine[:rows], sine[:rows]),
    )
    caches.insert(2, shifted(after(cache, copies), 2))
    weights_x = [weights, shifted(after(weights, copies), 1)]
    queries = a2a(copies, "z").reshape(XR * GQ, HD)
    parts = vmem_call(
        attend_kernel,
        shaped((NZ, 32, HD), bf16),
        (queries, key_pos, wide_row_pos, new, *caches),
        scratch=[pltpu.VMEM((HD, (NX * blocks + 2 * RI) * BLK), f32)],
    )
    weights_x += [shifted(after(weights, parts), step) for step in (2, 3)]
    share = vmem_call(
        combine_kernel, shaped((NZ, 8 * RI, HD), bf16), (a2a(parts, "z"),)
    )
    heads_out = a2a(share, "z").reshape(XR * GQ, HD)
    terms = vmem_call(
        output_kernel, shaped((NH, XR, NX * HD), bf16), (heads_out, *weights_x)
    )
    *resids, products = vmem_call(
        next_kernel,
        (*[shaped((XR, HD), bf16)] * NX, shaped((NZ, 32, HD), bf16)),
        (a2a(terms, "heads"), hidden_x, gain_x, *weights_x),
        scratch=[pltpu.VMEM((NZ, 32, HD), f32)],
    )
    resids = [resids[0]] + [shifted(resids[s], NX - s) for s in range(1, NX)]
    hidden_out = vmem_call(
        reorder_kernel, shaped(hidden_rows.shape, bf16), (x_scalar, *resids), scalars=1
    )
    next_qkv = vmem_call(
        finish_kernel, shaped((RI, (GQ + 2) * HD), bf16), (a2a(products, "z"),)
    )
    return hidden_out, next_qkv


def solution(mesh):
    split = Mesh(mesh.devices.reshape(NH, NZ, NX), ("heads", "z", "x"))
    return jax.shard_map(
        on_device,
        mesh=split,
        in_specs=(
            P(None, GROUPS),
            P(GROUPS, "heads"),
            P("heads", GROUPS),
            P(GROUPS),
            P(GROUPS, "heads"),
            P(GROUPS, "heads"),
            P(GROUPS, "heads"),
            P(),
            P(),
            P(),
            P(),
        ),
        out_specs=(P(None, GROUPS), P(GROUPS, "heads")),
        check_vma=False,
    )
```

```python
import functools

import jax
import jax.numpy as jnp
from jax import lax
from jax.experimental import pallas as pl
from jax.experimental.pallas import tpu as pltpu
from jax.sharding import Mesh
from jax.sharding import PartitionSpec as P

D = 8192
HD = 128
GQ = 8
BLK = 128
NZ = 16
NX = 4
NH = 8
FRESH = 16
RI = 3
XR = NZ * RI
TILE = 16
QT = RI * GQ
KT = 2 * NX * RI
HT = QT + KT
GROUPS = ("z", "x")
theta_base = 500000.0
epsilon = 1e-05
masked_score = -1e30
least_peak = -1e28
never = 2**30
LOG2E = 1.4426950408889634

bf16 = jnp.bfloat16
f32 = jnp.float32


def vmem_call(kernel, out_shape, operands, scratch=(), limit=32, scalars=0, hbm=False):
    space = pl.BlockSpec(memory_space=pltpu.VMEM)
    outs = jax.tree.map(lambda _: space, out_shape)
    rest = pl.BlockSpec(memory_space=pltpu.HBM) if hbm else space
    small = pl.BlockSpec(memory_space=pltpu.SMEM)
    return pl.pallas_call(
        kernel,
        out_shape=out_shape,
        in_specs=[small] * scalars + [rest] * (len(operands) - scalars),
        out_specs=outs,
        scratch_shapes=list(scratch),
        compiler_params=pltpu.CompilerParams(vmem_limit_bytes=limit * 2**20),
    )(*operands)


def shaped(shape, dtype):
    return jax.ShapeDtypeStruct(shape, dtype)


def three_pieces(value):
    high = value.astype(bf16).astype(f32)
    rest = value - high
    middle = rest.astype(bf16).astype(f32)
    low = (rest - middle).astype(bf16).astype(f32)
    return high, middle, low


def angles(positions, half_dim):
    freq = theta_base ** (-(jnp.arange(half_dim).astype(f32) * 2.0 / (2 * half_dim)))
    phase = positions.astype(f32)[:, None] * freq[None, :]
    return (jnp.cos(phase), jnp.sin(phase))


def rope_factors(positions):
    cosine, sine = angles(positions, HD // 2)
    return jnp.concatenate([cosine, cosine], -1), jnp.concatenate([-sine, sine], -1)


def bundle_kernel(keys_ref, values_ref, cos_ref, sin_ref, out_ref):
    blocks = keys_ref.shape[0] // BLK
    for b in range(blocks):
        out_ref[blocks + b] = values_ref[b * BLK : (b + 1) * BLK, :]
        block = keys_ref[b * BLK : (b + 1) * BLK, :].astype(f32)
        turned = (
            block * cos_ref[b : b + 1, :]
            + pltpu.roll(block, HD // 2, 1) * sin_ref[b : b + 1, :]
        )
        turned = turned.astype(bf16).astype(f32)
        out_ref[b] = turned.T.astype(bf16)


def project_kernel(hidden_hbm, weight_hbm, gain_hbm, out_ref, hidden_ref, weight_ref, gain_ref, sems):
    copies = [
        pltpu.make_async_copy(src, dst, sems.at[n])
        for n, (src, dst) in enumerate(
            ((hidden_hbm, hidden_ref), (gain_hbm, gain_ref), (weight_hbm, weight_ref))
        )
    ]
    for copy in copies:
        copy.start()
    rows = hidden_ref.shape[0]
    new = lax.broadcasted_iota(jnp.int32, (rows, 1), 0)
    src = (new % NZ) * (NX * RI) + (new // XR) * RI + (new % XR) // NZ
    chosen = lax.broadcasted_iota(jnp.int32, (rows, rows), 1) == src
    choice = jnp.where(chosen, 1.0, 0.0).astype(bf16)
    copies[0].wait()
    copies[1].wait()
    moved = jnp.dot(
        choice, hidden_ref[...], preferred_element_type=f32
    ).astype(bf16)
    high, middle, low = three_pieces(gain_ref[...])
    sub = lax.broadcasted_iota(jnp.int32, (TILE, HD), 0)
    gain = jnp.where(
        sub == 0, high, jnp.where(sub == 1, middle, jnp.where(sub == 2, low, 0.0))
    ).astype(bf16)
    copies[2].wait()
    for x in range(NX):
        part = moved[x * XR : (x + 1) * XR, :]
        product = jnp.dot(part, weight_ref[...], preferred_element_type=f32).astype(bf16)
        for i in range(RI):
            band = product[i * TILE : (i + 1) * TILE, :]
            for j in range(GQ):
                out_ref[x, i * GQ + j] = band[:, j * HD : (j + 1) * HD]
            for j in range(2):
                tile = band[:, (GQ + j) * HD : (GQ + j + 1) * HD]
                for to in range(NX):
                    out_ref[to, QT + j * NX * RI + x * RI + i] = tile
            out_ref[x, HT + i] = part[i * TILE : (i + 1) * TILE, :]
        out_ref[x, HT + RI] = gain


def sum_x_kernel(x_ref, in_ref, tiles_ref, hidden_ref, gain_ref, cut_ref):
    def total(t):
        result = in_ref[0, t].astype(f32)
        for x in range(1, NX):
            result = result + in_ref[x, t].astype(f32)
        return result

    for k in range(KT):
        cut_ref[:, k, :] = total(QT + k)
    rows = [total(t) for t in range(QT)]
    halves = [row[h * 8 : (h + 1) * 8, :] for row in rows for h in range(2)]
    for z in range(NZ):
        block = halves[z * RI : (z + 1) * RI] + [cut_ref[z]]
        tiles_ref[z] = jnp.concatenate(block, axis=0).astype(bf16)
    for s in range(NX):
        src = (x_ref[0] + NX - s) % NX
        for i in range(RI):
            hidden_ref[s, i] = in_ref[src, HT + i]
        pieces = in_ref[src, HT + RI].astype(f32)
        gain_ref[s : s + 1, :] = pieces[0:1] + pieces[1:2] + pieces[2:3]


def rope_kernel(in_ref, cos_ref, sin_ref, copies_ref, new_ref):
    total = in_ref[0].astype(f32)
    for z in range(1, NZ):
        total = total + in_ref[z].astype(f32)
    turned = total * cos_ref[...] + pltpu.roll(total, HD // 2, 1) * sin_ref[...]
    queries = turned[: 8 * RI, :].astype(bf16)
    for z in range(NZ):
        copies_ref[z] = queries
    new = turned[8 * RI :, :]
    pad = jnp.zeros((FRESH - NX * RI, HD), f32)
    new_ref[0] = jnp.concatenate([new[: NX * RI, :], pad], axis=0).astype(bf16)
    new_ref[1] = jnp.concatenate([new[NX * RI :, :], pad], axis=0).astype(bf16)


def attend_kernel(queries_ref, keypos_ref, rowpos_ref, new_ref, *refs):
    cache_refs, (out_ref, score_ref) = refs[:NX], refs[NX:]
    blocks = cache_refs[0].shape[0] // 2
    scale = HD ** (-0.5) * LOG2E
    contract_last = (((1,), (1,)), ((), ()))
    new_keys, new_values = new_ref[0], new_ref[1]
    fresh = new_keys.shape[0]
    every = queries_ref[...]
    for i in range(RI):
        queries = every[i * HD : (i + 1) * HD, :]
        row_pos = jnp.concatenate([rowpos_ref[i]] * GQ, axis=0)
        peak = jnp.full((HD, BLK), least_peak, f32)
        for x in range(NX):
            keys = jnp.concatenate([cache_refs[x][b] for b in range(blocks)], axis=1)
            score = jnp.dot(queries, keys, preferred_element_type=f32)
            for b in range(blocks):
                n = x * blocks + b
                cut = jnp.where(
                    keypos_ref[n : n + 1, :] <= row_pos,
                    score[:, b * BLK : (b + 1) * BLK],
                    masked_score,
                )
                score_ref[:, n * BLK : (n + 1) * BLK] = cut
                peak = jnp.maximum(peak, cut)
        n = NX * blocks
        score = lax.dot_general(queries, new_keys, contract_last, preferred_element_type=f32)
        last = jnp.where(keypos_ref[n : n + 1, :fresh] <= row_pos[:, :fresh], score, masked_score)
        top = jnp.maximum(
            jnp.max(peak, axis=1, keepdims=True), jnp.max(last, axis=1, keepdims=True)
        )
        top = top * scale
        weight = jnp.exp2(last * scale - top)
        total_last = jnp.sum(weight, axis=1, keepdims=True)
        numer = jnp.dot(weight.astype(bf16), new_values, preferred_element_type=f32)
        total = jnp.zeros((HD, BLK), f32)
        for x in range(NX):
            weights = []
            for b in range(blocks):
                n = x * blocks + b
                weight = jnp.exp2(score_ref[:, n * BLK : (n + 1) * BLK] * scale - top)
                total = total + weight
                weights.append(weight.astype(bf16))
            values = jnp.concatenate([cache_refs[x][blocks + b] for b in range(blocks)], axis=0)
            numer = numer + jnp.dot(
                jnp.concatenate(weights, axis=1), values, preferred_element_type=f32
            )
        total = jnp.sum(total, axis=1, keepdims=True) + total_last
        some = total > 0.0
        share = numer * jnp.where(some, 1.0 / jnp.where(some, total, 1.0), 0.0)
        level = top + jnp.where(some, jnp.log2(jnp.where(some, total, 1.0)), 0.0)
        share_at = (NX * blocks + i) * BLK
        score_ref[:, share_at : share_at + BLK] = share
        level_at = (NX * blocks + RI + i) * BLK
        score_ref[:, level_at : level_at + BLK] = jnp.broadcast_to(level, (HD, BLK))
    lane = lax.broadcasted_iota(jnp.int32, (8, HD), 1)
    for z in range(NZ):
        parts = []
        tail = jnp.zeros((8, HD), f32)
        for k in range(RI):
            row = 24 * z + 8 * k
            i, r = row // HD, row % HD
            share_at = (NX * blocks + i) * BLK
            level_at = (NX * blocks + RI + i) * BLK
            parts.append(score_ref[r : r + 8, share_at : share_at + BLK])
            for p, piece in enumerate(three_pieces(score_ref[r : r + 8, level_at : level_at + BLK])):
                tail = jnp.where(lane == 3 * k + p, piece, tail)
        out_ref[z] = jnp.concatenate(parts + [tail], axis=0).astype(bf16)


def combine_kernel(in_ref, out_ref):
    level = [[None] * RI for _ in range(NZ)]
    top = [None] * RI
    for z in range(NZ):
        tail = in_ref[z].astype(f32)[24:32, :]
        for k in range(RI):
            value = tail[:, 3 * k : 3 * k + 1] + tail[:, 3 * k + 1 : 3 * k + 2]
            value = value + tail[:, 3 * k + 2 : 3 * k + 3]
            level[z][k] = value
            top[k] = value if z == 0 else jnp.maximum(top[k], value)
    numer = jnp.zeros((8 * RI, HD), f32)
    total = jnp.zeros((8 * RI, 1), f32)
    for z in range(NZ):
        factor = jnp.concatenate([jnp.exp2(level[z][k] - top[k]) for k in range(RI)], axis=0)
        numer = numer + in_ref[z].astype(f32)[: 8 * RI, :] * factor
        total = total + factor
    result = (numer / total).astype(bf16)
    for z in range(NZ):
        out_ref[z] = result


def output_kernel(heads_ref, *refs):
    weight_refs, out_ref = refs[:NX], refs[NX]
    rows = heads_ref[...]
    bands = []
    for i in range(RI):
        at = i * GQ * TILE
        bands.append(
            jnp.concatenate([rows[at + g * TILE : at + (g + 1) * TILE, :] for g in range(GQ)], axis=1)
        )
    attended = jnp.concatenate(bands, axis=0)
    for x in range(NX):
        term = jnp.dot(attended, weight_refs[x][...], preferred_element_type=f32).astype(bf16)
        for h in range(NH):
            out_ref[h, :, x * HD : (x + 1) * HD] = term


def next_kernel(terms_ref, hidden_ref, gain_ref, *refs):
    weight_refs, resid_refs, (out_ref, cut_ref) = refs[:NX], refs[NX : 2 * NX], refs[2 * NX :]
    attended = terms_ref[0].astype(f32)
    for h in range(1, NH):
        attended = attended + terms_ref[h].astype(f32)
    squares = jnp.zeros((XR, 1), f32)
    product = jnp.zeros((XR, (GQ + 2) * HD), f32)
    for x in range(NX):
        before = jnp.concatenate([hidden_ref[x, i] for i in range(RI)], axis=0).astype(f32)
        resid = before + attended[:, x * HD : (x + 1) * HD]
        resid_refs[x][...] = resid.astype(bf16)
        squares = squares + jnp.sum(resid * resid, axis=1, keepdims=True)
        gained = (resid * gain_ref[x : x + 1, :]).astype(bf16)
        product = product + jnp.dot(gained, weight_refs[x][...], preferred_element_type=f32)
    for i in range(RI):
        for j in range(GQ + 2):
            cut_ref[:, i * (GQ + 2) + j, :] = product[
                i * TILE : (i + 1) * TILE, j * HD : (j + 1) * HD
            ]
    lane = lax.broadcasted_iota(jnp.int32, (TILE, HD), 1)
    tail = jnp.zeros((TILE, HD), f32)
    for i in range(RI):
        for p, piece in enumerate(three_pieces(squares[i * TILE : (i + 1) * TILE, :])):
            tail = jnp.where(lane == 3 * i + p, piece, tail)
    cut_ref[:, 30, :] = tail
    cut_ref[:, 31, :] = jnp.zeros((TILE, HD), f32)
    out_ref[...] = cut_ref[...].astype(bf16)


def finish_kernel(in_ref, out_ref):
    total = in_ref[0].astype(f32)
    for z in range(1, NZ):
        total = total + in_ref[z].astype(f32)
    rows = []
    for i in range(RI):
        squares = total[30:31, 3 * i : 3 * i + 1] + total[30:31, 3 * i + 1 : 3 * i + 2]
        squares = squares + total[30:31, 3 * i + 2 : 3 * i + 3]
        factor = lax.rsqrt(squares / D + epsilon)
        at = i * (GQ + 2)
        rows.append(
            jnp.concatenate(
                [total[at + j : at + j + 1, :] * factor for j in range(GQ + 2)], axis=1
            )
        )
    out_ref[...] = jnp.concatenate(rows, axis=0).astype(bf16)


def reorder_kernel(x_ref, *refs):
    in_refs, out_ref = refs[:NX], refs[NX]
    rows = out_ref.shape[0]
    new = lax.broadcasted_iota(jnp.int32, (rows, 1), 0)
    source = ((new // RI) % NX + NX - x_ref[0]) % NX
    src = source * XR + (new % RI) * NZ + new // (NX * RI)
    chosen = lax.broadcasted_iota(jnp.int32, (rows, rows), 1) == src
    data = jnp.concatenate([ref[...] for ref in in_refs], axis=0)
    out_ref[...] = jnp.dot(
        jnp.where(chosen, 1.0, 0.0).astype(bf16), data, preferred_element_type=f32
    ).astype(bf16)


def key_layout(owners, group_lengths, group_owner, group_start, listed_rows, blocks):
    length = group_lengths // BLK
    holder = (group_owner[None, :] == owners[:, None]).astype(jnp.int32)
    count = group_owner.shape[0]
    before = jnp.arange(count)[None, :] < jnp.arange(count)[:, None]
    held = holder * length[None, :]
    offset = jnp.sum(jnp.where(before[None], held[:, None, :], 0), axis=2)
    ids = jnp.arange(blocks, dtype=jnp.int32)[None, :, None]
    member = (
        (holder[:, None, :] == 1)
        & (ids >= offset[:, None, :])
        & (ids < offset[:, None, :] + length[None, None, :])
    ).astype(jnp.int32)
    start = group_start[None, None, :]
    shift = jnp.sum(member * start, axis=2)
    begin = jnp.sum(member * (start + (ids - offset[:, None, :]) * BLK), axis=2)
    live = jnp.sum(member, axis=2) > 0
    position = begin[:, :, None] + jnp.arange(BLK, dtype=jnp.int32)
    hit = jnp.any(position[..., None] == listed_rows, axis=-1)
    position = jnp.where(live[:, :, None] & ~hit, position, never)
    return shift, position.reshape(NX * blocks, BLK)


def on_device(
    hidden_rows,
    qkv_weight,
    out_weight,
    norm_gain,
    next_weight,
    cache_keys,
    cache_values,
    group_lengths,
    group_owner,
    group_start,
    listed_rows,
):
    z = lax.axis_index("z")
    x = lax.axis_index("x")
    held = cache_keys.shape[0]
    blocks = held // BLK
    a2a = functools.partial(lax.all_to_all, split_axis=0, concat_axis=0, tiled=True)

    def shifted(array, step):
        return lax.ppermute(array, "x", [(n, (n + step) % NX) for n in range(NX)])

    def after(array, *first):
        return lax.optimization_barrier((array, *first))[0]

    payload = vmem_call(
        project_kernel,
        shaped((NX, HT + RI + 1, TILE, HD), bf16),
        (hidden_rows, qkv_weight, norm_gain.reshape(1, HD)),
        scratch=[
            pltpu.VMEM(hidden_rows.shape, bf16),
            pltpu.VMEM(qkv_weight.shape, bf16),
            pltpu.VMEM((1, HD), f32),
            pltpu.SemaphoreType.DMA((3,)),
        ],
        hbm=True,
        limit=60,
    )
    payload = a2a(payload, "x")

    sources = (x + NX - jnp.arange(NX, dtype=jnp.int32)) % NX
    shift, key_pos = key_layout(
        z * NX + sources, group_lengths, group_owner, group_start, listed_rows, blocks
    )
    by_zxi = listed_rows.reshape(NZ, NX, RI)
    row_pos = lax.dynamic_slice_in_dim(by_zxi, x, 1, axis=1)[:, 0].T
    new_pos = lax.dynamic_slice_in_dim(by_zxi, z, 1, axis=0).reshape(-1)
    own = 8 * RI * z + jnp.arange(8 * RI)
    chosen = (own // HD * NZ + own % NZ)[:, None] == jnp.arange(XR)[None, :]
    query_pos = jnp.sum(jnp.where(chosen, row_pos.reshape(1, XR), 0), axis=1)
    rest = jnp.full((BLK - NX * RI,), never, jnp.int32)
    key_pos = jnp.concatenate([key_pos, jnp.concatenate([new_pos, rest])[None]], axis=0)
    wide_row_pos = jnp.broadcast_to(row_pos[:, :, None], (RI, NZ, BLK))
    cosine, sine = rope_factors(
        jnp.concatenate([query_pos, new_pos, jnp.zeros((NX * RI,), jnp.int32), shift[0]])
    )
    rows = 8 * RI + KT
    cache = vmem_call(
        bundle_kernel,
        shaped((2 * blocks, BLK, HD), bf16),
        (cache_keys, cache_values, cosine[rows:], sine[rows:]),
    )

    x_scalar = x.reshape(1).astype(jnp.int32)
    tiles, hidden_x, gain_x = vmem_call(
        sum_x_kernel,
        (
            shaped((NZ, rows, HD), bf16),
            shaped((NX, RI, TILE, HD), bf16),
            shaped((NX, HD), f32),
        ),
        (x_scalar, payload),
        scratch=[pltpu.VMEM((NZ, KT, HD), f32)],
        scalars=1,
    )
    caches = {0: cache} | {step: shifted(after(cache, tiles), step) for step in (2, 1)}
    copies, new = vmem_call(
        rope_kernel,
        (shaped((NZ, 8 * RI, HD), bf16), shaped((2, FRESH, HD), bf16)),
        (a2a(tiles, "z"), cosine[:rows], sine[:rows]),
    )
    caches[3] = shifted(after(cache, copies), 3)
    queries = a2a(copies, "z").reshape(XR * GQ, HD)
    parts = vmem_call(
        attend_kernel,
        shaped((NZ, 32, HD), bf16),
        (queries, key_pos, wide_row_pos, new, *(caches[step] for step in range(NX))),
        scratch=[pltpu.VMEM((HD, (NX * blocks + 2 * RI) * BLK), f32)],
    )
    outs = {0: out_weight} | {step: shifted(after(out_weight, parts), step) for step in (2, 1)}
    share = vmem_call(
        combine_kernel, shaped((NZ, 8 * RI, HD), bf16), (a2a(parts, "z"),)
    )
    outs[3] = shifted(after(out_weight, share), 3)
    nexts = {0: next_weight, 2: shifted(after(next_weight, share, outs[1], outs[2]), 2)}
    heads_out = a2a(share, "z").reshape(XR * GQ, HD)
    terms = vmem_call(
        output_kernel,
        shaped((NH, XR, NX * HD), bf16),
        (heads_out, *(outs[step] for step in range(NX))),
    )
    nexts |= {step: shifted(after(next_weight, terms, nexts[2]), step) for step in (1, 3)}
    *resids, products = vmem_call(
        next_kernel,
        (*[shaped((XR, HD), bf16)] * NX, shaped((NZ, 32, HD), bf16)),
        (a2a(terms, "heads"), hidden_x, gain_x, *(nexts[step] for step in range(NX))),
        scratch=[pltpu.VMEM((NZ, 32, HD), f32)],
    )
    resids = [resids[0]] + [shifted(resids[s], NX - s) for s in range(1, NX)]
    hidden_out = vmem_call(
        reorder_kernel, shaped(hidden_rows.shape, bf16), (x_scalar, *resids), scalars=1
    )
    next_qkv = vmem_call(
        finish_kernel, shaped((RI, (GQ + 2) * HD), bf16), (a2a(products, "z"),)
    )
    return hidden_out, next_qkv


def solution(mesh):
    split = Mesh(mesh.devices.reshape(NH, NZ, NX), ("heads", "z", "x"))
    return jax.shard_map(
        on_device,
        mesh=split,
        in_specs=(
            P(None, GROUPS),
            P(GROUPS, "heads"),
            P("heads", GROUPS),
            P(GROUPS),
            P(GROUPS, "heads"),
            P(GROUPS, "heads"),
            P(GROUPS, "heads"),
            P(),
            P(),
            P(),
            P(),
        ),
        out_specs=(P(None, GROUPS), P(GROUPS, "heads")),
        check_vma=False,
    )
```

```python
import functools

import jax
import jax.numpy as jnp
from jax import lax
from jax.experimental import pallas as pl
from jax.experimental.pallas import tpu as pltpu
from jax.sharding import Mesh
from jax.sharding import PartitionSpec as P

D = 8192
HD = 128
GQ = 8
BLK = 128
NZ = 16
NX = 4
NH = 8
FRESH = 16
RI = 3
XR = NZ * RI
TILE = 16
QT = RI * GQ
KT = 2 * NX * RI
HT = QT + KT
GROUPS = ("z", "x")
theta_base = 500000.0
epsilon = 1e-05
masked_score = -1e30
least_peak = -1e28
never = 2**30
LOG2E = 1.4426950408889634

bf16 = jnp.bfloat16
f32 = jnp.float32


def vmem_call(kernel, out_shape, operands, scratch=(), limit=12, scalars=0, hbm=False):
    space = pl.BlockSpec(memory_space=pltpu.VMEM)
    outs = jax.tree.map(lambda _: space, out_shape)
    rest = pl.BlockSpec(memory_space=pltpu.HBM) if hbm else space
    small = pl.BlockSpec(memory_space=pltpu.SMEM)
    return pl.pallas_call(
        kernel,
        out_shape=out_shape,
        in_specs=[small] * scalars + [rest] * (len(operands) - scalars),
        out_specs=outs,
        scratch_shapes=list(scratch),
        compiler_params=pltpu.CompilerParams(vmem_limit_bytes=limit * 2**20),
    )(*operands)


def shaped(shape, dtype):
    return jax.ShapeDtypeStruct(shape, dtype)


def three_pieces(value):
    high = value.astype(bf16).astype(f32)
    rest = value - high
    middle = rest.astype(bf16).astype(f32)
    low = (rest - middle).astype(bf16).astype(f32)
    return high, middle, low


def angles(positions, half_dim):
    freq = theta_base ** (-(jnp.arange(half_dim).astype(f32) * 2.0 / (2 * half_dim)))
    phase = positions.astype(f32)[:, None] * freq[None, :]
    return (jnp.cos(phase), jnp.sin(phase))


def rope_factors(positions):
    cosine, sine = angles(positions, HD // 2)
    return jnp.concatenate([cosine, cosine], -1), jnp.concatenate([-sine, sine], -1)


def bundle_kernel(keys_ref, values_ref, cos_ref, sin_ref, out_weight_ref, next_weight_ref, cache_ref, weights_ref, both_ref):
    blocks = keys_ref.shape[0] // BLK
    for b in range(blocks):
        values = values_ref[b * BLK : (b + 1) * BLK, :]
        cache_ref[blocks + b] = values
        both_ref[blocks + b] = values
        block = keys_ref[b * BLK : (b + 1) * BLK, :].astype(f32)
        turned = (
            block * cos_ref[b : b + 1, :]
            + pltpu.roll(block, HD // 2, 1) * sin_ref[b : b + 1, :]
        )
        turned = turned.astype(bf16).astype(f32)
        turned = turned.T.astype(bf16)
        cache_ref[b] = turned
        both_ref[b] = turned
    for g in range(GQ):
        block = out_weight_ref[g * HD : (g + 1) * HD, :]
        weights_ref[g] = block
        both_ref[2 * blocks + g] = block
    for j in range(GQ + 2):
        block = next_weight_ref[:, j * HD : (j + 1) * HD]
        weights_ref[GQ + j] = block
        both_ref[2 * blocks + GQ + j] = block


def project_kernel(hidden_hbm, weight_hbm, gain_hbm, out_ref, hidden_ref, weight_ref, gain_ref, sems):
    copies = [
        pltpu.make_async_copy(src, dst, sems.at[n])
        for n, (src, dst) in enumerate(
            ((hidden_hbm, hidden_ref), (gain_hbm, gain_ref), (weight_hbm, weight_ref))
        )
    ]
    for copy in copies:
        copy.start()
    rows = hidden_ref.shape[0]
    new = lax.broadcasted_iota(jnp.int32, (rows, 1), 0)
    src = (new % NZ) * (NX * RI) + (new // XR) * RI + (new % XR) // NZ
    chosen = lax.broadcasted_iota(jnp.int32, (rows, rows), 1) == src
    choice = jnp.where(chosen, 1.0, 0.0).astype(bf16)
    copies[0].wait()
    copies[1].wait()
    moved = jnp.dot(
        choice, hidden_ref[...], preferred_element_type=f32
    ).astype(bf16)
    high, middle, low = three_pieces(gain_ref[...])
    sub = lax.broadcasted_iota(jnp.int32, (TILE, HD), 0)
    gain = jnp.where(
        sub == 0, high, jnp.where(sub == 1, middle, jnp.where(sub == 2, low, 0.0))
    ).astype(bf16)
    copies[2].wait()
    for x in range(NX):
        part = moved[x * XR : (x + 1) * XR, :]
        product = jnp.dot(part, weight_ref[...], preferred_element_type=f32).astype(bf16)
        for i in range(RI):
            band = product[i * TILE : (i + 1) * TILE, :]
            for j in range(GQ):
                out_ref[x, i * GQ + j] = band[:, j * HD : (j + 1) * HD]
            for j in range(2):
                tile = band[:, (GQ + j) * HD : (GQ + j + 1) * HD]
                for to in range(NX):
                    out_ref[to, QT + j * NX * RI + x * RI + i] = tile
            out_ref[x, HT + i] = part[i * TILE : (i + 1) * TILE, :]
        out_ref[x, HT + RI] = gain


def sum_x_kernel(x_ref, in_ref, tiles_ref, hidden_ref, gain_ref, cut_ref):
    def total(t):
        result = in_ref[0, t].astype(f32)
        for x in range(1, NX):
            result = result + in_ref[x, t].astype(f32)
        return result

    for k in range(KT):
        cut_ref[:, k, :] = total(QT + k)
    rows = [total(t) for t in range(QT)]
    halves = [row[h * 8 : (h + 1) * 8, :] for row in rows for h in range(2)]
    for z in range(NZ):
        block = halves[z * RI : (z + 1) * RI] + [cut_ref[z]]
        tiles_ref[z] = jnp.concatenate(block, axis=0).astype(bf16)
    for s in range(NX):
        src = (x_ref[0] + NX - s) % NX
        for i in range(RI):
            hidden_ref[s, i] = in_ref[src, HT + i]
        pieces = in_ref[src, HT + RI].astype(f32)
        gain_ref[s : s + 1, :] = pieces[0:1] + pieces[1:2] + pieces[2:3]


def rope_kernel(in_ref, cos_ref, sin_ref, copies_ref, new_ref):
    total = in_ref[0].astype(f32)
    for z in range(1, NZ):
        total = total + in_ref[z].astype(f32)
    turned = total * cos_ref[...] + pltpu.roll(total, HD // 2, 1) * sin_ref[...]
    queries = turned[: 8 * RI, :].astype(bf16)
    for z in range(NZ):
        copies_ref[z] = queries
    new = turned[8 * RI :, :]
    pad = jnp.zeros((FRESH - NX * RI, HD), f32)
    new_ref[0] = jnp.concatenate([new[: NX * RI, :], pad], axis=0).astype(bf16)
    new_ref[1] = jnp.concatenate([new[NX * RI :, :], pad], axis=0).astype(bf16)


def attend_kernel(queries_ref, keypos_ref, rowpos_ref, new_ref, *refs):
    cache_refs, (out_ref, score_ref) = refs[:NX], refs[NX:]
    blocks = (keypos_ref.shape[0] - 1) // NX
    scale = HD ** (-0.5) * LOG2E
    contract_last = (((1,), (1,)), ((), ()))
    new_keys, new_values = new_ref[0], new_ref[1]
    fresh = new_keys.shape[0]
    every = queries_ref[...]
    for i in range(RI):
        queries = every[i * HD : (i + 1) * HD, :]
        row_pos = jnp.concatenate([rowpos_ref[i]] * GQ, axis=0)
        peak = jnp.full((HD, BLK), least_peak, f32)
        for x in range(NX):
            keys = jnp.concatenate([cache_refs[x][b] for b in range(blocks)], axis=1)
            score = jnp.dot(queries, keys, preferred_element_type=f32)
            for b in range(blocks):
                n = x * blocks + b
                cut = jnp.where(
                    keypos_ref[n : n + 1, :] <= row_pos,
                    score[:, b * BLK : (b + 1) * BLK],
                    masked_score,
                )
                score_ref[:, n * BLK : (n + 1) * BLK] = cut
                peak = jnp.maximum(peak, cut)
        n = NX * blocks
        score = lax.dot_general(queries, new_keys, contract_last, preferred_element_type=f32)
        last = jnp.where(keypos_ref[n : n + 1, :fresh] <= row_pos[:, :fresh], score, masked_score)
        top = jnp.maximum(
            jnp.max(peak, axis=1, keepdims=True), jnp.max(last, axis=1, keepdims=True)
        )
        top = top * scale
        weight = jnp.exp2(last * scale - top)
        total_last = jnp.sum(weight, axis=1, keepdims=True)
        numer = jnp.dot(weight.astype(bf16), new_values, preferred_element_type=f32)
        total = jnp.zeros((HD, BLK), f32)
        for x in range(NX):
            weights = []
            for b in range(blocks):
                n = x * blocks + b
                weight = jnp.exp2(score_ref[:, n * BLK : (n + 1) * BLK] * scale - top)
                total = total + weight
                weights.append(weight.astype(bf16))
            values = jnp.concatenate([cache_refs[x][blocks + b] for b in range(blocks)], axis=0)
            numer = numer + jnp.dot(
                jnp.concatenate(weights, axis=1), values, preferred_element_type=f32
            )
        total = jnp.sum(total, axis=1, keepdims=True) + total_last
        some = total > 0.0
        share = numer * jnp.where(some, 1.0 / jnp.where(some, total, 1.0), 0.0)
        level = top + jnp.where(some, jnp.log2(jnp.where(some, total, 1.0)), 0.0)
        share_at = (NX * blocks + i) * BLK
        score_ref[:, share_at : share_at + BLK] = share
        level_at = (NX * blocks + RI + i) * BLK
        score_ref[:, level_at : level_at + BLK] = jnp.broadcast_to(level, (HD, BLK))
    lane = lax.broadcasted_iota(jnp.int32, (8, HD), 1)
    for z in range(NZ):
        parts = []
        tail = jnp.zeros((8, HD), f32)
        for k in range(RI):
            row = 24 * z + 8 * k
            i, r = row // HD, row % HD
            share_at = (NX * blocks + i) * BLK
            level_at = (NX * blocks + RI + i) * BLK
            parts.append(score_ref[r : r + 8, share_at : share_at + BLK])
            for p, piece in enumerate(three_pieces(score_ref[r : r + 8, level_at : level_at + BLK])):
                tail = jnp.where(lane == 3 * k + p, piece, tail)
        out_ref[z] = jnp.concatenate(parts + [tail], axis=0).astype(bf16)


def combine_kernel(in_ref, out_ref):
    level = [[None] * RI for _ in range(NZ)]
    top = [None] * RI
    for z in range(NZ):
        tail = in_ref[z].astype(f32)[24:32, :]
        for k in range(RI):
            value = tail[:, 3 * k : 3 * k + 1] + tail[:, 3 * k + 1 : 3 * k + 2]
            value = value + tail[:, 3 * k + 2 : 3 * k + 3]
            level[z][k] = value
            top[k] = value if z == 0 else jnp.maximum(top[k], value)
    numer = jnp.zeros((8 * RI, HD), f32)
    total = jnp.zeros((8 * RI, 1), f32)
    for z in range(NZ):
        factor = jnp.concatenate([jnp.exp2(level[z][k] - top[k]) for k in range(RI)], axis=0)
        numer = numer + in_ref[z].astype(f32)[: 8 * RI, :] * factor
        total = total + factor
    result = (numer / total).astype(bf16)
    for z in range(NZ):
        out_ref[z] = result


def weight_blocks(refs, first, count):
    return [ref.at[pl.ds(ref.shape[0] - (2 * GQ + 2) + first, count)] for ref in refs]


def output_kernel(heads_ref, *refs):
    weight_refs, out_ref = weight_blocks(refs[:NX], 0, GQ), refs[NX]
    rows = heads_ref[...]
    bands = []
    for i in range(RI):
        at = i * GQ * TILE
        bands.append(
            jnp.concatenate([rows[at + g * TILE : at + (g + 1) * TILE, :] for g in range(GQ)], axis=1)
        )
    attended = jnp.concatenate(bands, axis=0)
    for x in range(NX):
        term = jnp.dot(attended, weight_refs[x][...].reshape(GQ * HD, HD), preferred_element_type=f32).astype(bf16)
        for h in range(NH):
            out_ref[h, :, x * HD : (x + 1) * HD] = term


def next_kernel(terms_ref, hidden_ref, gain_ref, *refs):
    weight_refs = weight_blocks(refs[:NX], GQ, GQ + 2)
    resid_refs, (out_ref, cut_ref) = refs[NX : 2 * NX], refs[2 * NX :]
    attended = terms_ref[0].astype(f32)
    for h in range(1, NH):
        attended = attended + terms_ref[h].astype(f32)
    squares = jnp.zeros((XR, 1), f32)
    product = jnp.zeros((XR, (GQ + 2) * HD), f32)
    for x in range(NX):
        before = jnp.concatenate([hidden_ref[x, i] for i in range(RI)], axis=0).astype(f32)
        resid = before + attended[:, x * HD : (x + 1) * HD]
        resid_refs[x][...] = resid.astype(bf16)
        squares = squares + jnp.sum(resid * resid, axis=1, keepdims=True)
        gained = (resid * gain_ref[x : x + 1, :]).astype(bf16)
        weight = jnp.concatenate([weight_refs[x][j] for j in range(GQ + 2)], axis=1)
        product = product + jnp.dot(gained, weight, preferred_element_type=f32)
    for i in range(RI):
        for j in range(GQ + 2):
            cut_ref[:, i * (GQ + 2) + j, :] = product[
                i * TILE : (i + 1) * TILE, j * HD : (j + 1) * HD
            ]
    lane = lax.broadcasted_iota(jnp.int32, (TILE, HD), 1)
    tail = jnp.zeros((TILE, HD), f32)
    for i in range(RI):
        for p, piece in enumerate(three_pieces(squares[i * TILE : (i + 1) * TILE, :])):
            tail = jnp.where(lane == 3 * i + p, piece, tail)
    cut_ref[:, 30, :] = tail
    cut_ref[:, 31, :] = jnp.zeros((TILE, HD), f32)
    out_ref[...] = cut_ref[...].astype(bf16)


def finish_kernel(in_ref, out_ref):
    total = in_ref[0].astype(f32)
    for z in range(1, NZ):
        total = total + in_ref[z].astype(f32)
    rows = []
    for i in range(RI):
        squares = total[30:31, 3 * i : 3 * i + 1] + total[30:31, 3 * i + 1 : 3 * i + 2]
        squares = squares + total[30:31, 3 * i + 2 : 3 * i + 3]
        factor = lax.rsqrt(squares / D + epsilon)
        at = i * (GQ + 2)
        rows.append(
            jnp.concatenate(
                [total[at + j : at + j + 1, :] * factor for j in range(GQ + 2)], axis=1
            )
        )
    out_ref[...] = jnp.concatenate(rows, axis=0).astype(bf16)


def reorder_kernel(x_ref, *refs):
    in_refs, out_ref = refs[:NX], refs[NX]
    rows = out_ref.shape[0]
    new = lax.broadcasted_iota(jnp.int32, (rows, 1), 0)
    source = ((new // RI) % NX + NX - x_ref[0]) % NX
    src = source * XR + (new % RI) * NZ + new // (NX * RI)
    chosen = lax.broadcasted_iota(jnp.int32, (rows, rows), 1) == src
    data = jnp.concatenate([ref[...] for ref in in_refs], axis=0)
    out_ref[...] = jnp.dot(
        jnp.where(chosen, 1.0, 0.0).astype(bf16), data, preferred_element_type=f32
    ).astype(bf16)


def key_layout(owners, group_lengths, group_owner, group_start, listed_rows, blocks):
    length = group_lengths // BLK
    holder = (group_owner[None, :] == owners[:, None]).astype(jnp.int32)
    count = group_owner.shape[0]
    before = jnp.arange(count)[None, :] < jnp.arange(count)[:, None]
    held = holder * length[None, :]
    offset = jnp.sum(jnp.where(before[None], held[:, None, :], 0), axis=2)
    ids = jnp.arange(blocks, dtype=jnp.int32)[None, :, None]
    member = (
        (holder[:, None, :] == 1)
        & (ids >= offset[:, None, :])
        & (ids < offset[:, None, :] + length[None, None, :])
    ).astype(jnp.int32)
    start = group_start[None, None, :]
    shift = jnp.sum(member * start, axis=2)
    begin = jnp.sum(member * (start + (ids - offset[:, None, :]) * BLK), axis=2)
    live = jnp.sum(member, axis=2) > 0
    position = begin[:, :, None] + jnp.arange(BLK, dtype=jnp.int32)
    hit = jnp.any(position[..., None] == listed_rows, axis=-1)
    position = jnp.where(live[:, :, None] & ~hit, position, never)
    return shift, position.reshape(NX * blocks, BLK)


def on_device(
    hidden_rows,
    qkv_weight,
    out_weight,
    norm_gain,
    next_weight,
    cache_keys,
    cache_values,
    group_lengths,
    group_owner,
    group_start,
    listed_rows,
):
    z = lax.axis_index("z")
    x = lax.axis_index("x")
    held = cache_keys.shape[0]
    blocks = held // BLK
    a2a = functools.partial(lax.all_to_all, split_axis=0, concat_axis=0, tiled=True)

    def shifted(array, step):
        return lax.ppermute(array, "x", [(n, (n + step) % NX) for n in range(NX)])

    payload = vmem_call(
        project_kernel,
        shaped((NX, HT + RI + 1, TILE, HD), bf16),
        (hidden_rows, qkv_weight, norm_gain.reshape(1, HD)),
        scratch=[
            pltpu.VMEM(hidden_rows.shape, bf16),
            pltpu.VMEM(qkv_weight.shape, bf16),
            pltpu.VMEM((1, HD), f32),
            pltpu.SemaphoreType.DMA((3,)),
        ],
        hbm=True,
        limit=60,
    )
    payload = a2a(payload, "x")

    sources = (x + NX - jnp.arange(NX, dtype=jnp.int32)) % NX
    shift, key_pos = key_layout(
        z * NX + sources, group_lengths, group_owner, group_start, listed_rows, blocks
    )
    by_zxi = listed_rows.reshape(NZ, NX, RI)
    row_pos = lax.dynamic_slice_in_dim(by_zxi, x, 1, axis=1)[:, 0].T
    new_pos = lax.dynamic_slice_in_dim(by_zxi, z, 1, axis=0).reshape(-1)
    own = 8 * RI * z + jnp.arange(8 * RI)
    chosen = (own // HD * NZ + own % NZ)[:, None] == jnp.arange(XR)[None, :]
    query_pos = jnp.sum(jnp.where(chosen, row_pos.reshape(1, XR), 0), axis=1)
    rest = jnp.full((BLK - NX * RI,), never, jnp.int32)
    key_pos = jnp.concatenate([key_pos, jnp.concatenate([new_pos, rest])[None]], axis=0)
    wide_row_pos = jnp.broadcast_to(row_pos[:, :, None], (RI, NZ, BLK))
    cosine, sine = rope_factors(
        jnp.concatenate([query_pos, new_pos, jnp.zeros((NX * RI,), jnp.int32), shift[0]])
    )
    rows = 8 * RI + KT
    counts = (2 * blocks, 2 * GQ + 2, 2 * blocks + 2 * GQ + 2)
    cache, weights, both = vmem_call(
        bundle_kernel,
        tuple(shaped((count, HD, HD), bf16) for count in counts),
        (cache_keys, cache_values, cosine[rows:], sine[rows:], out_weight, next_weight),
    )

    x_scalar = x.reshape(1).astype(jnp.int32)
    tiles, hidden_x, gain_x = vmem_call(
        sum_x_kernel,
        (
            shaped((NZ, rows, HD), bf16),
            shaped((NX, RI, TILE, HD), bf16),
            shaped((NX, HD), f32),
        ),
        (x_scalar, payload),
        scratch=[pltpu.VMEM((NZ, KT, HD), f32)],
        scalars=1,
    )
    tiles, cache, both = lax.optimization_barrier((tiles, cache, both))
    caches = [cache, shifted(cache, 1), shifted(cache, 2), shifted(both, 3)]
    copies, new = vmem_call(
        rope_kernel,
        (shaped((NZ, 8 * RI, HD), bf16), shaped((2, FRESH, HD), bf16)),
        (a2a(tiles, "z"), cosine[:rows], sine[:rows]),
    )
    queries = a2a(copies, "z").reshape(XR * GQ, HD)
    parts = vmem_call(
        attend_kernel,
        shaped((NZ, 32, HD), bf16),
        (queries, key_pos, wide_row_pos, new, *caches),
        scratch=[pltpu.VMEM((HD, (NX * blocks + 2 * RI) * BLK), f32)],
    )
    parts, weights = lax.optimization_barrier((parts, weights))
    weights_x = [weights, shifted(weights, 1), shifted(weights, 2), caches[3]]
    share = vmem_call(
        combine_kernel, shaped((NZ, 8 * RI, HD), bf16), (a2a(parts, "z"),)
    )
    heads_out = a2a(share, "z").reshape(XR * GQ, HD)
    terms = vmem_call(
        output_kernel, shaped((NH, XR, NX * HD), bf16), (heads_out, *weights_x)
    )
    *resids, products = vmem_call(
        next_kernel,
        (*[shaped((XR, HD), bf16)] * NX, shaped((NZ, 32, HD), bf16)),
        (a2a(terms, "heads"), hidden_x, gain_x, *weights_x),
        scratch=[pltpu.VMEM((NZ, 32, HD), f32)],
    )
    resids = [resids[0]] + [shifted(resids[s], NX - s) for s in range(1, NX)]
    hidden_out = vmem_call(
        reorder_kernel, shaped(hidden_rows.shape, bf16), (x_scalar, *resids), scalars=1
    )
    next_qkv = vmem_call(
        finish_kernel, shaped((RI, (GQ + 2) * HD), bf16), (a2a(products, "z"),)
    )
    return hidden_out, next_qkv


def solution(mesh):
    split = Mesh(mesh.devices.reshape(NH, NZ, NX), ("heads", "z", "x"))
    return jax.shard_map(
        on_device,
        mesh=split,
        in_specs=(
            P(None, GROUPS),
            P(GROUPS, "heads"),
            P("heads", GROUPS),
            P(GROUPS),
            P(GROUPS, "heads"),
            P(GROUPS, "heads"),
            P(GROUPS, "heads"),
            P(),
            P(),
            P(),
            P(),
        ),
        out_specs=(P(None, GROUPS), P(GROUPS, "heads")),
        check_vma=False,
    )
```

```python
import functools

import jax
import jax.numpy as jnp
from jax import lax
from jax.experimental import pallas as pl
from jax.experimental.pallas import tpu as pltpu
from jax.sharding import Mesh
from jax.sharding import PartitionSpec as P

D = 8192
HD = 128
GQ = 8
BLK = 128
NZ = 16
NX = 4
NH = 8
FRESH = 16
RI = 3
XR = NZ * RI
TILE = 16
QT = RI * GQ
KT = 2 * NX * RI
HT = QT + KT
GROUPS = ("z", "x")
theta_base = 500000.0
epsilon = 1e-05
masked_score = -1e30
least_peak = -1e28
never = 2**30
LOG2E = 1.4426950408889634

bf16 = jnp.bfloat16
f32 = jnp.float32


def vmem_call(kernel, out_shape, operands, scratch=(), limit=12, scalars=0, hbm=False):
    space = pl.BlockSpec(memory_space=pltpu.VMEM)
    outs = jax.tree.map(lambda _: space, out_shape)
    rest = pl.BlockSpec(memory_space=pltpu.HBM) if hbm else space
    small = pl.BlockSpec(memory_space=pltpu.SMEM)
    return pl.pallas_call(
        kernel,
        out_shape=out_shape,
        in_specs=[small] * scalars + [rest] * (len(operands) - scalars),
        out_specs=outs,
        scratch_shapes=list(scratch),
        compiler_params=pltpu.CompilerParams(vmem_limit_bytes=limit * 2**20),
    )(*operands)


def shaped(shape, dtype):
    return jax.ShapeDtypeStruct(shape, dtype)


def three_pieces(value):
    high = value.astype(bf16).astype(f32)
    rest = value - high
    middle = rest.astype(bf16).astype(f32)
    low = (rest - middle).astype(bf16).astype(f32)
    return high, middle, low


def angles(positions, half_dim):
    freq = theta_base ** (-(jnp.arange(half_dim).astype(f32) * 2.0 / (2 * half_dim)))
    phase = positions.astype(f32)[:, None] * freq[None, :]
    return (jnp.cos(phase), jnp.sin(phase))


def rope_factors(positions):
    cosine, sine = angles(positions, HD // 2)
    return jnp.concatenate([cosine, cosine], -1), jnp.concatenate([-sine, sine], -1)


def bundle_kernel(keys_ref, values_ref, cos_ref, sin_ref, out_weight_ref, next_weight_ref, cache_ref, weights_ref, both_ref):
    blocks = keys_ref.shape[0] // BLK
    for b in range(blocks):
        values = values_ref[b * BLK : (b + 1) * BLK, :]
        cache_ref[blocks + b] = values
        both_ref[blocks + b] = values
        block = keys_ref[b * BLK : (b + 1) * BLK, :].astype(f32)
        turned = (
            block * cos_ref[b : b + 1, :]
            + pltpu.roll(block, HD // 2, 1) * sin_ref[b : b + 1, :]
        )
        turned = turned.astype(bf16).astype(f32)
        turned = turned.T.astype(bf16)
        cache_ref[b] = turned
        both_ref[b] = turned
    for g in range(GQ):
        block = out_weight_ref[g * HD : (g + 1) * HD, :]
        weights_ref[g] = block
        both_ref[2 * blocks + g] = block
    for j in range(GQ + 2):
        block = next_weight_ref[:, j * HD : (j + 1) * HD]
        weights_ref[GQ + j] = block


def project_kernel(hidden_hbm, weight_hbm, gain_hbm, out_ref, hidden_ref, weight_ref, gain_ref, sems):
    copies = [
        pltpu.make_async_copy(src, dst, sems.at[n])
        for n, (src, dst) in enumerate(
            ((hidden_hbm, hidden_ref), (gain_hbm, gain_ref), (weight_hbm, weight_ref))
        )
    ]
    for copy in copies:
        copy.start()
    rows = hidden_ref.shape[0]
    new = lax.broadcasted_iota(jnp.int32, (rows, 1), 0)
    src = (new % NZ) * (NX * RI) + (new // XR) * RI + (new % XR) // NZ
    chosen = lax.broadcasted_iota(jnp.int32, (rows, rows), 1) == src
    choice = jnp.where(chosen, 1.0, 0.0).astype(bf16)
    copies[0].wait()
    copies[1].wait()
    moved = jnp.dot(
        choice, hidden_ref[...], preferred_element_type=f32
    ).astype(bf16)
    high, middle, low = three_pieces(gain_ref[...])
    sub = lax.broadcasted_iota(jnp.int32, (TILE, HD), 0)
    gain = jnp.where(
        sub == 0, high, jnp.where(sub == 1, middle, jnp.where(sub == 2, low, 0.0))
    ).astype(bf16)
    copies[2].wait()
    for x in range(NX):
        part = moved[x * XR : (x + 1) * XR, :]
        product = jnp.dot(part, weight_ref[...], preferred_element_type=f32).astype(bf16)
        for i in range(RI):
            band = product[i * TILE : (i + 1) * TILE, :]
            for j in range(GQ):
                out_ref[x, i * GQ + j] = band[:, j * HD : (j + 1) * HD]
            for j in range(2):
                tile = band[:, (GQ + j) * HD : (GQ + j + 1) * HD]
                for to in range(NX):
                    out_ref[to, QT + j * NX * RI + x * RI + i] = tile
            out_ref[x, HT + i] = part[i * TILE : (i + 1) * TILE, :]
        out_ref[x, HT + RI] = gain


def sum_x_kernel(x_ref, in_ref, tiles_ref, hidden_ref, gain_ref, cut_ref):
    def total(t):
        result = in_ref[0, t].astype(f32)
        for x in range(1, NX):
            result = result + in_ref[x, t].astype(f32)
        return result

    for k in range(KT):
        cut_ref[:, k, :] = total(QT + k)
    rows = [total(t) for t in range(QT)]
    halves = [row[h * 8 : (h + 1) * 8, :] for row in rows for h in range(2)]
    for z in range(NZ):
        block = halves[z * RI : (z + 1) * RI] + [cut_ref[z]]
        tiles_ref[z] = jnp.concatenate(block, axis=0).astype(bf16)
    for s in range(NX):
        src = (x_ref[0] + NX - s) % NX
        for i in range(RI):
            hidden_ref[s, i] = in_ref[src, HT + i]
        pieces = in_ref[src, HT + RI].astype(f32)
        gain_ref[s : s + 1, :] = pieces[0:1] + pieces[1:2] + pieces[2:3]


def rope_kernel(in_ref, cos_ref, sin_ref, copies_ref, new_ref):
    total = in_ref[0].astype(f32)
    for z in range(1, NZ):
        total = total + in_ref[z].astype(f32)
    turned = total * cos_ref[...] + pltpu.roll(total, HD // 2, 1) * sin_ref[...]
    queries = turned[: 8 * RI, :].astype(bf16)
    for z in range(NZ):
        copies_ref[z] = queries
    new = turned[8 * RI :, :]
    pad = jnp.zeros((FRESH - NX * RI, HD), f32)
    new_ref[0] = jnp.concatenate([new[: NX * RI, :], pad], axis=0).astype(bf16)
    new_ref[1] = jnp.concatenate([new[NX * RI :, :], pad], axis=0).astype(bf16)


def attend_kernel(queries_ref, keypos_ref, rowpos_ref, new_ref, *refs):
    cache_refs, (out_ref, score_ref) = refs[:NX], refs[NX:]
    blocks = (keypos_ref.shape[0] - 1) // NX
    scale = HD ** (-0.5) * LOG2E
    contract_last = (((1,), (1,)), ((), ()))
    new_keys, new_values = new_ref[0], new_ref[1]
    fresh = new_keys.shape[0]
    every = queries_ref[...]
    for i in range(RI):
        queries = every[i * HD : (i + 1) * HD, :]
        row_pos = jnp.concatenate([rowpos_ref[i]] * GQ, axis=0)
        peak = jnp.full((HD, BLK), least_peak, f32)
        for x in range(NX):
            keys = jnp.concatenate([cache_refs[x][b] for b in range(blocks)], axis=1)
            score = jnp.dot(queries, keys, preferred_element_type=f32)
            for b in range(blocks):
                n = x * blocks + b
                cut = jnp.where(
                    keypos_ref[n : n + 1, :] <= row_pos,
                    score[:, b * BLK : (b + 1) * BLK],
                    masked_score,
                )
                score_ref[:, n * BLK : (n + 1) * BLK] = cut
                peak = jnp.maximum(peak, cut)
        n = NX * blocks
        score = lax.dot_general(queries, new_keys, contract_last, preferred_element_type=f32)
        last = jnp.where(keypos_ref[n : n + 1, :fresh] <= row_pos[:, :fresh], score, masked_score)
        top = jnp.maximum(
            jnp.max(peak, axis=1, keepdims=True), jnp.max(last, axis=1, keepdims=True)
        )
        top = top * scale
        weight = jnp.exp2(last * scale - top)
        total_last = jnp.sum(weight, axis=1, keepdims=True)
        numer = jnp.dot(weight.astype(bf16), new_values, preferred_element_type=f32)
        total = jnp.zeros((HD, BLK), f32)
        for x in range(NX):
            weights = []
            for b in range(blocks):
                n = x * blocks + b
                weight = jnp.exp2(score_ref[:, n * BLK : (n + 1) * BLK] * scale - top)
                total = total + weight
                weights.append(weight.astype(bf16))
            values = jnp.concatenate([cache_refs[x][blocks + b] for b in range(blocks)], axis=0)
            numer = numer + jnp.dot(
                jnp.concatenate(weights, axis=1), values, preferred_element_type=f32
            )
        total = jnp.sum(total, axis=1, keepdims=True) + total_last
        some = total > 0.0
        share = numer * jnp.where(some, 1.0 / jnp.where(some, total, 1.0), 0.0)
        level = top + jnp.where(some, jnp.log2(jnp.where(some, total, 1.0)), 0.0)
        share_at = (NX * blocks + i) * BLK
        score_ref[:, share_at : share_at + BLK] = share
        level_at = (NX * blocks + RI + i) * BLK
        score_ref[:, level_at : level_at + BLK] = jnp.broadcast_to(level, (HD, BLK))
    lane = lax.broadcasted_iota(jnp.int32, (8, HD), 1)
    for z in range(NZ):
        parts = []
        tail = jnp.zeros((8, HD), f32)
        for k in range(RI):
            row = 24 * z + 8 * k
            i, r = row // HD, row % HD
            share_at = (NX * blocks + i) * BLK
            level_at = (NX * blocks + RI + i) * BLK
            parts.append(score_ref[r : r + 8, share_at : share_at + BLK])
            for p, piece in enumerate(three_pieces(score_ref[r : r + 8, level_at : level_at + BLK])):
                tail = jnp.where(lane == 3 * k + p, piece, tail)
        out_ref[z] = jnp.concatenate(parts + [tail], axis=0).astype(bf16)


def combine_kernel(in_ref, out_ref):
    level = [[None] * RI for _ in range(NZ)]
    top = [None] * RI
    for z in range(NZ):
        tail = in_ref[z].astype(f32)[24:32, :]
        for k in range(RI):
            value = tail[:, 3 * k : 3 * k + 1] + tail[:, 3 * k + 1 : 3 * k + 2]
            value = value + tail[:, 3 * k + 2 : 3 * k + 3]
            level[z][k] = value
            top[k] = value if z == 0 else jnp.maximum(top[k], value)
    numer = jnp.zeros((8 * RI, HD), f32)
    total = jnp.zeros((8 * RI, 1), f32)
    for z in range(NZ):
        factor = jnp.concatenate([jnp.exp2(level[z][k] - top[k]) for k in range(RI)], axis=0)
        numer = numer + in_ref[z].astype(f32)[: 8 * RI, :] * factor
        total = total + factor
    result = (numer / total).astype(bf16)
    for z in range(NZ):
        out_ref[z] = result


def output_kernel(heads_ref, *refs):
    weight_refs, out_ref = [ref.at[pl.ds(0, GQ)] for ref in refs[: NX - 1]], refs[NX]
    last = refs[NX - 1]
    weight_refs.append(last.at[pl.ds(last.shape[0] - GQ, GQ)])
    rows = heads_ref[...]
    bands = []
    for i in range(RI):
        at = i * GQ * TILE
        bands.append(
            jnp.concatenate([rows[at + g * TILE : at + (g + 1) * TILE, :] for g in range(GQ)], axis=1)
        )
    attended = jnp.concatenate(bands, axis=0)
    for x in range(NX):
        term = jnp.dot(attended, weight_refs[x][...].reshape(GQ * HD, HD), preferred_element_type=f32).astype(bf16)
        for h in range(NH):
            out_ref[h, :, x * HD : (x + 1) * HD] = term


def next_kernel(terms_ref, hidden_ref, gain_ref, *refs):
    wide = range(GQ, 2 * GQ + 2)
    weights = [jnp.concatenate([ref[j] for j in wide], axis=1) for ref in refs[: NX - 1]]
    weights.append(refs[NX - 1][...])
    resid_refs, (out_ref, cut_ref) = refs[NX : 2 * NX], refs[2 * NX :]
    attended = terms_ref[0].astype(f32)
    for h in range(1, NH):
        attended = attended + terms_ref[h].astype(f32)
    squares = jnp.zeros((XR, 1), f32)
    product = jnp.zeros((XR, (GQ + 2) * HD), f32)
    for x in range(NX):
        before = jnp.concatenate([hidden_ref[x, i] for i in range(RI)], axis=0).astype(f32)
        resid = before + attended[:, x * HD : (x + 1) * HD]
        resid_refs[x][...] = resid.astype(bf16)
        squares = squares + jnp.sum(resid * resid, axis=1, keepdims=True)
        gained = (resid * gain_ref[x : x + 1, :]).astype(bf16)
        product = product + jnp.dot(gained, weights[x], preferred_element_type=f32)
    for i in range(RI):
        for j in range(GQ + 2):
            cut_ref[:, i * (GQ + 2) + j, :] = product[
                i * TILE : (i + 1) * TILE, j * HD : (j + 1) * HD
            ]
    lane = lax.broadcasted_iota(jnp.int32, (TILE, HD), 1)
    tail = jnp.zeros((TILE, HD), f32)
    for i in range(RI):
        for p, piece in enumerate(three_pieces(squares[i * TILE : (i + 1) * TILE, :])):
            tail = jnp.where(lane == 3 * i + p, piece, tail)
    cut_ref[:, 30, :] = tail
    cut_ref[:, 31, :] = jnp.zeros((TILE, HD), f32)
    out_ref[...] = cut_ref[...].astype(bf16)


def finish_kernel(in_ref, out_ref):
    total = in_ref[0].astype(f32)
    for z in range(1, NZ):
        total = total + in_ref[z].astype(f32)
    rows = []
    for i in range(RI):
        squares = total[30:31, 3 * i : 3 * i + 1] + total[30:31, 3 * i + 1 : 3 * i + 2]
        squares = squares + total[30:31, 3 * i + 2 : 3 * i + 3]
        factor = lax.rsqrt(squares / D + epsilon)
        at = i * (GQ + 2)
        rows.append(
            jnp.concatenate(
                [total[at + j : at + j + 1, :] * factor for j in range(GQ + 2)], axis=1
            )
        )
    out_ref[...] = jnp.concatenate(rows, axis=0).astype(bf16)


def reorder_kernel(x_ref, *refs):
    in_refs, out_ref = refs[:NX], refs[NX]
    rows = out_ref.shape[0]
    new = lax.broadcasted_iota(jnp.int32, (rows, 1), 0)
    source = ((new // RI) % NX + NX - x_ref[0]) % NX
    src = source * XR + (new % RI) * NZ + new // (NX * RI)
    chosen = lax.broadcasted_iota(jnp.int32, (rows, rows), 1) == src
    data = jnp.concatenate([ref[...] for ref in in_refs], axis=0)
    out_ref[...] = jnp.dot(
        jnp.where(chosen, 1.0, 0.0).astype(bf16), data, preferred_element_type=f32
    ).astype(bf16)


def key_layout(owners, group_lengths, group_owner, group_start, listed_rows, blocks):
    length = group_lengths // BLK
    holder = (group_owner[None, :] == owners[:, None]).astype(jnp.int32)
    count = group_owner.shape[0]
    before = jnp.arange(count)[None, :] < jnp.arange(count)[:, None]
    held = holder * length[None, :]
    offset = jnp.sum(jnp.where(before[None], held[:, None, :], 0), axis=2)
    ids = jnp.arange(blocks, dtype=jnp.int32)[None, :, None]
    member = (
        (holder[:, None, :] == 1)
        & (ids >= offset[:, None, :])
        & (ids < offset[:, None, :] + length[None, None, :])
    ).astype(jnp.int32)
    start = group_start[None, None, :]
    shift = jnp.sum(member * start, axis=2)
    begin = jnp.sum(member * (start + (ids - offset[:, None, :]) * BLK), axis=2)
    live = jnp.sum(member, axis=2) > 0
    position = begin[:, :, None] + jnp.arange(BLK, dtype=jnp.int32)
    hit = jnp.any(position[..., None] == listed_rows, axis=-1)
    position = jnp.where(live[:, :, None] & ~hit, position, never)
    return shift, position.reshape(NX * blocks, BLK)


def on_device(
    hidden_rows,
    qkv_weight,
    out_weight,
    norm_gain,
    next_weight,
    cache_keys,
    cache_values,
    group_lengths,
    group_owner,
    group_start,
    listed_rows,
):
    z = lax.axis_index("z")
    x = lax.axis_index("x")
    held = cache_keys.shape[0]
    blocks = held // BLK
    a2a = functools.partial(lax.all_to_all, split_axis=0, concat_axis=0, tiled=True)

    def shifted(array, step):
        return lax.ppermute(array, "x", [(n, (n + step) % NX) for n in range(NX)])

    payload = vmem_call(
        project_kernel,
        shaped((NX, HT + RI + 1, TILE, HD), bf16),
        (hidden_rows, qkv_weight, norm_gain.reshape(1, HD)),
        scratch=[
            pltpu.VMEM(hidden_rows.shape, bf16),
            pltpu.VMEM(qkv_weight.shape, bf16),
            pltpu.VMEM((1, HD), f32),
            pltpu.SemaphoreType.DMA((3,)),
        ],
        hbm=True,
        limit=60,
    )
    payload = a2a(payload, "x")

    sources = (x + NX - jnp.arange(NX, dtype=jnp.int32)) % NX
    shift, key_pos = key_layout(
        z * NX + sources, group_lengths, group_owner, group_start, listed_rows, blocks
    )
    by_zxi = listed_rows.reshape(NZ, NX, RI)
    row_pos = lax.dynamic_slice_in_dim(by_zxi, x, 1, axis=1)[:, 0].T
    new_pos = lax.dynamic_slice_in_dim(by_zxi, z, 1, axis=0).reshape(-1)
    own = 8 * RI * z + jnp.arange(8 * RI)
    chosen = (own // HD * NZ + own % NZ)[:, None] == jnp.arange(XR)[None, :]
    query_pos = jnp.sum(jnp.where(chosen, row_pos.reshape(1, XR), 0), axis=1)
    rest = jnp.full((BLK - NX * RI,), never, jnp.int32)
    key_pos = jnp.concatenate([key_pos, jnp.concatenate([new_pos, rest])[None]], axis=0)
    wide_row_pos = jnp.broadcast_to(row_pos[:, :, None], (RI, NZ, BLK))
    cosine, sine = rope_factors(
        jnp.concatenate([query_pos, new_pos, jnp.zeros((NX * RI,), jnp.int32), shift[0]])
    )
    rows = 8 * RI + KT
    counts = (2 * blocks, 2 * GQ + 2, 2 * blocks + GQ)
    cache, weights, both = vmem_call(
        bundle_kernel,
        tuple(shaped((count, HD, HD), bf16) for count in counts),
        (cache_keys, cache_values, cosine[rows:], sine[rows:], out_weight, next_weight),
    )

    x_scalar = x.reshape(1).astype(jnp.int32)
    tiles, hidden_x, gain_x = vmem_call(
        sum_x_kernel,
        (
            shaped((NZ, rows, HD), bf16),
            shaped((NX, RI, TILE, HD), bf16),
            shaped((NX, HD), f32),
        ),
        (x_scalar, payload),
        scratch=[pltpu.VMEM((NZ, KT, HD), f32)],
        scalars=1,
    )
    tiles, cache, both = lax.optimization_barrier((tiles, cache, both))
    caches = [cache, shifted(cache, 1), shifted(cache, 2), shifted(both, 3)]
    copies, new = vmem_call(
        rope_kernel,
        (shaped((NZ, 8 * RI, HD), bf16), shaped((2, FRESH, HD), bf16)),
        (a2a(tiles, "z"), cosine[:rows], sine[:rows]),
    )
    queries = a2a(copies, "z").reshape(XR * GQ, HD)
    parts = vmem_call(
        attend_kernel,
        shaped((NZ, 32, HD), bf16),
        (queries, key_pos, wide_row_pos, new, *caches),
        scratch=[pltpu.VMEM((HD, (NX * blocks + 2 * RI) * BLK), f32)],
    )
    parts, weights = lax.optimization_barrier((parts, weights))
    weights_x = [weights, shifted(weights, 1), shifted(weights, 2)]
    share = vmem_call(
        combine_kernel, shaped((NZ, 8 * RI, HD), bf16), (a2a(parts, "z"),)
    )
    share, next_weight = lax.optimization_barrier((share, next_weight))
    next_last = shifted(next_weight, 3)
    heads_out = a2a(share, "z").reshape(XR * GQ, HD)
    terms = vmem_call(
        output_kernel, shaped((NH, XR, NX * HD), bf16), (heads_out, *weights_x, caches[3])
    )
    *resids, products = vmem_call(
        next_kernel,
        (*[shaped((XR, HD), bf16)] * NX, shaped((NZ, 32, HD), bf16)),
        (a2a(terms, "heads"), hidden_x, gain_x, *weights_x, next_last),
        scratch=[pltpu.VMEM((NZ, 32, HD), f32)],
    )
    resids = [resids[0]] + [shifted(resids[s], NX - s) for s in range(1, NX)]
    hidden_out = vmem_call(
        reorder_kernel, shaped(hidden_rows.shape, bf16), (x_scalar, *resids), scalars=1
    )
    next_qkv = vmem_call(
        finish_kernel, shaped((RI, (GQ + 2) * HD), bf16), (a2a(products, "z"),)
    )
    return hidden_out, next_qkv


def solution(mesh):
    split = Mesh(mesh.devices.reshape(NH, NZ, NX), ("heads", "z", "x"))
    return jax.shard_map(
        on_device,
        mesh=split,
        in_specs=(
            P(None, GROUPS),
            P(GROUPS, "heads"),
            P("heads", GROUPS),
            P(GROUPS),
            P(GROUPS, "heads"),
            P(GROUPS, "heads"),
            P(GROUPS, "heads"),
            P(),
            P(),
            P(),
            P(),
        ),
        out_specs=(P(None, GROUPS), P(GROUPS, "heads")),
        check_vma=False,
    )
```

```python
import functools

import jax
import jax.numpy as jnp
from jax import lax
from jax.experimental import pallas as pl
from jax.experimental.pallas import tpu as pltpu
from jax.sharding import Mesh
from jax.sharding import PartitionSpec as P

D = 8192
HD = 128
GQ = 8
BLK = 128
NZ = 16
NX = 4
NH = 8
FRESH = 16
RI = 3
XR = NZ * RI
TILE = 16
QT = RI * GQ
KT = 2 * NX * RI
HT = QT + KT
GROUPS = ("z", "x")
theta_base = 500000.0
epsilon = 1e-05
masked_score = -1e30
least_peak = -1e28
never = 2**30
LOG2E = 1.4426950408889634

bf16 = jnp.bfloat16
f32 = jnp.float32


def vmem_call(kernel, out_shape, operands, scratch=(), limit=12, scalars=0, hbm=False):
    space = pl.BlockSpec(memory_space=pltpu.VMEM)
    outs = jax.tree.map(lambda _: space, out_shape)
    rest = pl.BlockSpec(memory_space=pltpu.HBM) if hbm else space
    small = pl.BlockSpec(memory_space=pltpu.SMEM)
    return pl.pallas_call(
        kernel,
        out_shape=out_shape,
        in_specs=[small] * scalars + [rest] * (len(operands) - scalars),
        out_specs=outs,
        scratch_shapes=list(scratch),
        compiler_params=pltpu.CompilerParams(vmem_limit_bytes=limit * 2**20),
    )(*operands)


def shaped(shape, dtype):
    return jax.ShapeDtypeStruct(shape, dtype)


def three_pieces(value):
    high = value.astype(bf16).astype(f32)
    rest = value - high
    middle = rest.astype(bf16).astype(f32)
    low = (rest - middle).astype(bf16).astype(f32)
    return high, middle, low


def angles(positions, half_dim):
    freq = theta_base ** (-(jnp.arange(half_dim).astype(f32) * 2.0 / (2 * half_dim)))
    phase = positions.astype(f32)[:, None] * freq[None, :]
    return (jnp.cos(phase), jnp.sin(phase))


def rope_factors(positions):
    cosine, sine = angles(positions, HD // 2)
    return jnp.concatenate([cosine, cosine], -1), jnp.concatenate([-sine, sine], -1)


def bundle_kernel(keys_ref, values_ref, cos_ref, sin_ref, out_weight_ref, next_weight_ref, cache_ref, weights_ref):
    blocks = keys_ref.shape[0] // BLK
    for b in range(blocks):
        cache_ref[blocks + b] = values_ref[b * BLK : (b + 1) * BLK, :]
        block = keys_ref[b * BLK : (b + 1) * BLK, :].astype(f32)
        turned = (
            block * cos_ref[b : b + 1, :]
            + pltpu.roll(block, HD // 2, 1) * sin_ref[b : b + 1, :]
        )
        turned = turned.astype(bf16).astype(f32)
        cache_ref[b] = turned.T.astype(bf16)
    for g in range(GQ):
        weights_ref[g] = out_weight_ref[g * HD : (g + 1) * HD, :]
    for j in range(GQ + 2):
        weights_ref[GQ + j] = next_weight_ref[:, j * HD : (j + 1) * HD]


def project_kernel(hidden_hbm, weight_hbm, gain_hbm, out_ref, hidden_ref, weight_ref, gain_ref, sems):
    copies = [
        pltpu.make_async_copy(src, dst, sems.at[n])
        for n, (src, dst) in enumerate(
            ((hidden_hbm, hidden_ref), (gain_hbm, gain_ref), (weight_hbm, weight_ref))
        )
    ]
    for copy in copies:
        copy.start()
    rows = hidden_ref.shape[0]
    new = lax.broadcasted_iota(jnp.int32, (rows, 1), 0)
    src = (new % NZ) * (NX * RI) + (new // XR) * RI + (new % XR) // NZ
    chosen = lax.broadcasted_iota(jnp.int32, (rows, rows), 1) == src
    choice = jnp.where(chosen, 1.0, 0.0).astype(bf16)
    copies[0].wait()
    copies[1].wait()
    moved = jnp.dot(
        choice, hidden_ref[...], preferred_element_type=f32
    ).astype(bf16)
    high, middle, low = three_pieces(gain_ref[...])
    sub = lax.broadcasted_iota(jnp.int32, (TILE, HD), 0)
    gain = jnp.where(
        sub == 0, high, jnp.where(sub == 1, middle, jnp.where(sub == 2, low, 0.0))
    ).astype(bf16)
    copies[2].wait()
    for x in range(NX):
        part = moved[x * XR : (x + 1) * XR, :]
        product = jnp.dot(part, weight_ref[...], preferred_element_type=f32).astype(bf16)
        for i in range(RI):
            band = product[i * TILE : (i + 1) * TILE, :]
            for j in range(GQ):
                out_ref[x, i * GQ + j] = band[:, j * HD : (j + 1) * HD]
            for j in range(2):
                tile = band[:, (GQ + j) * HD : (GQ + j + 1) * HD]
                for to in range(NX):
                    out_ref[to, QT + j * NX * RI + x * RI + i] = tile
            out_ref[x, HT + i] = part[i * TILE : (i + 1) * TILE, :]
        out_ref[x, HT + RI] = gain


def sum_x_kernel(x_ref, in_ref, tiles_ref, hidden_ref, gain_ref, cut_ref):
    def total(t):
        result = in_ref[0, t].astype(f32)
        for x in range(1, NX):
            result = result + in_ref[x, t].astype(f32)
        return result

    for k in range(KT):
        cut_ref[:, k, :] = total(QT + k)
    rows = [total(t) for t in range(QT)]
    halves = [row[h * 8 : (h + 1) * 8, :] for row in rows for h in range(2)]
    for z in range(NZ):
        block = halves[z * RI : (z + 1) * RI] + [cut_ref[z]]
        tiles_ref[z] = jnp.concatenate(block, axis=0).astype(bf16)
    for s in range(NX):
        src = x_ref[0] ^ s
        for i in range(RI):
            hidden_ref[s, i] = in_ref[src, HT + i]
        pieces = in_ref[src, HT + RI].astype(f32)
        gain_ref[s : s + 1, :] = pieces[0:1] + pieces[1:2] + pieces[2:3]


def rope_kernel(in_ref, cos_ref, sin_ref, copies_ref, new_ref):
    total = in_ref[0].astype(f32)
    for z in range(1, NZ):
        total = total + in_ref[z].astype(f32)
    turned = total * cos_ref[...] + pltpu.roll(total, HD // 2, 1) * sin_ref[...]
    queries = turned[: 8 * RI, :].astype(bf16)
    for z in range(NZ):
        copies_ref[z] = queries
    new = turned[8 * RI :, :]
    pad = jnp.zeros((FRESH - NX * RI, HD), f32)
    new_ref[0] = jnp.concatenate([new[: NX * RI, :], pad], axis=0).astype(bf16)
    new_ref[1] = jnp.concatenate([new[NX * RI :, :], pad], axis=0).astype(bf16)


def attend_kernel(queries_ref, keypos_ref, rowpos_ref, new_ref, *refs):
    cache_refs, (out_ref, score_ref) = refs[:NX], refs[NX:]
    blocks = (keypos_ref.shape[0] - 1) // NX
    scale = HD ** (-0.5) * LOG2E
    contract_last = (((1,), (1,)), ((), ()))
    new_keys, new_values = new_ref[0], new_ref[1]
    fresh = new_keys.shape[0]
    every = queries_ref[...]
    for i in range(RI):
        queries = every[i * HD : (i + 1) * HD, :]
        row_pos = jnp.concatenate([rowpos_ref[i]] * GQ, axis=0)
        peak = jnp.full((HD, BLK), least_peak, f32)
        for x in range(NX):
            keys = jnp.concatenate([cache_refs[x][b] for b in range(blocks)], axis=1)
            score = jnp.dot(queries, keys, preferred_element_type=f32)
            for b in range(blocks):
                n = x * blocks + b
                cut = jnp.where(
                    keypos_ref[n : n + 1, :] <= row_pos,
                    score[:, b * BLK : (b + 1) * BLK],
                    masked_score,
                )
                score_ref[:, n * BLK : (n + 1) * BLK] = cut
                peak = jnp.maximum(peak, cut)
        n = NX * blocks
        score = lax.dot_general(queries, new_keys, contract_last, preferred_element_type=f32)
        last = jnp.where(keypos_ref[n : n + 1, :fresh] <= row_pos[:, :fresh], score, masked_score)
        top = jnp.maximum(
            jnp.max(peak, axis=1, keepdims=True), jnp.max(last, axis=1, keepdims=True)
        )
        top = top * scale
        weight = jnp.exp2(last * scale - top)
        total_last = jnp.sum(weight, axis=1, keepdims=True)
        numer = jnp.dot(weight.astype(bf16), new_values, preferred_element_type=f32)
        total = jnp.zeros((HD, BLK), f32)
        for x in range(NX):
            weights = []
            for b in range(blocks):
                n = x * blocks + b
                weight = jnp.exp2(score_ref[:, n * BLK : (n + 1) * BLK] * scale - top)
                total = total + weight
                weights.append(weight.astype(bf16))
            values = jnp.concatenate([cache_refs[x][blocks + b] for b in range(blocks)], axis=0)
            numer = numer + jnp.dot(
                jnp.concatenate(weights, axis=1), values, preferred_element_type=f32
            )
        total = jnp.sum(total, axis=1, keepdims=True) + total_last
        some = total > 0.0
        share = numer * jnp.where(some, 1.0 / jnp.where(some, total, 1.0), 0.0)
        level = top + jnp.where(some, jnp.log2(jnp.where(some, total, 1.0)), 0.0)
        share_at = (NX * blocks + i) * BLK
        score_ref[:, share_at : share_at + BLK] = share
        level_at = (NX * blocks + RI + i) * BLK
        score_ref[:, level_at : level_at + BLK] = jnp.broadcast_to(level, (HD, BLK))
    lane = lax.broadcasted_iota(jnp.int32, (8, HD), 1)
    for z in range(NZ):
        parts = []
        tail = jnp.zeros((8, HD), f32)
        for k in range(RI):
            row = 24 * z + 8 * k
            i, r = row // HD, row % HD
            share_at = (NX * blocks + i) * BLK
            level_at = (NX * blocks + RI + i) * BLK
            parts.append(score_ref[r : r + 8, share_at : share_at + BLK])
            for p, piece in enumerate(three_pieces(score_ref[r : r + 8, level_at : level_at + BLK])):
                tail = jnp.where(lane == 3 * k + p, piece, tail)
        out_ref[z] = jnp.concatenate(parts + [tail], axis=0).astype(bf16)


def combine_kernel(in_ref, out_ref):
    level = [[None] * RI for _ in range(NZ)]
    top = [None] * RI
    for z in range(NZ):
        tail = in_ref[z].astype(f32)[24:32, :]
        for k in range(RI):
            value = tail[:, 3 * k : 3 * k + 1] + tail[:, 3 * k + 1 : 3 * k + 2]
            value = value + tail[:, 3 * k + 2 : 3 * k + 3]
            level[z][k] = value
            top[k] = value if z == 0 else jnp.maximum(top[k], value)
    numer = jnp.zeros((8 * RI, HD), f32)
    total = jnp.zeros((8 * RI, 1), f32)
    for z in range(NZ):
        factor = jnp.concatenate([jnp.exp2(level[z][k] - top[k]) for k in range(RI)], axis=0)
        numer = numer + in_ref[z].astype(f32)[: 8 * RI, :] * factor
        total = total + factor
    result = (numer / total).astype(bf16)
    for z in range(NZ):
        out_ref[z] = result


def output_kernel(heads_ref, *refs):
    weight_refs, out_ref = refs[:NX], refs[NX]
    weights = [ref[:GQ].reshape(GQ * HD, HD) for ref in weight_refs]
    rows = heads_ref[...]
    bands = []
    for i in range(RI):
        at = i * GQ * TILE
        bands.append(
            jnp.concatenate([rows[at + g * TILE : at + (g + 1) * TILE, :] for g in range(GQ)], axis=1)
        )
    attended = jnp.concatenate(bands, axis=0)
    for x in range(NX):
        term = jnp.dot(attended, weights[x], preferred_element_type=f32).astype(bf16)
        for h in range(NH):
            out_ref[h, :, x * HD : (x + 1) * HD] = term


def next_kernel(terms_ref, hidden_ref, gain_ref, *refs):
    wide = range(GQ, 2 * GQ + 2)
    weights = [jnp.concatenate([ref[j] for j in wide], axis=1) for ref in refs[:NX]]
    resid_refs, (out_ref, cut_ref) = refs[NX : 2 * NX], refs[2 * NX :]
    attended = terms_ref[0].astype(f32)
    for h in range(1, NH):
        attended = attended + terms_ref[h].astype(f32)
    squares = jnp.zeros((XR, 1), f32)
    product = jnp.zeros((XR, (GQ + 2) * HD), f32)
    for x in range(NX):
        before = jnp.concatenate([hidden_ref[x, i] for i in range(RI)], axis=0).astype(f32)
        resid = before + attended[:, x * HD : (x + 1) * HD]
        resid_refs[x][...] = resid.astype(bf16)
        squares = squares + jnp.sum(resid * resid, axis=1, keepdims=True)
        gained = (resid * gain_ref[x : x + 1, :]).astype(bf16)
        product = product + jnp.dot(gained, weights[x], preferred_element_type=f32)
    for i in range(RI):
        for j in range(GQ + 2):
            cut_ref[:, i * (GQ + 2) + j, :] = product[
                i * TILE : (i + 1) * TILE, j * HD : (j + 1) * HD
            ]
    lane = lax.broadcasted_iota(jnp.int32, (TILE, HD), 1)
    tail = jnp.zeros((TILE, HD), f32)
    for i in range(RI):
        for p, piece in enumerate(three_pieces(squares[i * TILE : (i + 1) * TILE, :])):
            tail = jnp.where(lane == 3 * i + p, piece, tail)
    cut_ref[:, 30, :] = tail
    cut_ref[:, 31, :] = jnp.zeros((TILE, HD), f32)
    out_ref[...] = cut_ref[...].astype(bf16)


def finish_kernel(in_ref, out_ref):
    total = in_ref[0].astype(f32)
    for z in range(1, NZ):
        total = total + in_ref[z].astype(f32)
    rows = []
    for i in range(RI):
        squares = total[30:31, 3 * i : 3 * i + 1] + total[30:31, 3 * i + 1 : 3 * i + 2]
        squares = squares + total[30:31, 3 * i + 2 : 3 * i + 3]
        factor = lax.rsqrt(squares / D + epsilon)
        at = i * (GQ + 2)
        rows.append(
            jnp.concatenate(
                [total[at + j : at + j + 1, :] * factor for j in range(GQ + 2)], axis=1
            )
        )
    out_ref[...] = jnp.concatenate(rows, axis=0).astype(bf16)


def reorder_kernel(x_ref, *refs):
    in_refs, out_ref = refs[:NX], refs[NX]
    rows = out_ref.shape[0]
    new = lax.broadcasted_iota(jnp.int32, (rows, 1), 0)
    source = ((new // RI) % NX) ^ x_ref[0]
    src = source * XR + (new % RI) * NZ + new // (NX * RI)
    chosen = lax.broadcasted_iota(jnp.int32, (rows, rows), 1) == src
    data = jnp.concatenate([ref[...] for ref in in_refs], axis=0)
    out_ref[...] = jnp.dot(
        jnp.where(chosen, 1.0, 0.0).astype(bf16), data, preferred_element_type=f32
    ).astype(bf16)


def key_layout(owners, group_lengths, group_owner, group_start, listed_rows, blocks):
    length = group_lengths // BLK
    holder = (group_owner[None, :] == owners[:, None]).astype(jnp.int32)
    count = group_owner.shape[0]
    before = jnp.arange(count)[None, :] < jnp.arange(count)[:, None]
    held = holder * length[None, :]
    offset = jnp.sum(jnp.where(before[None], held[:, None, :], 0), axis=2)
    ids = jnp.arange(blocks, dtype=jnp.int32)[None, :, None]
    member = (
        (holder[:, None, :] == 1)
        & (ids >= offset[:, None, :])
        & (ids < offset[:, None, :] + length[None, None, :])
    ).astype(jnp.int32)
    start = group_start[None, None, :]
    shift = jnp.sum(member * start, axis=2)
    begin = jnp.sum(member * (start + (ids - offset[:, None, :]) * BLK), axis=2)
    live = jnp.sum(member, axis=2) > 0
    position = begin[:, :, None] + jnp.arange(BLK, dtype=jnp.int32)
    hit = jnp.any(position[..., None] == listed_rows, axis=-1)
    position = jnp.where(live[:, :, None] & ~hit, position, never)
    return shift, position.reshape(NX * blocks, BLK)


def on_device(
    hidden_rows,
    qkv_weight,
    out_weight,
    norm_gain,
    next_weight,
    cache_keys,
    cache_values,
    group_lengths,
    group_owner,
    group_start,
    listed_rows,
):
    z = lax.axis_index("z")
    x = lax.axis_index("x")
    held = cache_keys.shape[0]
    blocks = held // BLK
    a2a = functools.partial(lax.all_to_all, split_axis=0, concat_axis=0, tiled=True)

    def swapped(array, step):
        return lax.ppermute(array, "x", [(n, n ^ step) for n in range(NX)])

    payload = vmem_call(
        project_kernel,
        shaped((NX, HT + RI + 1, TILE, HD), bf16),
        (hidden_rows, qkv_weight, norm_gain.reshape(1, HD)),
        scratch=[
            pltpu.VMEM(hidden_rows.shape, bf16),
            pltpu.VMEM(qkv_weight.shape, bf16),
            pltpu.VMEM((1, HD), f32),
            pltpu.SemaphoreType.DMA((3,)),
        ],
        hbm=True,
        limit=60,
    )
    payload = a2a(payload, "x")

    sources = x ^ jnp.arange(NX, dtype=jnp.int32)
    shift, key_pos = key_layout(
        z * NX + sources, group_lengths, group_owner, group_start, listed_rows, blocks
    )
    by_zxi = listed_rows.reshape(NZ, NX, RI)
    row_pos = lax.dynamic_slice_in_dim(by_zxi, x, 1, axis=1)[:, 0].T
    new_pos = lax.dynamic_slice_in_dim(by_zxi, z, 1, axis=0).reshape(-1)
    own = 8 * RI * z + jnp.arange(8 * RI)
    chosen = (own // HD * NZ + own % NZ)[:, None] == jnp.arange(XR)[None, :]
    query_pos = jnp.sum(jnp.where(chosen, row_pos.reshape(1, XR), 0), axis=1)
    rest = jnp.full((BLK - NX * RI,), never, jnp.int32)
    key_pos = jnp.concatenate([key_pos, jnp.concatenate([new_pos, rest])[None]], axis=0)
    wide_row_pos = jnp.broadcast_to(row_pos[:, :, None], (RI, NZ, BLK))
    cosine, sine = rope_factors(
        jnp.concatenate([query_pos, new_pos, jnp.zeros((NX * RI,), jnp.int32), shift[0]])
    )
    rows = 8 * RI + KT
    cache, weights = vmem_call(
        bundle_kernel,
        (shaped((2 * blocks, BLK, HD), bf16), shaped((2 * GQ + 2, HD, HD), bf16)),
        (cache_keys, cache_values, cosine[rows:], sine[rows:], out_weight, next_weight),
    )

    x_scalar = x.reshape(1).astype(jnp.int32)
    tiles, hidden_x, gain_x = vmem_call(
        sum_x_kernel,
        (
            shaped((NZ, rows, HD), bf16),
            shaped((NX, RI, TILE, HD), bf16),
            shaped((NX, HD), f32),
        ),
        (x_scalar, payload),
        scratch=[pltpu.VMEM((NZ, KT, HD), f32)],
        scalars=1,
    )
    tiles, cache = lax.optimization_barrier((tiles, cache))
    caches = [cache] + [swapped(cache, step) for step in range(1, NX)]
    copies, new = vmem_call(
        rope_kernel,
        (shaped((NZ, 8 * RI, HD), bf16), shaped((2, FRESH, HD), bf16)),
        (a2a(tiles, "z"), cosine[:rows], sine[:rows]),
    )
    queries = a2a(copies, "z").reshape(XR * GQ, HD)
    parts = vmem_call(
        attend_kernel,
        shaped((NZ, 32, HD), bf16),
        (queries, key_pos, wide_row_pos, new, *caches),
        scratch=[pltpu.VMEM((HD, (NX * blocks + 2 * RI) * BLK), f32)],
    )
    parts, weights = lax.optimization_barrier((parts, weights))
    weights_x = [weights] + [swapped(weights, step) for step in range(1, NX)]
    share = vmem_call(
        combine_kernel, shaped((NZ, 8 * RI, HD), bf16), (a2a(parts, "z"),)
    )
    heads_out = a2a(share, "z").reshape(XR * GQ, HD)
    terms = vmem_call(
        output_kernel, shaped((NH, XR, NX * HD), bf16), (heads_out, *weights_x)
    )
    *resids, products = vmem_call(
        next_kernel,
        (*[shaped((XR, HD), bf16)] * NX, shaped((NZ, 32, HD), bf16)),
        (a2a(terms, "heads"), hidden_x, gain_x, *weights_x),
        scratch=[pltpu.VMEM((NZ, 32, HD), f32)],
    )
    resids = [resids[0]] + [swapped(resids[s], s) for s in range(1, NX)]
    hidden_out = vmem_call(
        reorder_kernel, shaped(hidden_rows.shape, bf16), (x_scalar, *resids), scalars=1
    )
    next_qkv = vmem_call(
        finish_kernel, shaped((RI, (GQ + 2) * HD), bf16), (a2a(products, "z"),)
    )
    return hidden_out, next_qkv


def solution(mesh):
    split = Mesh(mesh.devices.reshape(NH, NZ, NX), ("heads", "z", "x"))
    return jax.shard_map(
        on_device,
        mesh=split,
        in_specs=(
            P(None, GROUPS),
            P(GROUPS, "heads"),
            P("heads", GROUPS),
            P(GROUPS),
            P(GROUPS, "heads"),
            P(GROUPS, "heads"),
            P(GROUPS, "heads"),
            P(),
            P(),
            P(),
            P(),
        ),
        out_specs=(P(None, GROUPS), P(GROUPS, "heads")),
        check_vma=False,
    )
```

```python
import functools

import jax
import jax.numpy as jnp
from jax import lax
from jax.experimental import pallas as pl
from jax.experimental.pallas import tpu as pltpu
from jax.sharding import Mesh
from jax.sharding import PartitionSpec as P

D = 8192
HD = 128
GQ = 8
BLK = 128
NZ = 16
NX = 4
NH = 8
FRESH = 16
RI = 3
XR = NZ * RI
TILE = 16
QT = RI * GQ
KT = 2 * NX * RI
HT = QT + KT
GROUPS = ("z", "x")
theta_base = 500000.0
epsilon = 1e-05
masked_score = -1e30
least_peak = -1e28
never = 2**30
LOG2E = 1.4426950408889634

bf16 = jnp.bfloat16
f32 = jnp.float32


def vmem_call(kernel, out_shape, operands, scratch=(), limit=12, scalars=0, hbm=False):
    space = pl.BlockSpec(memory_space=pltpu.VMEM)
    outs = jax.tree.map(lambda _: space, out_shape)
    rest = pl.BlockSpec(memory_space=pltpu.HBM) if hbm else space
    small = pl.BlockSpec(memory_space=pltpu.SMEM)
    return pl.pallas_call(
        kernel,
        out_shape=out_shape,
        in_specs=[small] * scalars + [rest] * (len(operands) - scalars),
        out_specs=outs,
        scratch_shapes=list(scratch),
        compiler_params=pltpu.CompilerParams(vmem_limit_bytes=limit * 2**20),
    )(*operands)


def shaped(shape, dtype):
    return jax.ShapeDtypeStruct(shape, dtype)


def three_pieces(value):
    high = value.astype(bf16).astype(f32)
    rest = value - high
    middle = rest.astype(bf16).astype(f32)
    low = (rest - middle).astype(bf16).astype(f32)
    return high, middle, low


def angles(positions, half_dim):
    freq = theta_base ** (-(jnp.arange(half_dim).astype(f32) * 2.0 / (2 * half_dim)))
    phase = positions.astype(f32)[:, None] * freq[None, :]
    return (jnp.cos(phase), jnp.sin(phase))


def rope_factors(positions):
    cosine, sine = angles(positions, HD // 2)
    return jnp.concatenate([cosine, cosine], -1), jnp.concatenate([-sine, sine], -1)


def bundle_kernel(keys_ref, values_ref, cos_ref, sin_ref, out_weight_ref, next_weight_ref, cache_ref, weights_ref):
    blocks = keys_ref.shape[0] // BLK
    for b in range(blocks):
        cache_ref[blocks + b] = values_ref[b * BLK : (b + 1) * BLK, :]
        block = keys_ref[b * BLK : (b + 1) * BLK, :].astype(f32)
        turned = (
            block * cos_ref[b : b + 1, :]
            + pltpu.roll(block, HD // 2, 1) * sin_ref[b : b + 1, :]
        )
        turned = turned.astype(bf16).astype(f32)
        cache_ref[b] = turned.T.astype(bf16)
    for g in range(GQ):
        weights_ref[g] = out_weight_ref[g * HD : (g + 1) * HD, :]
    for j in range(GQ + 2):
        weights_ref[GQ + j] = next_weight_ref[:, j * HD : (j + 1) * HD]


def project_kernel(hidden_hbm, weight_hbm, gain_hbm, out_ref, hidden_ref, weight_ref, gain_ref, sems):
    copies = [
        pltpu.make_async_copy(src, dst, sems.at[n])
        for n, (src, dst) in enumerate(
            ((hidden_hbm, hidden_ref), (gain_hbm, gain_ref), (weight_hbm, weight_ref))
        )
    ]
    for copy in copies:
        copy.start()
    rows = hidden_ref.shape[0]
    new = lax.broadcasted_iota(jnp.int32, (rows, 1), 0)
    src = (new % NZ) * (NX * RI) + (new // XR) * RI + (new % XR) // NZ
    chosen = lax.broadcasted_iota(jnp.int32, (rows, rows), 1) == src
    choice = jnp.where(chosen, 1.0, 0.0).astype(bf16)
    copies[0].wait()
    copies[1].wait()
    moved = jnp.dot(
        choice, hidden_ref[...], preferred_element_type=f32
    ).astype(bf16)
    high, middle, low = three_pieces(gain_ref[...])
    sub = lax.broadcasted_iota(jnp.int32, (TILE, HD), 0)
    gain = jnp.where(
        sub == 0, high, jnp.where(sub == 1, middle, jnp.where(sub == 2, low, 0.0))
    ).astype(bf16)
    copies[2].wait()
    for x in range(NX):
        part = moved[x * XR : (x + 1) * XR, :]
        product = jnp.dot(part, weight_ref[...], preferred_element_type=f32).astype(bf16)
        for i in range(RI):
            band = product[i * TILE : (i + 1) * TILE, :]
            for j in range(GQ):
                out_ref[x, i * GQ + j] = band[:, j * HD : (j + 1) * HD]
            for j in range(2):
                tile = band[:, (GQ + j) * HD : (GQ + j + 1) * HD]
                for to in range(NX):
                    out_ref[to, QT + j * NX * RI + x * RI + i] = tile
            out_ref[x, HT + i] = part[i * TILE : (i + 1) * TILE, :]
        out_ref[x, HT + RI] = gain


def sum_x_kernel(x_ref, in_ref, tiles_ref, hidden_ref, gain_ref, cut_ref):
    def total(t):
        result = in_ref[0, t].astype(f32)
        for x in range(1, NX):
            result = result + in_ref[x, t].astype(f32)
        return result

    for k in range(KT):
        cut_ref[:, k, :] = total(QT + k)
    rows = [total(t) for t in range(QT)]
    halves = [row[h * 8 : (h + 1) * 8, :] for row in rows for h in range(2)]
    for z in range(NZ):
        block = halves[z * RI : (z + 1) * RI] + [cut_ref[z]]
        tiles_ref[z] = jnp.concatenate(block, axis=0).astype(bf16)
    for s in range(NX):
        src = x_ref[0] ^ s
        for i in range(RI):
            hidden_ref[s, i] = in_ref[src, HT + i]
        pieces = in_ref[src, HT + RI].astype(f32)
        gain_ref[s : s + 1, :] = pieces[0:1] + pieces[1:2] + pieces[2:3]


def rope_kernel(in_ref, cos_ref, sin_ref, copies_ref, new_ref):
    total = in_ref[0].astype(f32)
    for z in range(1, NZ):
        total = total + in_ref[z].astype(f32)
    turned = total * cos_ref[...] + pltpu.roll(total, HD // 2, 1) * sin_ref[...]
    queries = turned[: 8 * RI, :].astype(bf16)
    for z in range(NZ):
        copies_ref[z] = queries
    new = turned[8 * RI :, :]
    pad = jnp.zeros((FRESH - NX * RI, HD), f32)
    new_ref[0] = jnp.concatenate([new[: NX * RI, :], pad], axis=0).astype(bf16)
    new_ref[1] = jnp.concatenate([new[NX * RI :, :], pad], axis=0).astype(bf16)


def attend_kernel(queries_ref, keypos_ref, rowpos_ref, new_ref, *refs):
    cache_refs, (out_ref, score_ref) = refs[:NX], refs[NX:]
    blocks = (keypos_ref.shape[0] - 1) // NX
    scale = HD ** (-0.5) * LOG2E
    contract_last = (((1,), (1,)), ((), ()))
    new_keys, new_values = new_ref[0], new_ref[1]
    fresh = new_keys.shape[0]
    every = queries_ref[...]
    for i in range(RI):
        queries = every[i * HD : (i + 1) * HD, :]
        row_pos = jnp.concatenate([rowpos_ref[i]] * GQ, axis=0)
        peak = jnp.full((HD, BLK), least_peak, f32)
        for x in range(NX):
            keys = jnp.concatenate([cache_refs[x][b] for b in range(blocks)], axis=1)
            score = jnp.dot(queries, keys, preferred_element_type=f32)
            for b in range(blocks):
                n = x * blocks + b
                cut = jnp.where(
                    keypos_ref[n : n + 1, :] <= row_pos,
                    score[:, b * BLK : (b + 1) * BLK],
                    masked_score,
                )
                score_ref[:, n * BLK : (n + 1) * BLK] = cut
                peak = jnp.maximum(peak, cut)
        n = NX * blocks
        score = lax.dot_general(queries, new_keys, contract_last, preferred_element_type=f32)
        last = jnp.where(keypos_ref[n : n + 1, :fresh] <= row_pos[:, :fresh], score, masked_score)
        top = jnp.maximum(
            jnp.max(peak, axis=1, keepdims=True), jnp.max(last, axis=1, keepdims=True)
        )
        top = top * scale
        weight = jnp.exp2(last * scale - top)
        total_last = jnp.sum(weight, axis=1, keepdims=True)
        numer = jnp.dot(weight.astype(bf16), new_values, preferred_element_type=f32)
        total = jnp.zeros((HD, BLK), f32)
        for x in range(NX):
            weights = []
            for b in range(blocks):
                n = x * blocks + b
                weight = jnp.exp2(score_ref[:, n * BLK : (n + 1) * BLK] * scale - top)
                total = total + weight
                weights.append(weight.astype(bf16))
            values = jnp.concatenate([cache_refs[x][blocks + b] for b in range(blocks)], axis=0)
            numer = numer + jnp.dot(
                jnp.concatenate(weights, axis=1), values, preferred_element_type=f32
            )
        total = jnp.sum(total, axis=1, keepdims=True) + total_last
        some = total > 0.0
        share = numer * jnp.where(some, 1.0 / jnp.where(some, total, 1.0), 0.0)
        level = top + jnp.where(some, jnp.log2(jnp.where(some, total, 1.0)), 0.0)
        share_at = (NX * blocks + i) * BLK
        score_ref[:, share_at : share_at + BLK] = share
        level_at = (NX * blocks + RI + i) * BLK
        score_ref[:, level_at : level_at + BLK] = jnp.broadcast_to(level, (HD, BLK))
    lane = lax.broadcasted_iota(jnp.int32, (8, HD), 1)
    for z in range(NZ):
        parts = []
        tail = jnp.zeros((8, HD), f32)
        for k in range(RI):
            row = 24 * z + 8 * k
            i, r = row // HD, row % HD
            share_at = (NX * blocks + i) * BLK
            level_at = (NX * blocks + RI + i) * BLK
            parts.append(score_ref[r : r + 8, share_at : share_at + BLK])
            for p, piece in enumerate(three_pieces(score_ref[r : r + 8, level_at : level_at + BLK])):
                tail = jnp.where(lane == 3 * k + p, piece, tail)
        out_ref[z] = jnp.concatenate(parts + [tail], axis=0).astype(bf16)


def combine_kernel(in_ref, out_ref):
    level = [[None] * RI for _ in range(NZ)]
    top = [None] * RI
    for z in range(NZ):
        tail = in_ref[z].astype(f32)[24:32, :]
        for k in range(RI):
            value = tail[:, 3 * k : 3 * k + 1] + tail[:, 3 * k + 1 : 3 * k + 2]
            value = value + tail[:, 3 * k + 2 : 3 * k + 3]
            level[z][k] = value
            top[k] = value if z == 0 else jnp.maximum(top[k], value)
    numer = jnp.zeros((8 * RI, HD), f32)
    total = jnp.zeros((8 * RI, 1), f32)
    for z in range(NZ):
        factor = jnp.concatenate([jnp.exp2(level[z][k] - top[k]) for k in range(RI)], axis=0)
        numer = numer + in_ref[z].astype(f32)[: 8 * RI, :] * factor
        total = total + factor
    result = (numer / total).astype(bf16)
    for z in range(NZ):
        out_ref[z] = result


def output_kernel(heads_ref, *refs):
    weight_refs, out_ref = refs[:NX], refs[NX]
    weights = [ref[:GQ].reshape(GQ * HD, HD) for ref in weight_refs]
    rows = heads_ref[...]
    bands = []
    for i in range(RI):
        at = i * GQ * TILE
        bands.append(
            jnp.concatenate([rows[at + g * TILE : at + (g + 1) * TILE, :] for g in range(GQ)], axis=1)
        )
    attended = jnp.concatenate(bands, axis=0)
    for x in range(NX):
        term = jnp.dot(attended, weights[x], preferred_element_type=f32).astype(bf16)
        for h in range(NH):
            out_ref[h, :, x * HD : (x + 1) * HD] = term


def next_kernel(terms_ref, hidden_ref, gain_ref, *refs):
    wide = range(GQ, 2 * GQ + 2)
    weights = [jnp.concatenate([ref[j] for j in wide], axis=1) for ref in refs[:NX]]
    resid_refs, (out_ref, cut_ref) = refs[NX : 2 * NX], refs[2 * NX :]
    attended = terms_ref[0].astype(f32)
    for h in range(1, NH):
        attended = attended + terms_ref[h].astype(f32)
    squares = jnp.zeros((XR, 1), f32)
    product = jnp.zeros((XR, (GQ + 2) * HD), f32)
    for x in range(NX):
        before = jnp.concatenate([hidden_ref[x, i] for i in range(RI)], axis=0).astype(f32)
        resid = before + attended[:, x * HD : (x + 1) * HD]
        resid_refs[x][...] = resid.astype(bf16)
        squares = squares + jnp.sum(resid * resid, axis=1, keepdims=True)
        gained = (resid * gain_ref[x : x + 1, :]).astype(bf16)
        product = product + jnp.dot(gained, weights[x], preferred_element_type=f32)
    for i in range(RI):
        for j in range(GQ + 2):
            cut_ref[:, i * (GQ + 2) + j, :] = product[
                i * TILE : (i + 1) * TILE, j * HD : (j + 1) * HD
            ]
    lane = lax.broadcasted_iota(jnp.int32, (TILE, HD), 1)
    tail = jnp.zeros((TILE, HD), f32)
    for i in range(RI):
        for p, piece in enumerate(three_pieces(squares[i * TILE : (i + 1) * TILE, :])):
            tail = jnp.where(lane == 3 * i + p, piece, tail)
    cut_ref[:, 30, :] = tail
    cut_ref[:, 31, :] = jnp.zeros((TILE, HD), f32)
    out_ref[...] = cut_ref[...].astype(bf16)


def finish_kernel(in_ref, out_ref):
    total = in_ref[0].astype(f32)
    for z in range(1, NZ):
        total = total + in_ref[z].astype(f32)
    rows = []
    for i in range(RI):
        squares = total[30:31, 3 * i : 3 * i + 1] + total[30:31, 3 * i + 1 : 3 * i + 2]
        squares = squares + total[30:31, 3 * i + 2 : 3 * i + 3]
        factor = lax.rsqrt(squares / D + epsilon)
        at = i * (GQ + 2)
        rows.append(
            jnp.concatenate(
                [total[at + j : at + j + 1, :] * factor for j in range(GQ + 2)], axis=1
            )
        )
    out_ref[...] = jnp.concatenate(rows, axis=0).astype(bf16)


def reorder_kernel(x_ref, *refs):
    in_refs, out_ref = refs[:NX], refs[NX]
    rows = out_ref.shape[0]
    new = lax.broadcasted_iota(jnp.int32, (rows, 1), 0)
    source = ((new // RI) % NX) ^ x_ref[0]
    src = source * XR + (new % RI) * NZ + new // (NX * RI)
    chosen = lax.broadcasted_iota(jnp.int32, (rows, rows), 1) == src
    data = jnp.concatenate([ref[...] for ref in in_refs], axis=0)
    out_ref[...] = jnp.dot(
        jnp.where(chosen, 1.0, 0.0).astype(bf16), data, preferred_element_type=f32
    ).astype(bf16)


def key_layout(owners, group_lengths, group_owner, group_start, listed_rows, blocks):
    length = group_lengths // BLK
    holder = (group_owner[None, :] == owners[:, None]).astype(jnp.int32)
    count = group_owner.shape[0]
    before = jnp.arange(count)[None, :] < jnp.arange(count)[:, None]
    held = holder * length[None, :]
    offset = jnp.sum(jnp.where(before[None], held[:, None, :], 0), axis=2)
    ids = jnp.arange(blocks, dtype=jnp.int32)[None, :, None]
    member = (
        (holder[:, None, :] == 1)
        & (ids >= offset[:, None, :])
        & (ids < offset[:, None, :] + length[None, None, :])
    ).astype(jnp.int32)
    start = group_start[None, None, :]
    shift = jnp.sum(member * start, axis=2)
    begin = jnp.sum(member * (start + (ids - offset[:, None, :]) * BLK), axis=2)
    live = jnp.sum(member, axis=2) > 0
    position = begin[:, :, None] + jnp.arange(BLK, dtype=jnp.int32)
    hit = jnp.any(position[..., None] == listed_rows, axis=-1)
    position = jnp.where(live[:, :, None] & ~hit, position, never)
    return shift, position.reshape(NX * blocks, BLK)


def on_device(
    hidden_rows,
    qkv_weight,
    out_weight,
    norm_gain,
    next_weight,
    cache_keys,
    cache_values,
    group_lengths,
    group_owner,
    group_start,
    listed_rows,
):
    z = lax.axis_index("z")
    x = lax.axis_index("x")
    held = cache_keys.shape[0]
    blocks = held // BLK
    a2a = functools.partial(lax.all_to_all, split_axis=0, concat_axis=0, tiled=True)

    def swapped(array, step):
        return lax.ppermute(array, "x", [(n, n ^ step) for n in range(NX)])

    def after(array, *first):
        return lax.optimization_barrier((array, *first))[0]

    payload = vmem_call(
        project_kernel,
        shaped((NX, HT + RI + 1, TILE, HD), bf16),
        (hidden_rows, qkv_weight, norm_gain.reshape(1, HD)),
        scratch=[
            pltpu.VMEM(hidden_rows.shape, bf16),
            pltpu.VMEM(qkv_weight.shape, bf16),
            pltpu.VMEM((1, HD), f32),
            pltpu.SemaphoreType.DMA((3,)),
        ],
        hbm=True,
        limit=60,
    )
    payload = a2a(payload, "x")

    sources = x ^ jnp.arange(NX, dtype=jnp.int32)
    shift, key_pos = key_layout(
        z * NX + sources, group_lengths, group_owner, group_start, listed_rows, blocks
    )
    by_zxi = listed_rows.reshape(NZ, NX, RI)
    row_pos = lax.dynamic_slice_in_dim(by_zxi, x, 1, axis=1)[:, 0].T
    new_pos = lax.dynamic_slice_in_dim(by_zxi, z, 1, axis=0).reshape(-1)
    own = 8 * RI * z + jnp.arange(8 * RI)
    chosen = (own // HD * NZ + own % NZ)[:, None] == jnp.arange(XR)[None, :]
    query_pos = jnp.sum(jnp.where(chosen, row_pos.reshape(1, XR), 0), axis=1)
    rest = jnp.full((BLK - NX * RI,), never, jnp.int32)
    key_pos = jnp.concatenate([key_pos, jnp.concatenate([new_pos, rest])[None]], axis=0)
    wide_row_pos = jnp.broadcast_to(row_pos[:, :, None], (RI, NZ, BLK))
    cosine, sine = rope_factors(
        jnp.concatenate([query_pos, new_pos, jnp.zeros((NX * RI,), jnp.int32), shift[0]])
    )
    rows = 8 * RI + KT
    cache, weights = vmem_call(
        bundle_kernel,
        (shaped((2 * blocks, BLK, HD), bf16), shaped((2 * GQ + 2, HD, HD), bf16)),
        (cache_keys, cache_values, cosine[rows:], sine[rows:], out_weight, next_weight),
    )

    x_scalar = x.reshape(1).astype(jnp.int32)
    tiles, hidden_x, gain_x = vmem_call(
        sum_x_kernel,
        (
            shaped((NZ, rows, HD), bf16),
            shaped((NX, RI, TILE, HD), bf16),
            shaped((NX, HD), f32),
        ),
        (x_scalar, payload),
        scratch=[pltpu.VMEM((NZ, KT, HD), f32)],
        scalars=1,
    )
    tiles, cache = lax.optimization_barrier((tiles, cache))
    caches = [cache] + [swapped(cache, step) for step in range(1, NX)]
    copies, new = vmem_call(
        rope_kernel,
        (shaped((NZ, 8 * RI, HD), bf16), shaped((2, FRESH, HD), bf16)),
        (a2a(tiles, "z"), cosine[:rows], sine[:rows]),
    )
    weights_x = {0: weights, 2: swapped(after(weights, copies), 2)}
    queries = a2a(copies, "z").reshape(XR * GQ, HD)
    parts = vmem_call(
        attend_kernel,
        shaped((NZ, 32, HD), bf16),
        (queries, key_pos, wide_row_pos, new, *caches),
        scratch=[pltpu.VMEM((HD, (NX * blocks + 2 * RI) * BLK), f32)],
    )
    late = after(weights, parts, weights_x[2])
    weights_x |= {step: swapped(late, step) for step in (1, 3)}
    weights_x = [weights_x[step] for step in range(NX)]
    share = vmem_call(
        combine_kernel, shaped((NZ, 8 * RI, HD), bf16), (a2a(parts, "z"),)
    )
    heads_out = a2a(share, "z").reshape(XR * GQ, HD)
    terms = vmem_call(
        output_kernel, shaped((NH, XR, NX * HD), bf16), (heads_out, *weights_x)
    )
    *resids, products = vmem_call(
        next_kernel,
        (*[shaped((XR, HD), bf16)] * NX, shaped((NZ, 32, HD), bf16)),
        (a2a(terms, "heads"), hidden_x, gain_x, *weights_x),
        scratch=[pltpu.VMEM((NZ, 32, HD), f32)],
    )
    resids = [resids[0]] + [swapped(resids[s], s) for s in range(1, NX)]
    hidden_out = vmem_call(
        reorder_kernel, shaped(hidden_rows.shape, bf16), (x_scalar, *resids), scalars=1
    )
    next_qkv = vmem_call(
        finish_kernel, shaped((RI, (GQ + 2) * HD), bf16), (a2a(products, "z"),)
    )
    return hidden_out, next_qkv


def solution(mesh):
    split = Mesh(mesh.devices.reshape(NH, NZ, NX), ("heads", "z", "x"))
    return jax.shard_map(
        on_device,
        mesh=split,
        in_specs=(
            P(None, GROUPS),
            P(GROUPS, "heads"),
            P("heads", GROUPS),
            P(GROUPS),
            P(GROUPS, "heads"),
            P(GROUPS, "heads"),
            P(GROUPS, "heads"),
            P(),
            P(),
            P(),
            P(),
        ),
        out_specs=(P(None, GROUPS), P(GROUPS, "heads")),
        check_vma=False,
    )
```

```python
import functools

import jax
import jax.numpy as jnp
from jax import lax
from jax.experimental import pallas as pl
from jax.experimental.pallas import tpu as pltpu
from jax.sharding import Mesh
from jax.sharding import PartitionSpec as P

D = 8192
HD = 128
GQ = 8
BLK = 128
NZ = 16
NX = 4
NH = 8
FRESH = 16
RI = 3
XR = NZ * RI
TILE = 16
QT = RI * GQ
KT = 2 * NX * RI
WB = 2 * GQ + 3
GROUPS = ("z", "x")
HEADS = ("y", "core")
theta_base = 500000.0
epsilon = 1e-05
masked_score = -1e30
least_peak = -1e28
never = 2**30
LOG2E = 1.4426950408889634

bf16 = jnp.bfloat16
f32 = jnp.float32


def vmem_call(kernel, out_shape, operands, scratch=(), limit=12, scalars=0, hbm=False):
    space = pl.BlockSpec(memory_space=pltpu.VMEM)
    outs = jax.tree.map(lambda _: space, out_shape)
    rest = pl.BlockSpec(memory_space=pltpu.HBM) if hbm else space
    small = pl.BlockSpec(memory_space=pltpu.SMEM)
    return pl.pallas_call(
        kernel,
        out_shape=out_shape,
        in_specs=[small] * scalars + [rest] * (len(operands) - scalars),
        out_specs=outs,
        scratch_shapes=list(scratch),
        compiler_params=pltpu.CompilerParams(vmem_limit_bytes=limit * 2**20),
    )(*operands)


def shaped(shape, dtype):
    return jax.ShapeDtypeStruct(shape, dtype)


def three_pieces(value):
    high = value.astype(bf16).astype(f32)
    rest = value - high
    middle = rest.astype(bf16).astype(f32)
    low = (rest - middle).astype(bf16).astype(f32)
    return high, middle, low


def angles(positions, half_dim):
    freq = theta_base ** (-(jnp.arange(half_dim).astype(f32) * 2.0 / (2 * half_dim)))
    phase = positions.astype(f32)[:, None] * freq[None, :]
    return (jnp.cos(phase), jnp.sin(phase))


def rope_factors(positions):
    cosine, sine = angles(positions, HD // 2)
    return jnp.concatenate([cosine, cosine], -1), jnp.concatenate([-sine, sine], -1)


def bundle_kernel(
    x_ref, keys_ref, values_ref, cos_ref, sin_ref, out_weight_ref, next_weight_ref, hidden_ref, cache_ref, *bundle_refs
):
    blocks = keys_ref.shape[0] // BLK
    for b in range(blocks):
        cache_ref[blocks + b] = values_ref[b * BLK : (b + 1) * BLK, :]
        block = keys_ref[b * BLK : (b + 1) * BLK, :].astype(f32)
        turned = (
            block * cos_ref[b : b + 1, :]
            + pltpu.roll(block, HD // 2, 1) * sin_ref[b : b + 1, :]
        )
        turned = turned.astype(bf16).astype(f32)
        cache_ref[b] = turned.T.astype(bf16)
    for s, bundle_ref in enumerate(bundle_refs):
        for g in range(GQ):
            bundle_ref[g] = out_weight_ref[g * HD : (g + 1) * HD, :]
        for j in range(GQ + 2):
            bundle_ref[GQ + j] = next_weight_ref[:, j * HD : (j + 1) * HD]
        bundle_ref[WB - 1] = hidden_ref[x_ref[0] ^ s]


def project_kernel(hidden_hbm, weight_hbm, gain_hbm, out_ref, rows_ref, hidden_ref, weight_ref, gain_ref, sems):
    copies = [
        pltpu.make_async_copy(src, dst, sems.at[n])
        for n, (src, dst) in enumerate(
            ((hidden_hbm, hidden_ref), (gain_hbm, gain_ref), (weight_hbm, weight_ref))
        )
    ]
    for copy in copies:
        copy.start()
    rows = hidden_ref.shape[0]
    new = lax.broadcasted_iota(jnp.int32, (rows, 1), 0)
    src = (new % NZ) * (NX * RI) + (new // XR) * RI + (new % XR) // NZ
    chosen = lax.broadcasted_iota(jnp.int32, (rows, rows), 1) == src
    choice = jnp.where(chosen, 1.0, 0.0).astype(bf16)
    copies[0].wait()
    copies[1].wait()
    moved = jnp.dot(
        choice, hidden_ref[...], preferred_element_type=f32
    ).astype(bf16)
    high, middle, low = three_pieces(gain_ref[...])
    sub = lax.broadcasted_iota(jnp.int32, (TILE, HD), 0)
    gain = jnp.where(
        sub == 0, high, jnp.where(sub == 1, middle, jnp.where(sub == 2, low, 0.0))
    ).astype(bf16)
    copies[2].wait()
    for x in range(NX):
        part = moved[x * XR : (x + 1) * XR, :]
        product = jnp.dot(part, weight_ref[...], preferred_element_type=f32).astype(bf16)
        for i in range(RI):
            band = product[i * TILE : (i + 1) * TILE, :]
            for j in range(GQ):
                out_ref[x, i * GQ + j] = band[:, j * HD : (j + 1) * HD]
            for j in range(2):
                tile = band[:, (GQ + j) * HD : (GQ + j + 1) * HD]
                for to in range(NX):
                    out_ref[to, QT + j * NX * RI + x * RI + i] = tile
        rest = jnp.zeros((HD - XR - TILE, HD), bf16)
        rows_ref[x] = jnp.concatenate([part, gain, rest], axis=0)


def sum_x_kernel(in_ref, tiles_ref, cut_ref):
    def total(t):
        result = in_ref[0, t].astype(f32)
        for x in range(1, NX):
            result = result + in_ref[x, t].astype(f32)
        return result

    for k in range(KT):
        cut_ref[:, k, :] = total(QT + k)
    rows = [total(t) for t in range(QT)]
    halves = [row[h * 8 : (h + 1) * 8, :] for row in rows for h in range(2)]
    for z in range(NZ):
        block = halves[z * RI : (z + 1) * RI] + [cut_ref[z]]
        tiles_ref[z] = jnp.concatenate(block, axis=0).astype(bf16)


def rope_kernel(in_ref, cos_ref, sin_ref, copies_ref, new_ref):
    total = in_ref[0].astype(f32)
    for z in range(1, NZ):
        total = total + in_ref[z].astype(f32)
    turned = total * cos_ref[...] + pltpu.roll(total, HD // 2, 1) * sin_ref[...]
    queries = turned[: 8 * RI, :].astype(bf16)
    for z in range(NZ):
        copies_ref[z] = queries
    new = turned[8 * RI :, :]
    pad = jnp.zeros((FRESH - NX * RI, HD), f32)
    new_ref[0] = jnp.concatenate([new[: NX * RI, :], pad], axis=0).astype(bf16)
    new_ref[1] = jnp.concatenate([new[NX * RI :, :], pad], axis=0).astype(bf16)


def attend_kernel(queries_ref, keypos_ref, rowpos_ref, new_ref, *refs):
    cache_refs, (out_ref, score_ref) = refs[:NX], refs[NX:]
    blocks = (keypos_ref.shape[0] - 1) // NX
    scale = HD ** (-0.5) * LOG2E
    contract_last = (((1,), (1,)), ((), ()))
    new_keys, new_values = new_ref[0], new_ref[1]
    fresh = new_keys.shape[0]
    every = queries_ref[...]
    for i in range(RI):
        queries = every[i * HD : (i + 1) * HD, :]
        row_pos = jnp.concatenate([rowpos_ref[i]] * GQ, axis=0)
        peak = jnp.full((HD, BLK), least_peak, f32)
        for x in range(NX):
            keys = jnp.concatenate([cache_refs[x][b] for b in range(blocks)], axis=1)
            score = jnp.dot(queries, keys, preferred_element_type=f32)
            for b in range(blocks):
                n = x * blocks + b
                cut = jnp.where(
                    keypos_ref[n : n + 1, :] <= row_pos,
                    score[:, b * BLK : (b + 1) * BLK],
                    masked_score,
                )
                score_ref[:, n * BLK : (n + 1) * BLK] = cut
                peak = jnp.maximum(peak, cut)
        n = NX * blocks
        score = lax.dot_general(queries, new_keys, contract_last, preferred_element_type=f32)
        last = jnp.where(keypos_ref[n : n + 1, :fresh] <= row_pos[:, :fresh], score, masked_score)
        top = jnp.maximum(
            jnp.max(peak, axis=1, keepdims=True), jnp.max(last, axis=1, keepdims=True)
        )
        top = top * scale
        weight = jnp.exp2(last * scale - top)
        total_last = jnp.sum(weight, axis=1, keepdims=True)
        numer = jnp.dot(weight.astype(bf16), new_values, preferred_element_type=f32)
        total = jnp.zeros((HD, BLK), f32)
        for x in range(NX):
            weights = []
            for b in range(blocks):
                n = x * blocks + b
                weight = jnp.exp2(score_ref[:, n * BLK : (n + 1) * BLK] * scale - top)
                total = total + weight
                weights.append(weight.astype(bf16))
            values = jnp.concatenate([cache_refs[x][blocks + b] for b in range(blocks)], axis=0)
            numer = numer + jnp.dot(
                jnp.concatenate(weights, axis=1), values, preferred_element_type=f32
            )
        total = jnp.sum(total, axis=1, keepdims=True) + total_last
        some = total > 0.0
        share = numer * jnp.where(some, 1.0 / jnp.where(some, total, 1.0), 0.0)
        level = top + jnp.where(some, jnp.log2(jnp.where(some, total, 1.0)), 0.0)
        share_at = (NX * blocks + i) * BLK
        score_ref[:, share_at : share_at + BLK] = share
        level_at = (NX * blocks + RI + i) * BLK
        score_ref[:, level_at : level_at + BLK] = jnp.broadcast_to(level, (HD, BLK))
    lane = lax.broadcasted_iota(jnp.int32, (8, HD), 1)
    for z in range(NZ):
        parts = []
        tail = jnp.zeros((8, HD), f32)
        for k in range(RI):
            row = 24 * z + 8 * k
            i, r = row // HD, row % HD
            share_at = (NX * blocks + i) * BLK
            level_at = (NX * blocks + RI + i) * BLK
            parts.append(score_ref[r : r + 8, share_at : share_at + BLK])
            for p, piece in enumerate(three_pieces(score_ref[r : r + 8, level_at : level_at + BLK])):
                tail = jnp.where(lane == 3 * k + p, piece, tail)
        out_ref[z] = jnp.concatenate(parts + [tail], axis=0).astype(bf16)


def combine_kernel(in_ref, out_ref):
    level = [[None] * RI for _ in range(NZ)]
    top = [None] * RI
    for z in range(NZ):
        tail = in_ref[z].astype(f32)[24:32, :]
        for k in range(RI):
            value = tail[:, 3 * k : 3 * k + 1] + tail[:, 3 * k + 1 : 3 * k + 2]
            value = value + tail[:, 3 * k + 2 : 3 * k + 3]
            level[z][k] = value
            top[k] = value if z == 0 else jnp.maximum(top[k], value)
    numer = jnp.zeros((8 * RI, HD), f32)
    total = jnp.zeros((8 * RI, 1), f32)
    for z in range(NZ):
        factor = jnp.concatenate([jnp.exp2(level[z][k] - top[k]) for k in range(RI)], axis=0)
        numer = numer + in_ref[z].astype(f32)[: 8 * RI, :] * factor
        total = total + factor
    result = (numer / total).astype(bf16)
    for z in range(NZ):
        out_ref[z] = result


def output_kernel(heads_ref, *refs):
    weight_refs, out_ref = refs[:NX], refs[NX]
    weights = [ref[:GQ].reshape(GQ * HD, HD) for ref in weight_refs]
    rows = heads_ref[...]
    bands = []
    for i in range(RI):
        at = i * GQ * TILE
        bands.append(
            jnp.concatenate([rows[at + g * TILE : at + (g + 1) * TILE, :] for g in range(GQ)], axis=1)
        )
    attended = jnp.concatenate(bands, axis=0)
    for x in range(NX):
        term = jnp.dot(attended, weights[x], preferred_element_type=f32).astype(bf16)
        for h in range(NH):
            out_ref[h, :, x * HD : (x + 1) * HD] = term


def next_kernel(terms_ref, *refs):
    wide = range(GQ, 2 * GQ + 2)
    weights = [jnp.concatenate([ref[j] for j in wide], axis=1) for ref in refs[:NX]]
    resid_refs, (out_ref, cut_ref) = refs[NX : 2 * NX], refs[2 * NX :]
    attended = terms_ref[0].astype(f32)
    for h in range(1, NH):
        attended = attended + terms_ref[h].astype(f32)
    squares = jnp.zeros((XR, 1), f32)
    product = jnp.zeros((XR, (GQ + 2) * HD), f32)
    for x in range(NX):
        rest = refs[x][WB - 1].astype(f32)
        before = rest[:XR]
        gain = rest[XR : XR + 1] + rest[XR + 1 : XR + 2] + rest[XR + 2 : XR + 3]
        resid = before + attended[:, x * HD : (x + 1) * HD]
        resid_refs[x][...] = resid.astype(bf16)
        squares = squares + jnp.sum(resid * resid, axis=1, keepdims=True)
        gained = (resid * gain).astype(bf16)
        product = product + jnp.dot(gained, weights[x], preferred_element_type=f32)
    for i in range(RI):
        for j in range(GQ + 2):
            cut_ref[:, i * (GQ + 2) + j, :] = product[
                i * TILE : (i + 1) * TILE, j * HD : (j + 1) * HD
            ]
    lane = lax.broadcasted_iota(jnp.int32, (TILE, HD), 1)
    tail = jnp.zeros((TILE, HD), f32)
    for i in range(RI):
        for p, piece in enumerate(three_pieces(squares[i * TILE : (i + 1) * TILE, :])):
            tail = jnp.where(lane == 3 * i + p, piece, tail)
    cut_ref[:, 30, :] = tail
    cut_ref[:, 31, :] = jnp.zeros((TILE, HD), f32)
    out_ref[...] = cut_ref[...].astype(bf16)


def finish_kernel(in_ref, out_ref):
    total = in_ref[0].astype(f32)
    for z in range(1, NZ):
        total = total + in_ref[z].astype(f32)
    rows = []
    for i in range(RI):
        squares = total[30:31, 3 * i : 3 * i + 1] + total[30:31, 3 * i + 1 : 3 * i + 2]
        squares = squares + total[30:31, 3 * i + 2 : 3 * i + 3]
        factor = lax.rsqrt(squares / D + epsilon)
        at = i * (GQ + 2)
        rows.append(
            jnp.concatenate(
                [total[at + j : at + j + 1, :] * factor for j in range(GQ + 2)], axis=1
            )
        )
    out_ref[...] = jnp.concatenate(rows, axis=0).astype(bf16)


def reorder_kernel(x_ref, *refs):
    in_refs, out_ref = refs[:NX], refs[NX]
    rows = out_ref.shape[0]
    new = lax.broadcasted_iota(jnp.int32, (rows, 1), 0)
    source = ((new // RI) % NX) ^ x_ref[0]
    src = source * XR + (new % RI) * NZ + new // (NX * RI)
    chosen = lax.broadcasted_iota(jnp.int32, (rows, rows), 1) == src
    data = jnp.concatenate([ref[...] for ref in in_refs], axis=0)
    out_ref[...] = jnp.dot(
        jnp.where(chosen, 1.0, 0.0).astype(bf16), data, preferred_element_type=f32
    ).astype(bf16)


def key_layout(owners, group_lengths, group_owner, group_start, listed_rows, blocks):
    length = group_lengths // BLK
    holder = (group_owner[None, :] == owners[:, None]).astype(jnp.int32)
    count = group_owner.shape[0]
    before = jnp.arange(count)[None, :] < jnp.arange(count)[:, None]
    held = holder * length[None, :]
    offset = jnp.sum(jnp.where(before[None], held[:, None, :], 0), axis=2)
    ids = jnp.arange(blocks, dtype=jnp.int32)[None, :, None]
    member = (
        (holder[:, None, :] == 1)
        & (ids >= offset[:, None, :])
        & (ids < offset[:, None, :] + length[None, None, :])
    ).astype(jnp.int32)
    start = group_start[None, None, :]
    shift = jnp.sum(member * start, axis=2)
    begin = jnp.sum(member * (start + (ids - offset[:, None, :]) * BLK), axis=2)
    live = jnp.sum(member, axis=2) > 0
    position = begin[:, :, None] + jnp.arange(BLK, dtype=jnp.int32)
    hit = jnp.any(position[..., None] == listed_rows, axis=-1)
    position = jnp.where(live[:, :, None] & ~hit, position, never)
    return shift, position.reshape(NX * blocks, BLK)


def on_device(
    hidden_rows,
    qkv_weight,
    out_weight,
    norm_gain,
    next_weight,
    cache_keys,
    cache_values,
    group_lengths,
    group_owner,
    group_start,
    listed_rows,
):
    z = lax.axis_index("z")
    x = lax.axis_index("x")
    held = cache_keys.shape[0]
    blocks = held // BLK
    a2a = functools.partial(lax.all_to_all, split_axis=0, concat_axis=0, tiled=True)

    def swapped(array, step):
        return lax.ppermute(array, "x", [(n, n ^ step) for n in range(NX)])

    def after(array, *first):
        return lax.optimization_barrier((array, *first))[0]

    payload, hidden_rest = vmem_call(
        project_kernel,
        (shaped((NX, QT + KT, TILE, HD), bf16), shaped((NX, HD, HD), bf16)),
        (hidden_rows, qkv_weight, norm_gain.reshape(1, HD)),
        scratch=[
            pltpu.VMEM(hidden_rows.shape, bf16),
            pltpu.VMEM(qkv_weight.shape, bf16),
            pltpu.VMEM((1, HD), f32),
            pltpu.SemaphoreType.DMA((3,)),
        ],
        hbm=True,
        limit=60,
    )
    payload = a2a(payload, "x")

    sources = x ^ jnp.arange(NX, dtype=jnp.int32)
    shift, key_pos = key_layout(
        z * NX + sources, group_lengths, group_owner, group_start, listed_rows, blocks
    )
    by_zxi = listed_rows.reshape(NZ, NX, RI)
    row_pos = lax.dynamic_slice_in_dim(by_zxi, x, 1, axis=1)[:, 0].T
    new_pos = lax.dynamic_slice_in_dim(by_zxi, z, 1, axis=0).reshape(-1)
    own = 8 * RI * z + jnp.arange(8 * RI)
    chosen = (own // HD * NZ + own % NZ)[:, None] == jnp.arange(XR)[None, :]
    query_pos = jnp.sum(jnp.where(chosen, row_pos.reshape(1, XR), 0), axis=1)
    rest = jnp.full((BLK - NX * RI,), never, jnp.int32)
    key_pos = jnp.concatenate([key_pos, jnp.concatenate([new_pos, rest])[None]], axis=0)
    wide_row_pos = jnp.broadcast_to(row_pos[:, :, None], (RI, NZ, BLK))
    cosine, sine = rope_factors(
        jnp.concatenate([query_pos, new_pos, jnp.zeros((NX * RI,), jnp.int32), shift[0]])
    )
    rows = 8 * RI + KT
    x_scalar = x.reshape(1).astype(jnp.int32)
    cache, *bundles = vmem_call(
        bundle_kernel,
        (shaped((2 * blocks, BLK, HD), bf16), *[shaped((WB, HD, HD), bf16)] * NX),
        (
            x_scalar,
            cache_keys,
            cache_values,
            cosine[rows:],
            sine[rows:],
            out_weight,
            next_weight,
            hidden_rest,
        ),
        scalars=1,
    )

    tiles = vmem_call(
        sum_x_kernel,
        shaped((NZ, rows, HD), bf16),
        (payload,),
        scratch=[pltpu.VMEM((NZ, KT, HD), f32)],
    )
    tiles, cache = lax.optimization_barrier((tiles, cache))
    caches = [cache] + [swapped(cache, step) for step in range(1, NX)]
    copies, new = vmem_call(
        rope_kernel,
        (shaped((NZ, 8 * RI, HD), bf16), shaped((2, FRESH, HD), bf16)),
        (a2a(tiles, "z"), cosine[:rows], sine[:rows]),
    )
    weights_x = {0: bundles[0], 2: swapped(after(bundles[2], copies), 2)}
    queries = a2a(copies, "z").reshape(XR * GQ, HD)
    parts = vmem_call(
        attend_kernel,
        shaped((NZ, 32, HD), bf16),
        (queries, key_pos, wide_row_pos, new, *caches),
        scratch=[pltpu.VMEM((HD, (NX * blocks + 2 * RI) * BLK), f32)],
    )
    for step in (1, 3):
        weights_x[step] = swapped(after(bundles[step], parts, weights_x[2]), step)
    weights_x = [weights_x[step] for step in range(NX)]
    share = vmem_call(
        combine_kernel, shaped((NZ, 8 * RI, HD), bf16), (a2a(parts, "z"),)
    )
    heads_out = a2a(share, "z").reshape(XR * GQ, HD)
    terms = vmem_call(
        output_kernel, shaped((NH, XR, NX * HD), bf16), (heads_out, *weights_x)
    )
    *resids, products = vmem_call(
        next_kernel,
        (*[shaped((XR, HD), bf16)] * NX, shaped((NZ, 32, HD), bf16)),
        (a2a(terms, ("core", "y")), *weights_x),
        scratch=[pltpu.VMEM((NZ, 32, HD), f32)],
    )
    resids = [resids[0]] + [swapped(resids[s], s) for s in range(1, NX)]
    next_qkv = vmem_call(
        finish_kernel, shaped((RI, (GQ + 2) * HD), bf16), (a2a(products, "z"),)
    )
    *resids, next_qkv = lax.optimization_barrier((*resids, next_qkv))
    hidden_out = vmem_call(
        reorder_kernel, shaped(hidden_rows.shape, bf16), (x_scalar, *resids), scalars=1
    )
    return hidden_out, next_qkv


def solution(mesh):
    split = Mesh(mesh.devices.reshape(NH // 2, 2, NZ, NX), ("y", "core", "z", "x"))
    return jax.shard_map(
        on_device,
        mesh=split,
        in_specs=(
            P(None, GROUPS),
            P(GROUPS, HEADS),
            P(HEADS, GROUPS),
            P(GROUPS),
            P(GROUPS, HEADS),
            P(GROUPS, HEADS),
            P(GROUPS, HEADS),
            P(),
            P(),
            P(),
            P(),
        ),
        out_specs=(P(None, GROUPS), P(GROUPS, HEADS)),
        check_vma=False,
    )
```

```python
import functools

import jax
import jax.numpy as jnp
from jax import lax
from jax.experimental import pallas as pl
from jax.experimental.pallas import tpu as pltpu
from jax.sharding import Mesh
from jax.sharding import PartitionSpec as P

D = 8192
HD = 128
GQ = 8
BLK = 128
NZ = 16
NX = 4
NH = 8
FRESH = 16
RI = 3
XR = NZ * RI
TILE = 16
QT = RI * GQ
KT = 2 * NX * RI
WB = 2 * GQ + 3
GROUPS = ("z", "x")
HEADS = ("y", "core")
theta_base = 500000.0
epsilon = 1e-05
masked_score = -1e30
least_peak = -1e28
never = 2**30
LOG2E = 1.4426950408889634

bf16 = jnp.bfloat16
f32 = jnp.float32


def vmem_call(kernel, out_shape, operands, scratch=(), limit=12, scalars=0, hbm=False):
    space = pl.BlockSpec(memory_space=pltpu.VMEM)
    outs = jax.tree.map(lambda _: space, out_shape)
    rest = pl.BlockSpec(memory_space=pltpu.HBM) if hbm else space
    small = pl.BlockSpec(memory_space=pltpu.SMEM)
    return pl.pallas_call(
        kernel,
        out_shape=out_shape,
        in_specs=[small] * scalars + [rest] * (len(operands) - scalars),
        out_specs=outs,
        scratch_shapes=list(scratch),
        compiler_params=pltpu.CompilerParams(vmem_limit_bytes=limit * 2**20),
    )(*operands)


def shaped(shape, dtype):
    return jax.ShapeDtypeStruct(shape, dtype)


def three_pieces(value):
    high = value.astype(bf16).astype(f32)
    rest = value - high
    middle = rest.astype(bf16).astype(f32)
    low = (rest - middle).astype(bf16).astype(f32)
    return high, middle, low


def angles(positions, half_dim):
    freq = theta_base ** (-(jnp.arange(half_dim).astype(f32) * 2.0 / (2 * half_dim)))
    phase = positions.astype(f32)[:, None] * freq[None, :]
    return (jnp.cos(phase), jnp.sin(phase))


def rope_factors(positions):
    cosine, sine = angles(positions, HD // 2)
    return jnp.concatenate([cosine, cosine], -1), jnp.concatenate([-sine, sine], -1)


def bundle_kernel(
    x_ref, keys_ref, values_ref, cos_ref, sin_ref, out_weight_ref, next_weight_ref, hidden_ref, cache_ref, *bundle_refs
):
    blocks = keys_ref.shape[0] // BLK
    for b in range(blocks):
        cache_ref[blocks + b] = values_ref[b * BLK : (b + 1) * BLK, :]
        block = keys_ref[b * BLK : (b + 1) * BLK, :].astype(f32)
        turned = (
            block * cos_ref[b : b + 1, :]
            + pltpu.roll(block, HD // 2, 1) * sin_ref[b : b + 1, :]
        )
        turned = turned.astype(bf16).astype(f32)
        cache_ref[b] = turned.T.astype(bf16)
    for s, bundle_ref in enumerate(bundle_refs):
        for g in range(GQ):
            bundle_ref[g] = out_weight_ref[g * HD : (g + 1) * HD, :]
        for j in range(GQ + 2):
            bundle_ref[GQ + j] = next_weight_ref[:, j * HD : (j + 1) * HD]
        bundle_ref[WB - 1] = hidden_ref[x_ref[0] ^ s]


def project_kernel(hidden_hbm, weight_hbm, gain_hbm, out_ref, rows_ref, hidden_ref, weight_ref, gain_ref, sems):
    copies = [
        pltpu.make_async_copy(src, dst, sems.at[n])
        for n, (src, dst) in enumerate(
            ((hidden_hbm, hidden_ref), (gain_hbm, gain_ref), (weight_hbm, weight_ref))
        )
    ]
    for copy in copies:
        copy.start()
    rows = hidden_ref.shape[0]
    new = lax.broadcasted_iota(jnp.int32, (rows, 1), 0)
    src = (new % NZ) * (NX * RI) + (new // XR) * RI + (new % XR) // NZ
    chosen = lax.broadcasted_iota(jnp.int32, (rows, rows), 1) == src
    choice = jnp.where(chosen, 1.0, 0.0).astype(bf16)
    copies[0].wait()
    copies[1].wait()
    moved = jnp.dot(
        choice, hidden_ref[...], preferred_element_type=f32
    ).astype(bf16)
    high, middle, low = three_pieces(gain_ref[...])
    sub = lax.broadcasted_iota(jnp.int32, (TILE, HD), 0)
    gain = jnp.where(
        sub == 0, high, jnp.where(sub == 1, middle, jnp.where(sub == 2, low, 0.0))
    ).astype(bf16)
    rest = jnp.zeros((HD - XR - TILE, HD), bf16)
    for x in range(NX):
        rows_ref[x] = jnp.concatenate([moved[x * XR : (x + 1) * XR, :], gain, rest], axis=0)
    copies[2].wait()
    for first in range(0, GQ + 2, 2):
        columns = weight_ref[:, first * HD : (first + 2) * HD]
        product = jnp.dot(moved, columns, preferred_element_type=f32).astype(bf16)
        for j in range(first, first + 2):
            strip = product[:, (j - first) * HD : (j - first + 1) * HD]
            for x in range(NX):
                for i in range(RI):
                    tile = strip[x * XR + i * TILE : x * XR + (i + 1) * TILE, :]
                    if j < GQ:
                        out_ref[x, i * GQ + j] = tile
                    else:
                        for to in range(NX):
                            out_ref[to, QT + (j - GQ) * NX * RI + x * RI + i] = tile


def sum_x_kernel(in_ref, tiles_ref, cut_ref):
    def total(t):
        result = in_ref[0, t].astype(f32)
        for x in range(1, NX):
            result = result + in_ref[x, t].astype(f32)
        return result

    for k in range(KT):
        cut_ref[:, k, :] = total(QT + k)
    rows = [total(t) for t in range(QT)]
    halves = [row[h * 8 : (h + 1) * 8, :] for row in rows for h in range(2)]
    for z in range(NZ):
        block = halves[z * RI : (z + 1) * RI] + [cut_ref[z]]
        tiles_ref[z] = jnp.concatenate(block, axis=0).astype(bf16)


def rope_kernel(in_ref, cos_ref, sin_ref, copies_ref, new_ref):
    total = in_ref[0].astype(f32)
    for z in range(1, NZ):
        total = total + in_ref[z].astype(f32)
    turned = total * cos_ref[...] + pltpu.roll(total, HD // 2, 1) * sin_ref[...]
    queries = turned[: 8 * RI, :].astype(bf16)
    for z in range(NZ):
        copies_ref[z] = queries
    new = turned[8 * RI :, :]
    pad = jnp.zeros((FRESH - NX * RI, HD), f32)
    new_ref[0] = jnp.concatenate([new[: NX * RI, :], pad], axis=0).astype(bf16)
    new_ref[1] = jnp.concatenate([new[NX * RI :, :], pad], axis=0).astype(bf16)


def attend_kernel(queries_ref, keypos_ref, rowpos_ref, new_ref, *refs):
    cache_refs, (out_ref, score_ref) = refs[:NX], refs[NX:]
    blocks = (keypos_ref.shape[0] - 1) // NX
    scale = HD ** (-0.5) * LOG2E
    contract_last = (((1,), (1,)), ((), ()))
    new_keys, new_values = new_ref[0], new_ref[1]
    fresh = new_keys.shape[0]
    every = queries_ref[...]
    for i in range(RI):
        queries = every[i * HD : (i + 1) * HD, :]
        row_pos = jnp.concatenate([rowpos_ref[i]] * GQ, axis=0)
        peak = jnp.full((HD, BLK), least_peak, f32)
        for x in range(NX):
            keys = jnp.concatenate([cache_refs[x][b] for b in range(blocks)], axis=1)
            score = jnp.dot(queries, keys, preferred_element_type=f32)
            for b in range(blocks):
                n = x * blocks + b
                cut = jnp.where(
                    keypos_ref[n : n + 1, :] <= row_pos,
                    score[:, b * BLK : (b + 1) * BLK],
                    masked_score,
                )
                score_ref[:, n * BLK : (n + 1) * BLK] = cut
                peak = jnp.maximum(peak, cut)
        n = NX * blocks
        score = lax.dot_general(queries, new_keys, contract_last, preferred_element_type=f32)
        last = jnp.where(keypos_ref[n : n + 1, :fresh] <= row_pos[:, :fresh], score, masked_score)
        top = jnp.maximum(
            jnp.max(peak, axis=1, keepdims=True), jnp.max(last, axis=1, keepdims=True)
        )
        top = top * scale
        weight = jnp.exp2(last * scale - top)
        total_last = jnp.sum(weight, axis=1, keepdims=True)
        numer = jnp.dot(weight.astype(bf16), new_values, preferred_element_type=f32)
        total = jnp.zeros((HD, BLK), f32)
        for x in range(NX):
            weights = []
            for b in range(blocks):
                n = x * blocks + b
                weight = jnp.exp2(score_ref[:, n * BLK : (n + 1) * BLK] * scale - top)
                total = total + weight
                weights.append(weight.astype(bf16))
            values = jnp.concatenate([cache_refs[x][blocks + b] for b in range(blocks)], axis=0)
            numer = numer + jnp.dot(
                jnp.concatenate(weights, axis=1), values, preferred_element_type=f32
            )
        total = jnp.sum(total, axis=1, keepdims=True) + total_last
        some = total > 0.0
        share = numer * jnp.where(some, 1.0 / jnp.where(some, total, 1.0), 0.0)
        level = top + jnp.where(some, jnp.log2(jnp.where(some, total, 1.0)), 0.0)
        share_at = (NX * blocks + i) * BLK
        score_ref[:, share_at : share_at + BLK] = share
        level_at = (NX * blocks + RI + i) * BLK
        score_ref[:, level_at : level_at + BLK] = jnp.broadcast_to(level, (HD, BLK))
    lane = lax.broadcasted_iota(jnp.int32, (8, HD), 1)
    for z in range(NZ):
        parts = []
        tail = jnp.zeros((8, HD), f32)
        for k in range(RI):
            row = 24 * z + 8 * k
            i, r = row // HD, row % HD
            share_at = (NX * blocks + i) * BLK
            level_at = (NX * blocks + RI + i) * BLK
            parts.append(score_ref[r : r + 8, share_at : share_at + BLK])
            for p, piece in enumerate(three_pieces(score_ref[r : r + 8, level_at : level_at + BLK])):
                tail = jnp.where(lane == 3 * k + p, piece, tail)
        out_ref[z] = jnp.concatenate(parts + [tail], axis=0).astype(bf16)


def combine_kernel(in_ref, out_ref):
    level = [[None] * RI for _ in range(NZ)]
    top = [None] * RI
    for z in range(NZ):
        tail = in_ref[z].astype(f32)[24:32, :]
        for k in range(RI):
            value = tail[:, 3 * k : 3 * k + 1] + tail[:, 3 * k + 1 : 3 * k + 2]
            value = value + tail[:, 3 * k + 2 : 3 * k + 3]
            level[z][k] = value
            top[k] = value if z == 0 else jnp.maximum(top[k], value)
    numer = jnp.zeros((8 * RI, HD), f32)
    total = jnp.zeros((8 * RI, 1), f32)
    for z in range(NZ):
        factor = jnp.concatenate([jnp.exp2(level[z][k] - top[k]) for k in range(RI)], axis=0)
        numer = numer + in_ref[z].astype(f32)[: 8 * RI, :] * factor
        total = total + factor
    result = (numer / total).astype(bf16)
    for z in range(NZ):
        out_ref[z] = result


def output_kernel(heads_ref, *refs):
    weight_refs, out_ref = refs[:NX], refs[NX]
    weights = [ref[:GQ].reshape(GQ * HD, HD) for ref in weight_refs]
    rows = heads_ref[...]
    bands = []
    for i in range(RI):
        at = i * GQ * TILE
        bands.append(
            jnp.concatenate([rows[at + g * TILE : at + (g + 1) * TILE, :] for g in range(GQ)], axis=1)
        )
    attended = jnp.concatenate(bands, axis=0)
    for x in range(NX):
        term = jnp.dot(attended, weights[x], preferred_element_type=f32).astype(bf16)
        for h in range(NH):
            out_ref[h, :, x * HD : (x + 1) * HD] = term


def next_kernel(terms_ref, *refs):
    wide = range(GQ, 2 * GQ + 2)
    weights = [jnp.concatenate([ref[j] for j in wide], axis=1) for ref in refs[:NX]]
    resid_refs, (out_ref, cut_ref) = refs[NX : 2 * NX], refs[2 * NX :]
    attended = terms_ref[0].astype(f32)
    for h in range(1, NH):
        attended = attended + terms_ref[h].astype(f32)
    squares = jnp.zeros((XR, 1), f32)
    product = jnp.zeros((XR, (GQ + 2) * HD), f32)
    for x in range(NX):
        rest = refs[x][WB - 1].astype(f32)
        before = rest[:XR]
        gain = rest[XR : XR + 1] + rest[XR + 1 : XR + 2] + rest[XR + 2 : XR + 3]
        resid = before + attended[:, x * HD : (x + 1) * HD]
        resid_refs[x][...] = resid.astype(bf16)
        squares = squares + jnp.sum(resid * resid, axis=1, keepdims=True)
        gained = (resid * gain).astype(bf16)
        product = product + jnp.dot(gained, weights[x], preferred_element_type=f32)
    for i in range(RI):
        for j in range(GQ + 2):
            cut_ref[:, i * (GQ + 2) + j, :] = product[
                i * TILE : (i + 1) * TILE, j * HD : (j + 1) * HD
            ]
    lane = lax.broadcasted_iota(jnp.int32, (TILE, HD), 1)
    tail = jnp.zeros((TILE, HD), f32)
    for i in range(RI):
        for p, piece in enumerate(three_pieces(squares[i * TILE : (i + 1) * TILE, :])):
            tail = jnp.where(lane == 3 * i + p, piece, tail)
    cut_ref[:, 30, :] = tail
    cut_ref[:, 31, :] = jnp.zeros((TILE, HD), f32)
    out_ref[...] = cut_ref[...].astype(bf16)


def finish_kernel(in_ref, out_ref):
    total = in_ref[0].astype(f32)
    for z in range(1, NZ):
        total = total + in_ref[z].astype(f32)
    rows = []
    for i in range(RI):
        squares = total[30:31, 3 * i : 3 * i + 1] + total[30:31, 3 * i + 1 : 3 * i + 2]
        squares = squares + total[30:31, 3 * i + 2 : 3 * i + 3]
        factor = lax.rsqrt(squares / D + epsilon)
        at = i * (GQ + 2)
        rows.append(
            jnp.concatenate(
                [total[at + j : at + j + 1, :] * factor for j in range(GQ + 2)], axis=1
            )
        )
    out_ref[...] = jnp.concatenate(rows, axis=0).astype(bf16)


def reorder_kernel(x_ref, *refs):
    in_refs, out_ref = refs[:NX], refs[NX]
    rows = out_ref.shape[0]
    new = lax.broadcasted_iota(jnp.int32, (rows, 1), 0)
    source = ((new // RI) % NX) ^ x_ref[0]
    src = source * XR + (new % RI) * NZ + new // (NX * RI)
    chosen = lax.broadcasted_iota(jnp.int32, (rows, rows), 1) == src
    data = jnp.concatenate([ref[...] for ref in in_refs], axis=0)
    out_ref[...] = jnp.dot(
        jnp.where(chosen, 1.0, 0.0).astype(bf16), data, preferred_element_type=f32
    ).astype(bf16)


def key_layout(owners, group_lengths, group_owner, group_start, blocks):
    length = group_lengths // BLK
    holder = (group_owner[None, :] == owners[:, None]).astype(jnp.int32)
    count = group_owner.shape[0]
    before = jnp.arange(count)[None, :] < jnp.arange(count)[:, None]
    held = holder * length[None, :]
    offset = jnp.sum(jnp.where(before[None], held[:, None, :], 0), axis=2)
    ids = jnp.arange(blocks, dtype=jnp.int32)[None, :, None]
    member = (
        (holder[:, None, :] == 1)
        & (ids >= offset[:, None, :])
        & (ids < offset[:, None, :] + length[None, None, :])
    ).astype(jnp.int32)
    start = group_start[None, None, :]
    shift = jnp.sum(member * start, axis=2)
    begin = jnp.sum(member * (start + (ids - offset[:, None, :]) * BLK), axis=2)
    live = jnp.sum(member, axis=2) > 0
    return shift, begin, live


def key_positions(begin, live, listed_rows):
    position = begin[:, :, None] + jnp.arange(BLK, dtype=jnp.int32)
    hit = jnp.any(position[..., None] == listed_rows, axis=-1)
    return jnp.where(live[:, :, None] & ~hit, position, never).reshape(-1, BLK)


def on_device(
    hidden_rows,
    qkv_weight,
    out_weight,
    norm_gain,
    next_weight,
    cache_keys,
    cache_values,
    group_lengths,
    group_owner,
    group_start,
    listed_rows,
):
    z = lax.axis_index("z")
    x = lax.axis_index("x")
    held = cache_keys.shape[0]
    blocks = held // BLK
    a2a = functools.partial(lax.all_to_all, split_axis=0, concat_axis=0, tiled=True)

    def swapped(array, step):
        return lax.ppermute(array, "x", [(n, n ^ step) for n in range(NX)])

    def after(array, *first):
        return lax.optimization_barrier((array, *first))[0]

    payload, hidden_rest = vmem_call(
        project_kernel,
        (shaped((NX, QT + KT, TILE, HD), bf16), shaped((NX, HD, HD), bf16)),
        (hidden_rows, qkv_weight, norm_gain.reshape(1, HD)),
        scratch=[
            pltpu.VMEM(hidden_rows.shape, bf16),
            pltpu.VMEM(qkv_weight.shape, bf16),
            pltpu.VMEM((1, HD), f32),
            pltpu.SemaphoreType.DMA((3,)),
        ],
        hbm=True,
        limit=60,
    )
    payload = a2a(payload, "x")

    sources = x ^ jnp.arange(NX, dtype=jnp.int32)
    shift, begin, live = key_layout(
        z * NX + sources, group_lengths, group_owner, group_start, blocks
    )
    by_zxi = listed_rows.reshape(NZ, NX, RI)
    row_pos = lax.dynamic_slice_in_dim(by_zxi, x, 1, axis=1)[:, 0].T
    new_pos = lax.dynamic_slice_in_dim(by_zxi, z, 1, axis=0).reshape(-1)
    own = 8 * RI * z + jnp.arange(8 * RI)
    chosen = (own // HD * NZ + own % NZ)[:, None] == jnp.arange(XR)[None, :]
    query_pos = jnp.sum(jnp.where(chosen, row_pos.reshape(1, XR), 0), axis=1)
    rest = jnp.full((BLK - NX * RI,), never, jnp.int32)
    wide_row_pos = jnp.broadcast_to(row_pos[:, :, None], (RI, NZ, BLK))
    cosine, sine = rope_factors(
        jnp.concatenate([query_pos, new_pos, jnp.zeros((NX * RI,), jnp.int32), shift[0]])
    )
    rows = 8 * RI + KT
    x_scalar = x.reshape(1).astype(jnp.int32)
    cache, *bundles = vmem_call(
        bundle_kernel,
        (shaped((2 * blocks, BLK, HD), bf16), *[shaped((WB, HD, HD), bf16)] * NX),
        (
            x_scalar,
            cache_keys,
            cache_values,
            cosine[rows:],
            sine[rows:],
            out_weight,
            next_weight,
            hidden_rest,
        ),
        scalars=1,
    )

    tiles = vmem_call(
        sum_x_kernel,
        shaped((NZ, rows, HD), bf16),
        (payload,),
        scratch=[pltpu.VMEM((NZ, KT, HD), f32)],
    )
    tiles, cache = lax.optimization_barrier((tiles, cache))
    caches = [cache] + [swapped(cache, step) for step in range(1, NX)]
    copies, new = vmem_call(
        rope_kernel,
        (shaped((NZ, 8 * RI, HD), bf16), shaped((2, FRESH, HD), bf16)),
        (a2a(tiles, "z"), cosine[:rows], sine[:rows]),
    )
    weights_x = {0: bundles[0], 2: swapped(after(bundles[2], copies), 2)}
    queries = a2a(copies, "z").reshape(XR * GQ, HD)
    key_pos = key_positions(begin, live, after(listed_rows, copies))
    key_pos = jnp.concatenate([key_pos, jnp.concatenate([new_pos, rest])[None]], axis=0)
    parts = vmem_call(
        attend_kernel,
        shaped((NZ, 32, HD), bf16),
        (queries, key_pos, wide_row_pos, new, *caches),
        scratch=[pltpu.VMEM((HD, (NX * blocks + 2 * RI) * BLK), f32)],
    )
    for step in (1, 3):
        weights_x[step] = swapped(after(bundles[step], parts, weights_x[2]), step)
    weights_x = [weights_x[step] for step in range(NX)]
    share = vmem_call(
        combine_kernel, shaped((NZ, 8 * RI, HD), bf16), (a2a(parts, "z"),)
    )
    heads_out = a2a(share, "z").reshape(XR * GQ, HD)
    terms = vmem_call(
        output_kernel, shaped((NH, XR, NX * HD), bf16), (heads_out, *weights_x)
    )
    *resids, products = vmem_call(
        next_kernel,
        (*[shaped((XR, HD), bf16)] * NX, shaped((NZ, 32, HD), bf16)),
        (a2a(terms, ("core", "y")), *weights_x),
        scratch=[pltpu.VMEM((NZ, 32, HD), f32)],
    )
    resids = [resids[0]] + [swapped(resids[s], s) for s in range(1, NX)]
    next_qkv = vmem_call(
        finish_kernel, shaped((RI, (GQ + 2) * HD), bf16), (a2a(products, "z"),)
    )
    *resids, next_qkv = lax.optimization_barrier((*resids, next_qkv))
    hidden_out = vmem_call(
        reorder_kernel, shaped(hidden_rows.shape, bf16), (x_scalar, *resids), scalars=1
    )
    return hidden_out, next_qkv


def solution(mesh):
    split = Mesh(mesh.devices.reshape(NH // 2, 2, NZ, NX), ("y", "core", "z", "x"))
    return jax.shard_map(
        on_device,
        mesh=split,
        in_specs=(
            P(None, GROUPS),
            P(GROUPS, HEADS),
            P(HEADS, GROUPS),
            P(GROUPS),
            P(GROUPS, HEADS),
            P(GROUPS, HEADS),
            P(GROUPS, HEADS),
            P(),
            P(),
            P(),
            P(),
        ),
        out_specs=(P(None, GROUPS), P(GROUPS, HEADS)),
        check_vma=False,
    )
```

```python
import functools

import jax
import jax.numpy as jnp
from jax import lax
from jax.experimental import pallas as pl
from jax.experimental.pallas import tpu as pltpu
from jax.sharding import Mesh
from jax.sharding import PartitionSpec as P

D = 8192
HD = 128
GQ = 8
BLK = 128
NZ = 16
NX = 4
NH = 8
FRESH = 16
RI = 3
XR = NZ * RI
TILE = 16
QT = RI * GQ
KT = 2 * NX * RI
WB = 2 * GQ + 3
GROUPS = ("z", "x")
HEADS = ("y", "core")
theta_base = 500000.0
epsilon = 1e-05
masked_score = -1e30
least_peak = -1e28
never = 2**30
LOG2E = 1.4426950408889634

bf16 = jnp.bfloat16
f32 = jnp.float32


def vmem_call(kernel, out_shape, operands, scratch=(), limit=12, scalars=0, hbm=False):
    space = pl.BlockSpec(memory_space=pltpu.VMEM)
    outs = jax.tree.map(lambda _: space, out_shape)
    rest = pl.BlockSpec(memory_space=pltpu.HBM) if hbm else space
    small = pl.BlockSpec(memory_space=pltpu.SMEM)
    return pl.pallas_call(
        kernel,
        out_shape=out_shape,
        in_specs=[small] * scalars + [rest] * (len(operands) - scalars),
        out_specs=outs,
        scratch_shapes=list(scratch),
        compiler_params=pltpu.CompilerParams(vmem_limit_bytes=limit * 2**20),
    )(*operands)


def shaped(shape, dtype):
    return jax.ShapeDtypeStruct(shape, dtype)


def three_pieces(value):
    high = value.astype(bf16).astype(f32)
    rest = value - high
    middle = rest.astype(bf16).astype(f32)
    low = (rest - middle).astype(bf16).astype(f32)
    return high, middle, low


def angles(positions, half_dim):
    freq = theta_base ** (-(jnp.arange(half_dim).astype(f32) * 2.0 / (2 * half_dim)))
    phase = positions.astype(f32)[:, None] * freq[None, :]
    return (jnp.cos(phase), jnp.sin(phase))


def rope_factors(positions):
    cosine, sine = angles(positions, HD // 2)
    return jnp.concatenate([cosine, cosine], -1), jnp.concatenate([-sine, sine], -1)


def bundle_kernel(
    x_ref, keys_ref, values_ref, cos_ref, sin_ref, out_weight_ref, next_weight_ref, hidden_ref, cache_ref, *bundle_refs
):
    blocks = keys_ref.shape[0] // BLK
    for b in range(blocks):
        cache_ref[blocks + b] = values_ref[b * BLK : (b + 1) * BLK, :]
        block = keys_ref[b * BLK : (b + 1) * BLK, :].astype(f32)
        turned = (
            block * cos_ref[b : b + 1, :]
            + pltpu.roll(block, HD // 2, 1) * sin_ref[b : b + 1, :]
        )
        turned = turned.astype(bf16).astype(f32)
        cache_ref[b] = turned.T.astype(bf16)
    for s, bundle_ref in enumerate(bundle_refs):
        for g in range(GQ):
            bundle_ref[g] = out_weight_ref[g * HD : (g + 1) * HD, :]
        for j in range(GQ + 2):
            bundle_ref[GQ + j] = next_weight_ref[:, j * HD : (j + 1) * HD]
        bundle_ref[WB - 1] = hidden_ref[x_ref[0] ^ s]


def project_kernel(hidden_hbm, weight_hbm, gain_hbm, out_ref, rows_ref, hidden_ref, weight_ref, gain_ref, sems):
    copies = [
        pltpu.make_async_copy(src, dst, sems.at[n])
        for n, (src, dst) in enumerate(
            ((hidden_hbm, hidden_ref), (gain_hbm, gain_ref), (weight_hbm, weight_ref))
        )
    ]
    for copy in copies:
        copy.start()
    rows = hidden_ref.shape[0]
    new = lax.broadcasted_iota(jnp.int32, (rows, 1), 0)
    src = (new % NZ) * (NX * RI) + (new // XR) * RI + (new % XR) // NZ
    chosen = lax.broadcasted_iota(jnp.int32, (rows, rows), 1) == src
    choice = jnp.where(chosen, 1.0, 0.0).astype(bf16)
    copies[0].wait()
    copies[1].wait()
    moved = jnp.dot(
        choice, hidden_ref[...], preferred_element_type=f32
    ).astype(bf16)
    high, middle, low = three_pieces(gain_ref[...])
    sub = lax.broadcasted_iota(jnp.int32, (TILE, HD), 0)
    gain = jnp.where(
        sub == 0, high, jnp.where(sub == 1, middle, jnp.where(sub == 2, low, 0.0))
    ).astype(bf16)
    rest = jnp.zeros((HD - XR - TILE, HD), bf16)
    for x in range(NX):
        rows_ref[x] = jnp.concatenate([moved[x * XR : (x + 1) * XR, :], gain, rest], axis=0)
    copies[2].wait()
    for first in range(0, GQ + 2, 2):
        columns = weight_ref[:, first * HD : (first + 2) * HD]
        product = jnp.dot(moved, columns, preferred_element_type=f32).astype(bf16)
        for j in range(first, first + 2):
            strip = product[:, (j - first) * HD : (j - first + 1) * HD]
            for x in range(NX):
                for i in range(RI):
                    tile = strip[x * XR + i * TILE : x * XR + (i + 1) * TILE, :]
                    if j < GQ:
                        out_ref[x, i * GQ + j] = tile
                    else:
                        for to in range(NX):
                            out_ref[to, QT + (j - GQ) * NX * RI + x * RI + i] = tile


def sum_x_kernel(in_ref, tiles_ref, cut_ref):
    def total(t):
        result = in_ref[0, t].astype(f32)
        for x in range(1, NX):
            result = result + in_ref[x, t].astype(f32)
        return result

    for k in range(KT):
        cut_ref[:, k, :] = total(QT + k)
    rows = [total(t) for t in range(QT)]
    halves = [row[h * 8 : (h + 1) * 8, :] for row in rows for h in range(2)]
    for z in range(NZ):
        block = halves[z * RI : (z + 1) * RI] + [cut_ref[z]]
        tiles_ref[z] = jnp.concatenate(block, axis=0).astype(bf16)


def rope_kernel(in_ref, cos_ref, sin_ref, copies_ref, new_ref):
    total = in_ref[0].astype(f32)
    for z in range(1, NZ):
        total = total + in_ref[z].astype(f32)
    turned = total * cos_ref[...] + pltpu.roll(total, HD // 2, 1) * sin_ref[...]
    queries = turned[: 8 * RI, :].astype(bf16)
    for z in range(NZ):
        copies_ref[z] = queries
    new = turned[8 * RI :, :]
    pad = jnp.zeros((FRESH - NX * RI, HD), f32)
    new_ref[0] = jnp.concatenate([new[: NX * RI, :], pad], axis=0).astype(bf16)
    new_ref[1] = jnp.concatenate([new[NX * RI :, :], pad], axis=0).astype(bf16)


def attend_kernel(queries_ref, keypos_ref, rowpos_ref, new_ref, *refs):
    cache_refs, (out_ref, score_ref) = refs[:NX], refs[NX:]
    blocks = (keypos_ref.shape[0] - 1) // NX
    scale = HD ** (-0.5) * LOG2E
    contract_last = (((1,), (1,)), ((), ()))
    new_keys, new_values = new_ref[0], new_ref[1]
    fresh = new_keys.shape[0]
    every = queries_ref[...]
    row_pos = [jnp.concatenate([rowpos_ref[i]] * GQ, axis=0) for i in range(RI)]
    peaks = [jnp.full((HD, BLK), least_peak, f32)] * RI
    for x in range(NX):
        keys = jnp.concatenate([cache_refs[x][b] for b in range(blocks)], axis=1)
        score = jnp.dot(every, keys, preferred_element_type=f32)
        for i in range(RI):
            at = i * HD
            for b in range(blocks):
                n = x * blocks + b
                cut = jnp.where(
                    keypos_ref[n : n + 1, :] <= row_pos[i],
                    score[at : at + HD, b * BLK : (b + 1) * BLK],
                    masked_score,
                )
                score_ref[at : at + HD, n * BLK : (n + 1) * BLK] = cut
                peaks[i] = jnp.maximum(peaks[i], cut)
    n = NX * blocks
    score = lax.dot_general(every, new_keys, contract_last, preferred_element_type=f32)
    tops, totals, weights = [], [], []
    for i in range(RI):
        allowed = keypos_ref[n : n + 1, :fresh] <= row_pos[i][:, :fresh]
        last = jnp.where(allowed, score[i * HD : (i + 1) * HD, :], masked_score)
        top = scale * jnp.maximum(
            jnp.max(peaks[i], axis=1, keepdims=True), jnp.max(last, axis=1, keepdims=True)
        )
        weight = jnp.exp2(last * scale - top)
        tops.append(top)
        totals.append(jnp.sum(weight, axis=1, keepdims=True))
        weights.append(weight.astype(bf16))
    numer = jnp.dot(jnp.concatenate(weights, axis=0), new_values, preferred_element_type=f32)
    sums = [jnp.zeros((HD, BLK), f32)] * RI
    for x in range(NX):
        bands = []
        for i in range(RI):
            weights = []
            for b in range(blocks):
                n = x * blocks + b
                cut = score_ref[i * HD : (i + 1) * HD, n * BLK : (n + 1) * BLK]
                weight = jnp.exp2(cut * scale - tops[i])
                sums[i] = sums[i] + weight
                weights.append(weight.astype(bf16))
            bands.append(jnp.concatenate(weights, axis=1))
        values = jnp.concatenate([cache_refs[x][blocks + b] for b in range(blocks)], axis=0)
        numer = numer + jnp.dot(
            jnp.concatenate(bands, axis=0), values, preferred_element_type=f32
        )
    shares, levels = [], []
    for i in range(RI):
        total = jnp.sum(sums[i], axis=1, keepdims=True) + totals[i]
        some = total > 0.0
        factor = jnp.where(some, 1.0 / jnp.where(some, total, 1.0), 0.0)
        shares.append(numer[i * HD : (i + 1) * HD, :] * factor)
        level = tops[i] + jnp.where(some, jnp.log2(jnp.where(some, total, 1.0)), 0.0)
        levels.append(jnp.broadcast_to(level, (HD, BLK)))
    lane = lax.broadcasted_iota(jnp.int32, (8, HD), 1)
    for z in range(NZ):
        parts = []
        tail = jnp.zeros((8, HD), f32)
        for k in range(RI):
            row = 24 * z + 8 * k
            i, r = row // HD, row % HD
            parts.append(shares[i][r : r + 8, :])
            for p, piece in enumerate(three_pieces(levels[i][r : r + 8, :])):
                tail = jnp.where(lane == 3 * k + p, piece, tail)
        out_ref[z] = jnp.concatenate(parts + [tail], axis=0).astype(bf16)


def combine_kernel(in_ref, out_ref):
    level = [[None] * RI for _ in range(NZ)]
    top = [None] * RI
    for z in range(NZ):
        tail = in_ref[z].astype(f32)[24:32, :]
        for k in range(RI):
            value = tail[:, 3 * k : 3 * k + 1] + tail[:, 3 * k + 1 : 3 * k + 2]
            value = value + tail[:, 3 * k + 2 : 3 * k + 3]
            level[z][k] = value
            top[k] = value if z == 0 else jnp.maximum(top[k], value)
    numer = jnp.zeros((8 * RI, HD), f32)
    total = jnp.zeros((8 * RI, 1), f32)
    for z in range(NZ):
        factor = jnp.concatenate([jnp.exp2(level[z][k] - top[k]) for k in range(RI)], axis=0)
        numer = numer + in_ref[z].astype(f32)[: 8 * RI, :] * factor
        total = total + factor
    result = (numer / total).astype(bf16)
    for z in range(NZ):
        out_ref[z] = result


def output_kernel(heads_ref, *refs):
    weight_refs, out_ref = refs[:NX], refs[NX]
    weights = [ref[:GQ].reshape(GQ * HD, HD) for ref in weight_refs]
    rows = heads_ref[...]
    bands = []
    for i in range(RI):
        at = i * GQ * TILE
        bands.append(
            jnp.concatenate([rows[at + g * TILE : at + (g + 1) * TILE, :] for g in range(GQ)], axis=1)
        )
    attended = jnp.concatenate(bands, axis=0)
    for x in range(NX):
        term = jnp.dot(attended, weights[x], preferred_element_type=f32).astype(bf16)
        for h in range(NH):
            out_ref[h, :, x * HD : (x + 1) * HD] = term


def next_kernel(terms_ref, *refs):
    gained = []
    resid_refs, (out_ref, cut_ref) = refs[NX : 2 * NX], refs[2 * NX :]
    attended = terms_ref[0].astype(f32)
    for h in range(1, NH):
        attended = attended + terms_ref[h].astype(f32)
    squares = jnp.zeros((XR, 1), f32)
    for x in range(NX):
        rest = refs[x][WB - 1].astype(f32)
        before = rest[:XR]
        gain = rest[XR : XR + 1] + rest[XR + 1 : XR + 2] + rest[XR + 2 : XR + 3]
        resid = before + attended[:, x * HD : (x + 1) * HD]
        resid_refs[x][...] = resid.astype(bf16)
        squares = squares + jnp.sum(resid * resid, axis=1, keepdims=True)
        gained.append((resid * gain).astype(bf16))
    gained = jnp.concatenate(gained, axis=1)
    for first in range(0, GQ + 2, 2):
        pair = range(GQ + first, GQ + first + 2)
        columns = [jnp.concatenate([ref[j] for j in pair], axis=1) for ref in refs[:NX]]
        product = jnp.dot(
            gained, jnp.concatenate(columns, axis=0), preferred_element_type=f32
        )
        for i in range(RI):
            for j in range(2):
                cut_ref[:, i * (GQ + 2) + first + j, :] = product[
                    i * TILE : (i + 1) * TILE, j * HD : (j + 1) * HD
                ]
    lane = lax.broadcasted_iota(jnp.int32, (TILE, HD), 1)
    tail = jnp.zeros((TILE, HD), f32)
    for i in range(RI):
        for p, piece in enumerate(three_pieces(squares[i * TILE : (i + 1) * TILE, :])):
            tail = jnp.where(lane == 3 * i + p, piece, tail)
    cut_ref[:, 30, :] = tail
    cut_ref[:, 31, :] = jnp.zeros((TILE, HD), f32)
    out_ref[...] = cut_ref[...].astype(bf16)


def finish_kernel(in_ref, out_ref):
    total = in_ref[0].astype(f32)
    for z in range(1, NZ):
        total = total + in_ref[z].astype(f32)
    rows = []
    for i in range(RI):
        squares = total[30:31, 3 * i : 3 * i + 1] + total[30:31, 3 * i + 1 : 3 * i + 2]
        squares = squares + total[30:31, 3 * i + 2 : 3 * i + 3]
        factor = lax.rsqrt(squares / D + epsilon)
        at = i * (GQ + 2)
        rows.append(
            jnp.concatenate(
                [total[at + j : at + j + 1, :] * factor for j in range(GQ + 2)], axis=1
            )
        )
    out_ref[...] = jnp.concatenate(rows, axis=0).astype(bf16)


def reorder_kernel(x_ref, *refs):
    in_refs, out_ref = refs[:NX], refs[NX]
    rows = out_ref.shape[0]
    new = lax.broadcasted_iota(jnp.int32, (rows, 1), 0)
    source = ((new // RI) % NX) ^ x_ref[0]
    src = source * XR + (new % RI) * NZ + new // (NX * RI)
    chosen = lax.broadcasted_iota(jnp.int32, (rows, rows), 1) == src
    data = jnp.concatenate([ref[...] for ref in in_refs], axis=0)
    out_ref[...] = jnp.dot(
        jnp.where(chosen, 1.0, 0.0).astype(bf16), data, preferred_element_type=f32
    ).astype(bf16)


def key_layout(owners, group_lengths, group_owner, group_start, blocks):
    length = group_lengths // BLK
    holder = (group_owner[None, :] == owners[:, None]).astype(jnp.int32)
    count = group_owner.shape[0]
    before = jnp.arange(count)[None, :] < jnp.arange(count)[:, None]
    held = holder * length[None, :]
    offset = jnp.sum(jnp.where(before[None], held[:, None, :], 0), axis=2)
    ids = jnp.arange(blocks, dtype=jnp.int32)[None, :, None]
    member = (
        (holder[:, None, :] == 1)
        & (ids >= offset[:, None, :])
        & (ids < offset[:, None, :] + length[None, None, :])
    ).astype(jnp.int32)
    start = group_start[None, None, :]
    shift = jnp.sum(member * start, axis=2)
    begin = jnp.sum(member * (start + (ids - offset[:, None, :]) * BLK), axis=2)
    live = jnp.sum(member, axis=2) > 0
    return shift, begin, live


def key_positions(begin, live, listed_rows):
    position = begin[:, :, None] + jnp.arange(BLK, dtype=jnp.int32)
    hit = jnp.any(position[..., None] == listed_rows, axis=-1)
    return jnp.where(live[:, :, None] & ~hit, position, never).reshape(-1, BLK)


def on_device(
    hidden_rows,
    qkv_weight,
    out_weight,
    norm_gain,
    next_weight,
    cache_keys,
    cache_values,
    group_lengths,
    group_owner,
    group_start,
    listed_rows,
):
    z = lax.axis_index("z")
    x = lax.axis_index("x")
    held = cache_keys.shape[0]
    blocks = held // BLK
    a2a = functools.partial(lax.all_to_all, split_axis=0, concat_axis=0, tiled=True)

    def swapped(array, step):
        return lax.ppermute(array, "x", [(n, n ^ step) for n in range(NX)])

    def after(array, *first):
        return lax.optimization_barrier((array, *first))[0]

    payload, hidden_rest = vmem_call(
        project_kernel,
        (shaped((NX, QT + KT, TILE, HD), bf16), shaped((NX, HD, HD), bf16)),
        (hidden_rows, qkv_weight, norm_gain.reshape(1, HD)),
        scratch=[
            pltpu.VMEM(hidden_rows.shape, bf16),
            pltpu.VMEM(qkv_weight.shape, bf16),
            pltpu.VMEM((1, HD), f32),
            pltpu.SemaphoreType.DMA((3,)),
        ],
        hbm=True,
        limit=60,
    )
    payload = a2a(payload, "x")

    sources = x ^ jnp.arange(NX, dtype=jnp.int32)
    shift, begin, live = key_layout(
        z * NX + sources, group_lengths, group_owner, group_start, blocks
    )
    by_zxi = listed_rows.reshape(NZ, NX, RI)
    row_pos = lax.dynamic_slice_in_dim(by_zxi, x, 1, axis=1)[:, 0].T
    new_pos = lax.dynamic_slice_in_dim(by_zxi, z, 1, axis=0).reshape(-1)
    own = 8 * RI * z + jnp.arange(8 * RI)
    chosen = (own // HD * NZ + own % NZ)[:, None] == jnp.arange(XR)[None, :]
    query_pos = jnp.sum(jnp.where(chosen, row_pos.reshape(1, XR), 0), axis=1)
    rest = jnp.full((BLK - NX * RI,), never, jnp.int32)
    wide_row_pos = jnp.broadcast_to(row_pos[:, :, None], (RI, NZ, BLK))
    cosine, sine = rope_factors(
        jnp.concatenate([query_pos, new_pos, jnp.zeros((NX * RI,), jnp.int32), shift[0]])
    )
    rows = 8 * RI + KT
    x_scalar = x.reshape(1).astype(jnp.int32)
    cache, *bundles = vmem_call(
        bundle_kernel,
        (shaped((2 * blocks, BLK, HD), bf16), *[shaped((WB, HD, HD), bf16)] * NX),
        (
            x_scalar,
            cache_keys,
            cache_values,
            cosine[rows:],
            sine[rows:],
            out_weight,
            next_weight,
            hidden_rest,
        ),
        scalars=1,
    )

    tiles = vmem_call(
        sum_x_kernel,
        shaped((NZ, rows, HD), bf16),
        (payload,),
        scratch=[pltpu.VMEM((NZ, KT, HD), f32)],
    )
    tiles, cache = lax.optimization_barrier((tiles, cache))
    caches = [cache] + [swapped(cache, step) for step in range(1, NX)]
    copies, new = vmem_call(
        rope_kernel,
        (shaped((NZ, 8 * RI, HD), bf16), shaped((2, FRESH, HD), bf16)),
        (a2a(tiles, "z"), cosine[:rows], sine[:rows]),
    )
    weights_x = {0: bundles[0], 2: swapped(after(bundles[2], copies), 2)}
    queries = a2a(copies, "z").reshape(XR * GQ, HD)
    key_pos = key_positions(begin, live, after(listed_rows, copies))
    key_pos = jnp.concatenate([key_pos, jnp.concatenate([new_pos, rest])[None]], axis=0)
    parts = vmem_call(
        attend_kernel,
        shaped((NZ, 32, HD), bf16),
        (queries, key_pos, wide_row_pos, new, *caches),
        scratch=[pltpu.VMEM((XR * GQ, NX * blocks * BLK), f32)],
        limit=20,
    )
    for step in (1, 3):
        weights_x[step] = swapped(after(bundles[step], parts, weights_x[2]), step)
    weights_x = [weights_x[step] for step in range(NX)]
    share = vmem_call(
        combine_kernel, shaped((NZ, 8 * RI, HD), bf16), (a2a(parts, "z"),)
    )
    heads_out = a2a(share, "z").reshape(XR * GQ, HD)
    terms = vmem_call(
        output_kernel, shaped((NH, XR, NX * HD), bf16), (heads_out, *weights_x)
    )
    *resids, products = vmem_call(
        next_kernel,
        (*[shaped((XR, HD), bf16)] * NX, shaped((NZ, 32, HD), bf16)),
        (a2a(terms, ("core", "y")), *weights_x),
        scratch=[pltpu.VMEM((NZ, 32, HD), f32)],
    )
    resids = [resids[0]] + [swapped(resids[s], s) for s in range(1, NX)]
    next_qkv = vmem_call(
        finish_kernel, shaped((RI, (GQ + 2) * HD), bf16), (a2a(products, "z"),)
    )
    *resids, next_qkv = lax.optimization_barrier((*resids, next_qkv))
    hidden_out = vmem_call(
        reorder_kernel, shaped(hidden_rows.shape, bf16), (x_scalar, *resids), scalars=1
    )
    return hidden_out, next_qkv


def solution(mesh):
    split = Mesh(mesh.devices.reshape(NH // 2, 2, NZ, NX), ("y", "core", "z", "x"))
    return jax.shard_map(
        on_device,
        mesh=split,
        in_specs=(
            P(None, GROUPS),
            P(GROUPS, HEADS),
            P(HEADS, GROUPS),
            P(GROUPS),
            P(GROUPS, HEADS),
            P(GROUPS, HEADS),
            P(GROUPS, HEADS),
            P(),
            P(),
            P(),
            P(),
        ),
        out_specs=(P(None, GROUPS), P(GROUPS, HEADS)),
        check_vma=False,
    )
```

```python
import functools

import jax
import jax.numpy as jnp
from jax import lax
from jax.experimental import pallas as pl
from jax.experimental.pallas import tpu as pltpu
from jax.sharding import Mesh
from jax.sharding import PartitionSpec as P

D = 8192
HD = 128
GQ = 8
BLK = 128
NZ = 16
NX = 4
NH = 8
FRESH = 16
RI = 3
XR = NZ * RI
TILE = 16
QT = RI * GQ
KT = 2 * NX * RI
WB = 2 * GQ + 3
GROUPS = ("z", "x")
HEADS = ("y", "core")
theta_base = 500000.0
epsilon = 1e-05
masked_score = -1e30
least_peak = -1e28
never = 2**30
LOG2E = 1.4426950408889634

bf16 = jnp.bfloat16
f32 = jnp.float32


def vmem_call(kernel, out_shape, operands, scratch=(), limit=12, scalars=0, hbm=False):
    space = pl.BlockSpec(memory_space=pltpu.VMEM)
    outs = jax.tree.map(lambda _: space, out_shape)
    rest = pl.BlockSpec(memory_space=pltpu.HBM) if hbm else space
    small = pl.BlockSpec(memory_space=pltpu.SMEM)
    return pl.pallas_call(
        kernel,
        out_shape=out_shape,
        in_specs=[small] * scalars + [rest] * (len(operands) - scalars),
        out_specs=outs,
        scratch_shapes=list(scratch),
        compiler_params=pltpu.CompilerParams(vmem_limit_bytes=limit * 2**20),
    )(*operands)


def shaped(shape, dtype):
    return jax.ShapeDtypeStruct(shape, dtype)


def three_pieces(value):
    high = value.astype(bf16).astype(f32)
    rest = value - high
    middle = rest.astype(bf16).astype(f32)
    low = (rest - middle).astype(bf16).astype(f32)
    return high, middle, low


def angles(positions, half_dim):
    freq = theta_base ** (-(jnp.arange(half_dim).astype(f32) * 2.0 / (2 * half_dim)))
    phase = positions.astype(f32)[:, None] * freq[None, :]
    return (jnp.cos(phase), jnp.sin(phase))


def rope_factors(positions):
    cosine, sine = angles(positions, HD // 2)
    return jnp.concatenate([cosine, cosine], -1), jnp.concatenate([-sine, sine], -1)


def bundle_kernel(
    x_ref, keys_ref, values_ref, cos_ref, sin_ref, out_weight_ref, next_weight_ref, hidden_ref, cache_ref, *bundle_refs
):
    blocks = keys_ref.shape[0] // BLK
    for b in range(blocks):
        cache_ref[blocks + b] = values_ref[b * BLK : (b + 1) * BLK, :]
        block = keys_ref[b * BLK : (b + 1) * BLK, :].astype(f32)
        turned = (
            block * cos_ref[b : b + 1, :]
            + pltpu.roll(block, HD // 2, 1) * sin_ref[b : b + 1, :]
        )
        turned = turned.astype(bf16).astype(f32)
        cache_ref[b] = turned.T.astype(bf16)
    for s, bundle_ref in enumerate(bundle_refs):
        for g in range(GQ):
            bundle_ref[g] = out_weight_ref[g * HD : (g + 1) * HD, :]
        for j in range(GQ + 2):
            bundle_ref[GQ + j] = next_weight_ref[:, j * HD : (j + 1) * HD]
        bundle_ref[WB - 1] = hidden_ref[x_ref[0] ^ s]


def project_kernel(hidden_hbm, weight_hbm, gain_hbm, out_ref, rows_ref, hidden_ref, weight_ref, gain_ref, sems):
    copies = [
        pltpu.make_async_copy(src, dst, sems.at[n])
        for n, (src, dst) in enumerate(
            ((hidden_hbm, hidden_ref), (gain_hbm, gain_ref), (weight_hbm, weight_ref))
        )
    ]
    for copy in copies:
        copy.start()
    rows = hidden_ref.shape[0]
    new = lax.broadcasted_iota(jnp.int32, (rows, 1), 0)
    src = (new % NZ) * (NX * RI) + (new // XR) * RI + (new % XR) // NZ
    chosen = lax.broadcasted_iota(jnp.int32, (rows, rows), 1) == src
    choice = jnp.where(chosen, 1.0, 0.0).astype(bf16)
    copies[0].wait()
    copies[1].wait()
    moved = jnp.dot(
        choice, hidden_ref[...], preferred_element_type=f32
    ).astype(bf16)
    high, middle, low = three_pieces(gain_ref[...])
    sub = lax.broadcasted_iota(jnp.int32, (TILE, HD), 0)
    gain = jnp.where(
        sub == 0, high, jnp.where(sub == 1, middle, jnp.where(sub == 2, low, 0.0))
    ).astype(bf16)
    rest = jnp.zeros((HD - XR - TILE, HD), bf16)
    for x in range(NX):
        rows_ref[x] = jnp.concatenate([moved[x * XR : (x + 1) * XR, :], gain, rest], axis=0)
    copies[2].wait()
    for first in range(0, GQ + 2, 2):
        columns = weight_ref[:, first * HD : (first + 2) * HD]
        product = jnp.dot(moved, columns, preferred_element_type=f32).astype(bf16)
        for j in range(first, first + 2):
            strip = product[:, (j - first) * HD : (j - first + 1) * HD]
            for x in range(NX):
                for i in range(RI):
                    tile = strip[x * XR + i * TILE : x * XR + (i + 1) * TILE, :]
                    if j < GQ:
                        out_ref[x, i * GQ + j] = tile
                    else:
                        for to in range(NX):
                            out_ref[to, QT + (j - GQ) * NX * RI + x * RI + i] = tile


def sum_x_kernel(in_ref, tiles_ref, cut_ref):
    def total(t):
        result = in_ref[0, t].astype(f32)
        for x in range(1, NX):
            result = result + in_ref[x, t].astype(f32)
        return result

    for k in range(KT):
        cut_ref[:, k, :] = total(QT + k)
    rows = [total(t) for t in range(QT)]
    halves = [row[h * 8 : (h + 1) * 8, :] for row in rows for h in range(2)]
    for z in range(NZ):
        block = halves[z * RI : (z + 1) * RI] + [cut_ref[z]]
        tiles_ref[z] = jnp.concatenate(block, axis=0).astype(bf16)


def rope_kernel(in_ref, cos_ref, sin_ref, copies_ref, new_ref):
    total = in_ref[0].astype(f32)
    for z in range(1, NZ):
        total = total + in_ref[z].astype(f32)
    turned = total * cos_ref[...] + pltpu.roll(total, HD // 2, 1) * sin_ref[...]
    queries = turned[: 8 * RI, :].astype(bf16)
    for z in range(NZ):
        copies_ref[z] = queries
    new = turned[8 * RI :, :]
    pad = jnp.zeros((FRESH - NX * RI, HD), f32)
    new_ref[0] = jnp.concatenate([new[: NX * RI, :], pad], axis=0).astype(bf16)
    new_ref[1] = jnp.concatenate([new[NX * RI :, :], pad], axis=0).astype(bf16)


def attend_kernel(queries_ref, keypos_ref, rowpos_ref, new_ref, *refs):
    cache_refs, (out_ref, score_ref) = refs[:NX], refs[NX:]
    blocks = (keypos_ref.shape[0] - 1) // NX
    scale = HD ** (-0.5) * LOG2E
    contract_last = (((1,), (1,)), ((), ()))
    new_keys, new_values = new_ref[0], new_ref[1]
    fresh = new_keys.shape[0]
    every = queries_ref[...]
    for i in range(RI):
        queries = every[i * HD : (i + 1) * HD, :]
        row_pos = jnp.concatenate([rowpos_ref[i]] * GQ, axis=0)
        peak = jnp.full((HD, BLK), least_peak, f32)
        for x in range(NX):
            for first in range(0, blocks, 2):
                keys = jnp.concatenate([cache_refs[x][first], cache_refs[x][first + 1]], axis=1)
                score = jnp.dot(queries, keys, preferred_element_type=f32)
                for b in range(2):
                    n = x * blocks + first + b
                    cut = jnp.where(
                        keypos_ref[n : n + 1, :] <= row_pos,
                        score[:, b * BLK : (b + 1) * BLK],
                        masked_score,
                    )
                    score_ref[:, n * BLK : (n + 1) * BLK] = cut
                    peak = jnp.maximum(peak, cut)
        n = NX * blocks
        score = lax.dot_general(queries, new_keys, contract_last, preferred_element_type=f32)
        last = jnp.where(keypos_ref[n : n + 1, :fresh] <= row_pos[:, :fresh], score, masked_score)
        top = jnp.maximum(
            jnp.max(peak, axis=1, keepdims=True), jnp.max(last, axis=1, keepdims=True)
        )
        top = top * scale
        weight = jnp.exp2(last * scale - top)
        total_last = jnp.sum(weight, axis=1, keepdims=True)
        numer = jnp.dot(weight.astype(bf16), new_values, preferred_element_type=f32)
        total = jnp.zeros((HD, BLK), f32)
        for x in range(NX):
            for first in range(blocks, 2 * blocks, 2):
                weights = []
                for b in range(2):
                    n = (x - 1) * blocks + first + b
                    weight = jnp.exp2(score_ref[:, n * BLK : (n + 1) * BLK] * scale - top)
                    total = total + weight
                    weights.append(weight.astype(bf16))
                values = jnp.concatenate([cache_refs[x][first], cache_refs[x][first + 1]], axis=0)
                numer = numer + jnp.dot(
                    jnp.concatenate(weights, axis=1), values, preferred_element_type=f32
                )
        total = jnp.sum(total, axis=1, keepdims=True) + total_last
        some = total > 0.0
        share = numer * jnp.where(some, 1.0 / jnp.where(some, total, 1.0), 0.0)
        level = top + jnp.where(some, jnp.log2(jnp.where(some, total, 1.0)), 0.0)
        share_at = (NX * blocks + i) * BLK
        score_ref[:, share_at : share_at + BLK] = share
        level_at = (NX * blocks + RI + i) * BLK
        score_ref[:, level_at : level_at + BLK] = jnp.broadcast_to(level, (HD, BLK))
    lane = lax.broadcasted_iota(jnp.int32, (8, HD), 1)
    for z in range(NZ):
        parts = []
        tail = jnp.zeros((8, HD), f32)
        for k in range(RI):
            row = 24 * z + 8 * k
            i, r = row // HD, row % HD
            share_at = (NX * blocks + i) * BLK
            level_at = (NX * blocks + RI + i) * BLK
            parts.append(score_ref[r : r + 8, share_at : share_at + BLK])
            for p, piece in enumerate(three_pieces(score_ref[r : r + 8, level_at : level_at + BLK])):
                tail = jnp.where(lane == 3 * k + p, piece, tail)
        out_ref[z] = jnp.concatenate(parts + [tail], axis=0).astype(bf16)


def combine_kernel(in_ref, out_ref):
    level = [[None] * RI for _ in range(NZ)]
    top = [None] * RI
    for z in range(NZ):
        tail = in_ref[z].astype(f32)[24:32, :]
        for k in range(RI):
            value = tail[:, 3 * k : 3 * k + 1] + tail[:, 3 * k + 1 : 3 * k + 2]
            value = value + tail[:, 3 * k + 2 : 3 * k + 3]
            level[z][k] = value
            top[k] = value if z == 0 else jnp.maximum(top[k], value)
    numer = jnp.zeros((8 * RI, HD), f32)
    total = jnp.zeros((8 * RI, 1), f32)
    for z in range(NZ):
        factor = jnp.concatenate([jnp.exp2(level[z][k] - top[k]) for k in range(RI)], axis=0)
        numer = numer + in_ref[z].astype(f32)[: 8 * RI, :] * factor
        total = total + factor
    result = (numer / total).astype(bf16)
    for z in range(NZ):
        out_ref[z] = result


def output_kernel(heads_ref, *refs):
    weight_refs, out_ref = refs[:NX], refs[NX]
    weights = [ref[:GQ].reshape(GQ * HD, HD) for ref in weight_refs]
    rows = heads_ref[...]
    bands = []
    for i in range(RI):
        at = i * GQ * TILE
        bands.append(
            jnp.concatenate([rows[at + g * TILE : at + (g + 1) * TILE, :] for g in range(GQ)], axis=1)
        )
    attended = jnp.concatenate(bands, axis=0)
    for x in range(NX):
        term = jnp.dot(attended, weights[x], preferred_element_type=f32).astype(bf16)
        for h in range(NH):
            out_ref[h, :, x * HD : (x + 1) * HD] = term


def next_kernel(terms_ref, *refs):
    wide = range(GQ, 2 * GQ + 2)
    weights = [jnp.concatenate([ref[j] for j in wide], axis=1) for ref in refs[:NX]]
    resid_refs, (out_ref, cut_ref) = refs[NX : 2 * NX], refs[2 * NX :]
    attended = terms_ref[0].astype(f32)
    for h in range(1, NH):
        attended = attended + terms_ref[h].astype(f32)
    squares = jnp.zeros((XR, 1), f32)
    product = jnp.zeros((XR, (GQ + 2) * HD), f32)
    for x in range(NX):
        rest = refs[x][WB - 1].astype(f32)
        before = rest[:XR]
        gain = rest[XR : XR + 1] + rest[XR + 1 : XR + 2] + rest[XR + 2 : XR + 3]
        resid = before + attended[:, x * HD : (x + 1) * HD]
        resid_refs[x][...] = resid.astype(bf16)
        squares = squares + jnp.sum(resid * resid, axis=1, keepdims=True)
        gained = (resid * gain).astype(bf16)
        product = product + jnp.dot(gained, weights[x], preferred_element_type=f32)
    for i in range(RI):
        for j in range(GQ + 2):
            cut_ref[:, i * (GQ + 2) + j, :] = product[
                i * TILE : (i + 1) * TILE, j * HD : (j + 1) * HD
            ]
    lane = lax.broadcasted_iota(jnp.int32, (TILE, HD), 1)
    tail = jnp.zeros((TILE, HD), f32)
    for i in range(RI):
        for p, piece in enumerate(three_pieces(squares[i * TILE : (i + 1) * TILE, :])):
            tail = jnp.where(lane == 3 * i + p, piece, tail)
    cut_ref[:, 30, :] = tail
    cut_ref[:, 31, :] = jnp.zeros((TILE, HD), f32)
    out_ref[...] = cut_ref[...].astype(bf16)


def finish_kernel(in_ref, out_ref):
    total = in_ref[0].astype(f32)
    for z in range(1, NZ):
        total = total + in_ref[z].astype(f32)
    rows = []
    for i in range(RI):
        squares = total[30:31, 3 * i : 3 * i + 1] + total[30:31, 3 * i + 1 : 3 * i + 2]
        squares = squares + total[30:31, 3 * i + 2 : 3 * i + 3]
        factor = lax.rsqrt(squares / D + epsilon)
        at = i * (GQ + 2)
        rows.append(
            jnp.concatenate(
                [total[at + j : at + j + 1, :] * factor for j in range(GQ + 2)], axis=1
            )
        )
    out_ref[...] = jnp.concatenate(rows, axis=0).astype(bf16)


def reorder_kernel(x_ref, *refs):
    in_refs, out_ref = refs[:NX], refs[NX]
    rows = out_ref.shape[0]
    new = lax.broadcasted_iota(jnp.int32, (rows, 1), 0)
    source = ((new // RI) % NX) ^ x_ref[0]
    src = source * XR + (new % RI) * NZ + new // (NX * RI)
    chosen = lax.broadcasted_iota(jnp.int32, (rows, rows), 1) == src
    data = jnp.concatenate([ref[...] for ref in in_refs], axis=0)
    out_ref[...] = jnp.dot(
        jnp.where(chosen, 1.0, 0.0).astype(bf16), data, preferred_element_type=f32
    ).astype(bf16)


def key_layout(owners, group_lengths, group_owner, group_start, blocks):
    length = group_lengths // BLK
    holder = (group_owner[None, :] == owners[:, None]).astype(jnp.int32)
    count = group_owner.shape[0]
    before = jnp.arange(count)[None, :] < jnp.arange(count)[:, None]
    held = holder * length[None, :]
    offset = jnp.sum(jnp.where(before[None], held[:, None, :], 0), axis=2)
    ids = jnp.arange(blocks, dtype=jnp.int32)[None, :, None]
    member = (
        (holder[:, None, :] == 1)
        & (ids >= offset[:, None, :])
        & (ids < offset[:, None, :] + length[None, None, :])
    ).astype(jnp.int32)
    start = group_start[None, None, :]
    shift = jnp.sum(member * start, axis=2)
    begin = jnp.sum(member * (start + (ids - offset[:, None, :]) * BLK), axis=2)
    live = jnp.sum(member, axis=2) > 0
    return shift, begin, live


def key_positions(begin, live, listed_rows):
    position = begin[:, :, None] + jnp.arange(BLK, dtype=jnp.int32)
    hit = jnp.any(position[..., None] == listed_rows, axis=-1)
    return jnp.where(live[:, :, None] & ~hit, position, never).reshape(-1, BLK)


def on_device(
    hidden_rows,
    qkv_weight,
    out_weight,
    norm_gain,
    next_weight,
    cache_keys,
    cache_values,
    group_lengths,
    group_owner,
    group_start,
    listed_rows,
):
    z = lax.axis_index("z")
    x = lax.axis_index("x")
    held = cache_keys.shape[0]
    blocks = held // BLK
    a2a = functools.partial(lax.all_to_all, split_axis=0, concat_axis=0, tiled=True)

    def swapped(array, step):
        return lax.ppermute(array, "x", [(n, n ^ step) for n in range(NX)])

    def after(array, *first):
        return lax.optimization_barrier((array, *first))[0]

    payload, hidden_rest = vmem_call(
        project_kernel,
        (shaped((NX, QT + KT, TILE, HD), bf16), shaped((NX, HD, HD), bf16)),
        (hidden_rows, qkv_weight, norm_gain.reshape(1, HD)),
        scratch=[
            pltpu.VMEM(hidden_rows.shape, bf16),
            pltpu.VMEM(qkv_weight.shape, bf16),
            pltpu.VMEM((1, HD), f32),
            pltpu.SemaphoreType.DMA((3,)),
        ],
        hbm=True,
        limit=60,
    )
    payload = a2a(payload, "x")

    sources = x ^ jnp.arange(NX, dtype=jnp.int32)
    shift, begin, live = key_layout(
        z * NX + sources, group_lengths, group_owner, group_start, blocks
    )
    by_zxi = listed_rows.reshape(NZ, NX, RI)
    row_pos = lax.dynamic_slice_in_dim(by_zxi, x, 1, axis=1)[:, 0].T
    new_pos = lax.dynamic_slice_in_dim(by_zxi, z, 1, axis=0).reshape(-1)
    own = 8 * RI * z + jnp.arange(8 * RI)
    chosen = (own // HD * NZ + own % NZ)[:, None] == jnp.arange(XR)[None, :]
    query_pos = jnp.sum(jnp.where(chosen, row_pos.reshape(1, XR), 0), axis=1)
    rest = jnp.full((BLK - NX * RI,), never, jnp.int32)
    wide_row_pos = jnp.broadcast_to(row_pos[:, :, None], (RI, NZ, BLK))
    cosine, sine = rope_factors(
        jnp.concatenate([query_pos, new_pos, jnp.zeros((NX * RI,), jnp.int32), shift[0]])
    )
    rows = 8 * RI + KT
    x_scalar = x.reshape(1).astype(jnp.int32)
    cache, *bundles = vmem_call(
        bundle_kernel,
        (shaped((2 * blocks, BLK, HD), bf16), *[shaped((WB, HD, HD), bf16)] * NX),
        (
            x_scalar,
            cache_keys,
            cache_values,
            cosine[rows:],
            sine[rows:],
            out_weight,
            next_weight,
            hidden_rest,
        ),
        scalars=1,
    )

    tiles = vmem_call(
        sum_x_kernel,
        shaped((NZ, rows, HD), bf16),
        (payload,),
        scratch=[pltpu.VMEM((NZ, KT, HD), f32)],
    )
    tiles, cache = lax.optimization_barrier((tiles, cache))
    caches = [cache] + [swapped(cache, step) for step in range(1, NX)]
    copies, new = vmem_call(
        rope_kernel,
        (shaped((NZ, 8 * RI, HD), bf16), shaped((2, FRESH, HD), bf16)),
        (a2a(tiles, "z"), cosine[:rows], sine[:rows]),
    )
    weights_x = {0: bundles[0], 2: swapped(after(bundles[2], copies), 2)}
    queries = a2a(copies, "z").reshape(XR * GQ, HD)
    key_pos = key_positions(begin, live, after(listed_rows, copies))
    key_pos = jnp.concatenate([key_pos, jnp.concatenate([new_pos, rest])[None]], axis=0)
    parts = vmem_call(
        attend_kernel,
        shaped((NZ, 32, HD), bf16),
        (queries, key_pos, wide_row_pos, new, *caches),
        scratch=[pltpu.VMEM((HD, (NX * blocks + 2 * RI) * BLK), f32)],
    )
    for step in (1, 3):
        weights_x[step] = swapped(after(bundles[step], parts, weights_x[2]), step)
    weights_x = [weights_x[step] for step in range(NX)]
    share = vmem_call(
        combine_kernel, shaped((NZ, 8 * RI, HD), bf16), (a2a(parts, "z"),)
    )
    heads_out = a2a(share, "z").reshape(XR * GQ, HD)
    terms = vmem_call(
        output_kernel, shaped((NH, XR, NX * HD), bf16), (heads_out, *weights_x)
    )
    *resids, products = vmem_call(
        next_kernel,
        (*[shaped((XR, HD), bf16)] * NX, shaped((NZ, 32, HD), bf16)),
        (a2a(terms, ("core", "y")), *weights_x),
        scratch=[pltpu.VMEM((NZ, 32, HD), f32)],
    )
    resids = [resids[0]] + [swapped(resids[s], s) for s in range(1, NX)]
    next_qkv = vmem_call(
        finish_kernel, shaped((RI, (GQ + 2) * HD), bf16), (a2a(products, "z"),)
    )
    *resids, next_qkv = lax.optimization_barrier((*resids, next_qkv))
    hidden_out = vmem_call(
        reorder_kernel, shaped(hidden_rows.shape, bf16), (x_scalar, *resids), scalars=1
    )
    return hidden_out, next_qkv


def solution(mesh):
    split = Mesh(mesh.devices.reshape(NH // 2, 2, NZ, NX), ("y", "core", "z", "x"))
    return jax.shard_map(
        on_device,
        mesh=split,
        in_specs=(
            P(None, GROUPS),
            P(GROUPS, HEADS),
            P(HEADS, GROUPS),
            P(GROUPS),
            P(GROUPS, HEADS),
            P(GROUPS, HEADS),
            P(GROUPS, HEADS),
            P(),
            P(),
            P(),
            P(),
        ),
        out_specs=(P(None, GROUPS), P(GROUPS, HEADS)),
        check_vma=False,
    )
```
